256 devices in a mesh: sub: 16 (over z_lo, y, core), col: 16 (over z_hi, x).
Axes of the slice: x: 4, y: 4, z: 8 (z_hi: 4, z_lo: 2; z = z_hi * 2 + z_lo), core: 2. Of those that a mesh axis runs over, the one named last changes fastest.
Arguments:
- initial_state: float32 [5, 64, 32768], P(None, None, ('sub', 'col')), may hold values from -6 to 6
- state_cotangent: float32 [5, 64, 32768], P(None, None, ('sub', 'col')), may hold values from -6 to 6
- element_order: int32 [256, 128], P(('sub', 'col')), may hold values from 0 to 127, each once within a row
- element_weight: float32 [32768], P(('sub', 'col')), may hold values from 1 to 3
- element_diffusivity: float32 [32768], P(('sub', 'col')), may hold values from 0.1 to 0.4
- in_weight: float32 [64, 5], replicated, may hold values from -2.5 to 2.5
- in_bias: float32 [64], replicated, may hold values from -3 to 3
- mid_weight: float32 [64, 64], replicated, may hold values from -0.75 to 0.75
- mid_bias: float32 [64], replicated, may hold values from -3 to 3
- out_weight: float32 [5, 64], replicated, may hold values from -0.75 to 0.75
- out_bias: float32 [5], replicated, may hold values from -6 to 6
Outputs:
- final_state: float32 [5, 64, 32768], P(None, None, ('sub', 'col'))
- initial_adjoint: float32 [5, 64, 32768], P(None, None, ('sub', 'col'))
- grad_in_weight: float32 [64, 5], replicated
- grad_in_bias: float32 [64], replicated
- grad_mid_weight: float32 [64, 64], replicated
- grad_mid_bias: float32 [64], replicated
- grad_out_weight: float32 [5, 64], replicated
- grad_out_bias: float32 [5], replicated
The draws below stay inside these ranges and needn't reach their ends.
Inputs may be any that keep to these rules, and one draw needn't show every extreme that they name: `element_order`: each row is a permutation of the local element positions 0 .. 127.
All inputs are finite; a program needn't handle non-finite values.
Results may differ from the reference program's by a relative error of at most 0.00027.
Values sent between devices are 32-bit elements; how exact they have to be, the bound alone decides.
No kernel may reach another device: no remote copies, remote signals or barrier semaphores. Data moves between devices by JAX's collectives and lax.ppermute only.
A program may use at most 128 MiB of HBM per device.

```python
import math
from functools import partial
import jax
import jax.numpy as jnp
import numpy as np
from jax import lax

F = 5
H = 64
STEPS = 2
EX = 1
EY = 2
EZ = 64
E = 128
NE = 32768
N_SUB = 16
N_COL = 16


def shard_levels(stream_key, extent, split, least, high):
    factor_of, own = 1.0, jax.random.fold_in(stream_key, 6)
    for axis_at, shards_of in split:
        draws = jnp.exp(jax.random.uniform(jax.random.fold_in(own, axis_at), (shards_of,), jnp.float32, least / len(split), high / len(split)))
        factor_of = factor_of * jnp.repeat(draws, extent[axis_at] // shards_of).reshape([-1 if axis == axis_at else 1 for axis in range(len(extent))])
    return factor_of


def noise(key, dims, deviation, limit, split=(), kind=jnp.bfloat16):
    entries = jax.random.normal(key, dims, jnp.float32) * deviation
    if len(split) > 0:
        entries = shard_levels(key, dims, split, -0.22, 0.18) * entries
    return jnp.clip(entries, min=-limit, max=limit).astype(kind)


def setup_inputs(seed: int = 0) -> dict:
    arg_keys = jax.random.split(jax.random.key(seed), 12)
    return {
        "initial_state": noise(arg_keys[0], (F, 64, NE), 1.0, 6.0, ((2, 256),), jnp.float32),
        "state_cotangent": noise(arg_keys[1], (F, 64, NE), 1.0, 6.0, ((2, 256),), jnp.float32),
        "element_order": jax.vmap(lambda own: jax.random.permutation(own, E))(jax.random.split(arg_keys[2], (N_SUB * N_COL))).reshape((N_SUB * N_COL, E)).astype(jnp.int32),
        "element_weight": jnp.clip(jnp.exp(math.log(3.0) - 1.0986123 * jax.random.uniform(arg_keys[3], (NE,), jnp.float32) ** shard_levels(arg_keys[3], (NE,), ((0, 256),), -0.2, 0.2)), 1.0, 3.0),
        "element_diffusivity": jnp.clip(jnp.exp(math.log(0.4) - 1.3862944 * jax.random.uniform(arg_keys[4], (NE,), jnp.float32) ** shard_levels(arg_keys[4], (NE,), ((0, 256),), -0.2, 0.2)), 0.1, 0.4),
        "in_weight": noise(arg_keys[5], (H, F), F ** -0.5, 2.5, (), jnp.float32),
        "in_bias": noise(arg_keys[6], (H,), 0.5, 3.0, (), jnp.float32),
        "mid_weight": noise(arg_keys[7], (H, H), H ** -0.5, 0.75, (), jnp.float32),
        "mid_bias": noise(arg_keys[8], (H,), 0.5, 3.0, (), jnp.float32),
        "out_weight": noise(arg_keys[9], (F, H), H ** -0.5, 0.75, (), jnp.float32),
        "out_bias": noise(arg_keys[10], (F,), 1.5, 6.0, (), jnp.float32),
    }


highest = lax.Precision.HIGHEST
time_step = 0.05

def gll_tables():
    nodes_at = [-1.0, -math.sqrt(0.2), math.sqrt(0.2), 1.0]
    quad_weights = np.array([1.0 / 6.0, 5.0 / 6.0, 5.0 / 6.0, 1.0 / 6.0])
    products = [np.prod([nodes_at[row_index] - nodes_at[partner] for partner in range(4) if partner != row_index]) for row_index in range(4)]
    deriv_table = np.zeros((4, 4))
    for row_index in range(4):
        for col_index in range(4):
            if row_index == col_index:
                deriv_table[row_index, col_index] = sum((1.0 / (nodes_at[row_index] - nodes_at[partner]) for partner in range(4) if partner != row_index))
            else:
                deriv_table[row_index, col_index] = products[row_index] / (products[col_index] * (nodes_at[row_index] - nodes_at[col_index]))
    return (quad_weights, deriv_table)

def pair_sum(extended, along_dim):
    inner_size = extended.shape[along_dim] - 2
    elem_count = inner_size // 4
    inner_part = lax.slice_in_dim(extended, 1, inner_size + 1, axis=along_dim)
    inner_part = inner_part.reshape(extended.shape[:along_dim] + (elem_count, 4) + extended.shape[along_dim + 1:])
    last_nodes = lax.index_in_dim(inner_part, 3, along_dim + 1, keepdims=False)
    first_nodes = lax.index_in_dim(inner_part, 0, along_dim + 1, keepdims=False)
    before = lax.slice_in_dim(extended, 0, 1, axis=along_dim)
    after_rim = lax.slice_in_dim(extended, inner_size + 1, inner_size + 2, axis=along_dim)
    next_first = jnp.concatenate([lax.slice_in_dim(first_nodes, 1, elem_count, axis=along_dim), after_rim], axis=along_dim)
    prev_last = jnp.concatenate([before, lax.slice_in_dim(last_nodes, 0, elem_count - 1, axis=along_dim)], axis=along_dim)
    upper_sum = last_nodes + next_first
    lower_sum = prev_last + first_nodes
    middle = lax.slice_in_dim(inner_part, 1, 3, axis=along_dim + 1)
    joined = jnp.concatenate([jnp.expand_dims(lower_sum, along_dim + 1), middle, jnp.expand_dims(upper_sum, along_dim + 1)], axis=along_dim + 1)
    return joined.reshape(extended.shape[:along_dim] + (inner_size,) + extended.shape[along_dim + 1:])

def pair_sum_z(grid_field):
    last_nodes = grid_field[..., 3, :]
    first_nodes = grid_field[..., 0, :]
    upper_sum = last_nodes + jnp.roll(first_nodes, -1, axis=-1)
    lower_sum = jnp.roll(upper_sum, 1, axis=-1)
    return jnp.concatenate([lower_sum[..., None, :], grid_field[..., 1:3, :], upper_sum[..., None, :]], axis=-2)

def periodic_pad(grid_field, along_dim):
    inner_size = grid_field.shape[along_dim]
    return jnp.concatenate([lax.slice_in_dim(grid_field, inner_size - 1, inner_size, axis=along_dim), grid_field, lax.slice_in_dim(grid_field, 0, 1, axis=along_dim)], axis=along_dim)

def assemble(grid_field):
    grid_field = pair_sum(periodic_pad(grid_field, 0), 0)
    grid_field = pair_sum(periodic_pad(grid_field, 1), 1)
    return pair_sum_z(grid_field)

def apply_stiffness(grid_field, weighted, deriv_table):
    size_x, size_y, fields, nodes_z, depth_z = grid_field.shape
    split_x = grid_field.reshape(size_x // 4, 4, size_y, fields, nodes_z, depth_z)
    coef_x = weighted.reshape(size_x // 4, 4, size_y, 1, nodes_z, depth_z)
    grad_x = jnp.einsum('iayfcz,ba->ibyfcz', split_x, deriv_table, precision=highest)
    term_x = jnp.einsum('ibyfcz,ba->iayfcz', coef_x * grad_x, deriv_table, precision=highest).reshape(grid_field.shape)
    split_y = grid_field.reshape(size_x, size_y // 4, 4, fields, nodes_z, depth_z)
    coef_y = weighted.reshape(size_x, size_y // 4, 4, 1, nodes_z, depth_z)
    grad_y = jnp.einsum('xjbfcz,db->xjdfcz', split_y, deriv_table, precision=highest)
    term_y = jnp.einsum('xjdfcz,db->xjbfcz', coef_y * grad_y, deriv_table, precision=highest).reshape(grid_field.shape)
    grad_z = jnp.einsum('xyfcz,dc->xyfdz', grid_field, deriv_table, precision=highest)
    term_z = jnp.einsum('xyfdz,dc->xyfcz', weighted * grad_z, deriv_table, precision=highest)
    return term_x + term_y + term_z

def closure_layer(params, layer_values):
    in_weight, in_bias, mid_weight, mid_bias, out_weight, out_bias = params
    first_hidden = jnp.tanh(jnp.einsum('hf,yfcz->yhcz', in_weight, layer_values, precision=highest) + in_bias[None, :, None, None])
    second_hidden = jnp.tanh(jnp.einsum('gh,yhcz->ygcz', mid_weight, first_hidden, precision=highest) + mid_bias[None, :, None, None])
    return jnp.einsum('fg,ygcz->yfcz', out_weight, second_hidden, precision=highest) + out_bias[None, :, None, None]

def closure_adjoint(params, grid_field, cotangent):
    zero_grads = jax.tree.map(jnp.zeros_like, params)

    def scan_body(carry_grads, inputs):
        layer_values, layer_cot = inputs
        unused, pullback = jax.vjp(closure_layer, params, layer_values)
        param_cot, layer_grad = pullback(layer_cot)
        return (jax.tree.map(jnp.add, carry_grads, param_cot), layer_grad)
    return lax.scan(scan_body, zero_grads, (grid_field, cotangent))

def node_field(elements, quad_weights):
    spread = jnp.repeat(jnp.repeat(elements, 4, axis=0), 4, axis=1)
    along_x = jnp.tile(quad_weights, elements.shape[0])
    along_y = jnp.tile(quad_weights, elements.shape[1])
    return along_x[:, None, None, None, None] * along_y[None, :, None, None, None] * quad_weights[None, None, None, :, None] * spread[:, :, None, None, :]

def scatter_slots(values, slot_order):
    return jnp.zeros_like(values).at[..., slot_order].set(values)

def gather_slots(values, slot_order):
    return values[..., slot_order]

def to_global(slots, slot_order):
    split_slots = slots.reshape(F, 64, N_SUB, N_COL, EX * EY * EZ).transpose(2, 3, 0, 1, 4)
    placed = jax.vmap(jax.vmap(scatter_slots))(split_slots, slot_order)
    placed = placed.reshape(N_SUB, N_COL, F, 4, 4, 4, EX, EY, EZ).transpose(0, 6, 3, 1, 7, 4, 2, 5, 8)
    return placed.reshape(N_SUB * EX * 4, N_COL * EY * 4, F, 4, EZ)

def from_global(grid_values, slot_order):
    split_grid = grid_values.reshape(N_SUB, EX, 4, N_COL, EY, 4, F, 4, EZ).transpose(0, 3, 6, 2, 5, 7, 1, 4, 8)
    split_grid = split_grid.reshape(N_SUB, N_COL, F, 64, EX * EY * EZ)
    picked = jax.vmap(jax.vmap(gather_slots))(split_grid, slot_order)
    return picked.transpose(2, 3, 0, 1, 4).reshape(F, 64, N_SUB * N_COL * EX * EY * EZ)

def element_global(values, slot_order):
    placed = jax.vmap(jax.vmap(scatter_slots))(values.reshape(N_SUB, N_COL, EX * EY * EZ), slot_order)
    return placed.reshape(N_SUB, N_COL, EX, EY, EZ).transpose(0, 2, 1, 3, 4).reshape(N_SUB * EX, N_COL * EY, EZ)

def reference(initial_state, state_cotangent, element_order, element_weight, element_diffusivity, in_weight, in_bias, mid_weight, mid_bias, out_weight, out_bias):
    quad_np, deriv_np = gll_tables()
    quad_weights = jnp.asarray(quad_np, jnp.float32)
    deriv_table = jnp.asarray(deriv_np, jnp.float32)
    slot_order = element_order.reshape(N_SUB, N_COL, EX * EY * EZ).astype(jnp.int32)
    params = (in_weight, in_bias, mid_weight, mid_bias, out_weight, out_bias)
    mass_local = node_field(element_global(element_weight, slot_order), quad_weights)
    weighted = node_field(element_global(element_diffusivity, slot_order), quad_weights)
    grid_raw = to_global(initial_state, slot_order)
    stacked = jnp.concatenate([mass_local * grid_raw, mass_local], axis=2)
    assembled = assemble(stacked)
    mass_total = assembled[:, :, F:]
    state_now = assembled[:, :, :F] / mass_total
    saved_states = []
    for step_index in range(STEPS):
        saved_states.append(state_now)
        forcing = lax.map(partial(closure_layer, params), state_now)
        residual = mass_local * forcing - apply_stiffness(state_now, weighted, deriv_table)
        state_now = state_now + time_step * assemble(residual) / mass_total
    adjoint = to_global(state_cotangent, slot_order)
    grads_total = None
    for step_index in reversed(range(STEPS)):
        scaled = time_step * assemble(adjoint / mass_total)
        totals, back_state = closure_adjoint(params, saved_states[step_index], mass_local * scaled)
        adjoint = adjoint - apply_stiffness(scaled, weighted, deriv_table) + back_state
        grads_total = totals if grads_total is None else jax.tree.map(jnp.add, grads_total, totals)
    initial_grid = mass_local * assemble(adjoint / mass_total)
    scale_down = 1.0 / (N_SUB * N_COL)
    return (from_global(state_now, slot_order), from_global(initial_grid, slot_order), grads_total[0] * scale_down, grads_total[1] * scale_down, grads_total[2] * scale_down, grads_total[3] * scale_down, grads_total[4] * scale_down, grads_total[5] * scale_down)
```

```python
import math

import jax
import jax.numpy as jnp
import numpy as np
from jax import lax
from jax.experimental import pallas as pl
from jax.experimental.pallas import tpu as pltpu
from jax.sharding import PartitionSpec as P

F = 5
STEP = 0.05
CH = 16
NW = CH * 128
f32, bf16 = jnp.float32, jnp.bfloat16
VM = pl.BlockSpec(memory_space=pltpu.VMEM)


def stiffness_matrix():
    at = [-1.0, -math.sqrt(0.2), math.sqrt(0.2), 1.0]
    w = np.array([1.0 / 6.0, 5.0 / 6.0, 5.0 / 6.0, 1.0 / 6.0])
    prods = [np.prod([at[r] - at[p] for p in range(4) if p != r]) for r in range(4)]
    d = np.zeros((4, 4))
    for r in range(4):
        for c in range(4):
            if r == c:
                d[r, c] = sum(1.0 / (at[r] - at[p]) for p in range(4) if p != r)
            else:
                d[r, c] = prods[r] / (prods[c] * (at[r] - at[c]))
    s = d.T @ np.diag(w) @ d
    m = np.diag(w)
    k = np.kron(m, np.kron(s, m)) + np.kron(m, np.kron(m, s)) + np.kron(s, np.kron(m, m))
    k = k.astype(np.float32)
    hi = k.astype(bf16).astype(np.float32)
    lo = k - hi
    return np.concatenate([hi, hi, lo], axis=1).astype(bf16)


def iota(shape, dim):
    return lax.broadcasted_iota(jnp.int32, shape, dim)


def next_k(x):
    ax = x.ndim - 1
    lane = iota(x.shape, ax) & 63
    return jnp.where(lane == 63, pltpu.roll(x, 63, ax), pltpu.roll(x, 127, ax))


def prev_k(x):
    ax = x.ndim - 1
    lane = iota(x.shape, ax) & 63
    return jnp.where(lane == 0, pltpu.roll(x, 65, ax), pltpu.roll(x, 1, ax))


def zsum(v):
    n = v.shape[0]
    top = v[:, 48:64] + next_k(v[:, 0:16])
    return jnp.concatenate([v[:, 16:48], top], axis=1)


def zfill(w):
    return jnp.concatenate([prev_k(w[:, 32:48]), w], axis=1)


def sroll(x, s):
    return pltpu.roll(x, s % 8, x.ndim - 2) if s % 8 else x


def xpack(w):
    n = w.shape[0]
    h = n // 2
    t = w.reshape(n, 3, 2, 8, 128)
    v0, v1 = t[:, :, 0].reshape(n * 3, 8, 128), t[:, :, 1].reshape(n * 3, 8, 128)
    low = iota((h * 3, 8, 128), 1) < 4
    up = jnp.where(low, sroll(v1[: h * 3], 4), v1[h * 3 :])
    dn = jnp.where(low, v0[: h * 3], sroll(v0[h * 3 :], 4))
    return up, dn


def xadd(w, rp, rm):
    n = w.shape[0]
    h = n // 2
    t = w.reshape(n, 3, 2, 8, 128)
    v0, v1 = t[:, :, 0].reshape(n * 3, 8, 128), t[:, :, 1].reshape(n * 3, 8, 128)
    low = iota((h * 3, 8, 128), 1) < 4
    zero = jnp.zeros_like(rp)
    a0 = jnp.concatenate([jnp.where(low, rp, zero), jnp.where(low, sroll(rp, 4), zero)], axis=0)
    a1 = jnp.concatenate([jnp.where(low, zero, sroll(rm, 4)), jnp.where(low, zero, rm)], axis=0)
    v0, v1 = v0 + a0, v1 + a1
    return v0, v1


def ylocal(v):
    b = iota(v.shape, 1) & 3
    left = iota(v.shape, 2) < 64
    d = jnp.where(b == 0, sroll(v, 5), sroll(v, 3))
    d = pltpu.roll(d, 64, 2)
    zero = jnp.zeros_like(v)
    here = ((b == 0) & (~left)) | ((b == 3) & left)
    out = ((b == 0) & left) | ((b == 3) & (~left))
    return v + jnp.where(here, d, zero), jnp.where(out, d, zero)


def xy_body(n, w_ref, rp_ref, rm_ref, wo_ref, y_ref):
    w = w_ref[...]
    v0, v1 = xadd(w, rp_ref[...], rm_ref[...])
    for part, v in enumerate((v0, v1)):
        v, e = ylocal(v)
        wo_ref[:, :, part] = v.reshape(n, 3, 8, 128)
        e = e.reshape(n, 3, 8, 128)
        y_ref[:, part] = e[:, 0] + sroll(e[:, 1], 1) + sroll(e[:, 2], 2)


def yadd(w, yl, yr):
    n = w.shape[0]
    left = iota((n * 2, 8, 128), 2) < 64
    b = iota((n * 2, 8, 128), 1) & 3
    z = jnp.where(left, yl.reshape(n * 2, 8, 128), yr.reshape(n * 2, 8, 128))
    use = ((b == 0) & left) | ((b == 3) & (~left))
    parts = []
    for q in range(3):
        add = jnp.where(use, sroll(z, -q), jnp.zeros_like(z)).reshape(n, 2, 8, 128)
        parts.append((w[:, q] + add).reshape(n, 16, 128))
    return jnp.concatenate(parts, axis=1)


def one_hot(order):
    row = jnp.broadcast_to(order, (128, 128))
    return jnp.where(row == iota((128, 128), 0), 1.0, 0.0).astype(bf16)


def split3(x):
    h = x.astype(bf16)
    r = x - h.astype(f32)
    m = r.astype(bf16)
    l = (r - m.astype(f32)).astype(bf16)
    return h, m, l


def permute_nt(x, g):
    dims = (((1,), (1,)), ((), ()))
    h, m, l = (lax.dot_general(p, g, dims, preferred_element_type=f32) for p in split3(x))
    return h + m + l


def permute_nn(x, g):
    h, m, l = (jnp.dot(p, g, preferred_element_type=f32) for p in split3(x))
    return h + m + l


def quad(shape):
    r = iota(shape, 0)
    w = 1.0
    for i in (r >> 4, (r >> 2) & 3, r & 3):
        w = w * jnp.where((i == 0) | (i == 3), 1.0 / 6.0, 5.0 / 6.0)
    return w


def start_body(s_ref, c_ref, o_ref, ew_ref, ed_ref, w_ref, up_ref, dn_ref, mk_ref):
    g = one_hot(o_ref[...])
    rows = []
    for ref in (s_ref, c_ref):
        for f in range(F):
            for q in range(4):
                rows.append(ref[f, pl.ds(q, 16, stride=4), :])
    el = jnp.concatenate(
        [jnp.broadcast_to(ew_ref[...], (8, 128)), jnp.broadcast_to(ed_ref[...], (8, 128))], axis=0
    )
    x = permute_nt(jnp.concatenate(rows + [el], axis=0), g)
    mass = quad((64, 128)) * x[640:641]
    mk_ref[...] = x[640:656]
    s = x[:320].reshape(F, 64, 128) * mass[None]
    c = x[320:640].reshape(F, 64, 128)
    v = jnp.concatenate([s, mass[None], c, jnp.zeros((1, 64, 128), f32)], axis=0)
    w = zsum(v)
    w_ref[...] = w
    up_ref[...], dn_ref[...] = xpack(w)


def stiffness(v, kmat, kappa):
    n = v.shape[0]
    x = jnp.concatenate([v[i] for i in range(n)], axis=1)
    h = x.astype(bf16)
    l = (x - h.astype(f32)).astype(bf16)
    y = jnp.dot(kmat, jnp.concatenate([h, l, h], axis=0), preferred_element_type=f32)
    return jnp.stack([y[:, i * 128 : (i + 1) * 128] * kappa for i in range(n)], axis=0)


def state_body(w_ref, yl_ref, yr_ref, mk_ref, k_ref, sa_ref, im_ref, w2_ref, up_ref, dn_ref):
    v = zfill(yadd(w_ref[...], yl_ref[...], yr_ref[...]))
    im = 1.0 / v[F]
    im_ref[...] = im
    sa = jnp.concatenate([v[:F], v[F + 1 : 2 * F + 1]], axis=0) * im[None]
    sa_ref[...] = sa
    w = zsum(stiffness(sa, k_ref[...], mk_ref[8:9]))
    w2_ref[...] = w
    up_ref[...], dn_ref[...] = xpack(w)


def weights(p_ref):
    p = p_ref[...]
    h = p.astype(bf16)
    l = (p - h.astype(f32)).astype(bf16)
    hf, lf = h.astype(f32), l.astype(f32)
    col = iota((128, 256), 1)
    wide = (col < 128) | (col == 192)
    big = jnp.where(wide, hf[0:128], lf[0:128]).astype(bf16)
    thin = jnp.where(iota((128, 256), 1) < 16, hf[128:256], lf[128:256]).astype(bf16)
    wide16 = wide[:16]
    small = jnp.where(wide16, hf[256:272], lf[256:272]).astype(bf16)
    return dict(
        l2=big[0:64, 0:208],
        l2t=big[64:128, 0:192],
        l1=thin[0:64, 0:32],
        lot=thin[64:128, 0:32],
        lo=small[:, 0:208],
    )


def two(x):
    h = x.astype(bf16)
    return h, (x - h.astype(f32)).astype(bf16)


def stack8(x):
    h = x.astype(bf16).astype(f32)
    l = x - h
    return jnp.concatenate([h, l, h, l], axis=0).astype(bf16)


def mm(a, b):
    return jnp.dot(a, b, preferred_element_type=f32)


def nt(a, b):
    return lax.dot_general(a, b, (((1,), (1,)), ((), ())), preferred_element_type=f32)


def load8(ref, n0):
    return jnp.concatenate([ref[pl.ds(n0 + i, 8, stride=64), :] for i in range(CH)], axis=1)


def store8(ref, n0, x):
    for i in range(CH):
        ref[pl.ds(n0 + i, 8, stride=64), :] = x[:, i * 128 : (i + 1) * 128]


def put_fields(ref, x, ones):
    ref[0 : F * 64, :] = x.reshape(F * 64, 128)
    ref[F * 64 : F * 64 + 64, :] = jnp.full((64, 128), 1.0 if ones else 0.0, f32)
    ref[F * 64 + 64 :, :] = jnp.zeros((128, 128), f32)


def bias_rows():
    return jnp.where(iota((16, NW), 0) < 2, 1.0, 0.0).astype(bf16)


def forward(x8, w, ones):
    h1 = jnp.tanh(mm(w["l1"], stack8(x8)))
    h1h, h1l = two(h1)
    h2 = jnp.tanh(mm(w["l2"], jnp.concatenate([h1h, h1l, h1h, ones], axis=0)))
    return h1, h1h, h1l, h2


def closure_body(sa_ref, p_ref, c_ref, h1_ref, h2_ref, x_ref, o_ref):
    put_fields(x_ref, sa_ref[0:F], True)
    w = weights(p_ref)
    ones = bias_rows()

    def chunk(i, carry):
        n0 = i * CH
        h1, _, _, h2 = forward(load8(x_ref, n0), w, ones)
        lanes = pl.ds(pl.multiple_of(i * NW, NW), NW)
        h1_ref[:, lanes] = h1
        h2_ref[:, lanes] = h2
        h2h, h2l = two(h2)
        out = mm(w["lo"], jnp.concatenate([h2h, h2l, h2h, ones], axis=0))
        store8(o_ref, n0, out[0:8])
        return carry

    lax.fori_loop(0, 64 // CH, chunk, 0)
    c_ref[...] = o_ref[0 : F * 64].reshape(F, 64, 128)


def backward(x8, c8, h1, h1h, h1l, h2, h2h, h2l, w, acc):
    gw, gx, gc, gb = acc
    d2 = mm(w["lot"], stack8(c8)) * (1.0 - h2 * h2)
    d2h, d2l = two(d2)
    d1 = mm(w["l2t"], jnp.concatenate([d2h, d2l, d2h], axis=0)) * (1.0 - h1 * h1)
    d1h, d1l = two(d1)
    back = mm(w["lo"][:, 0:192], jnp.concatenate([d1h, d1l, d1h], axis=0))[8:16]
    gw = gw + nt(jnp.concatenate([d2h, d2l], axis=0), jnp.concatenate([h1h, h1l], axis=0))
    xh = x8.astype(bf16).astype(f32)
    ch = c8.astype(bf16).astype(f32)
    xs = jnp.concatenate([xh, x8 - xh], axis=0).astype(bf16)
    cs = jnp.concatenate([ch, c8 - ch], axis=0).astype(bf16)
    gx = gx + nt(xs, jnp.concatenate([d1h, d1l, d2h, d2l], axis=0))
    gc = gc + nt(cs, jnp.concatenate([h2h, h2l], axis=0))
    for i in range(CH):
        gb = gb + c8[:, i * 128 : (i + 1) * 128]
    return back, (gw, gx, gc, gb)


def no_grads():
    return (
        jnp.zeros((128, 128), f32),
        jnp.zeros((16, 256), f32),
        jnp.zeros((16, 128), f32),
        jnp.zeros((8, 128), f32),
    )


def second_body(
    w_ref, yl_ref, yr_ref, mk_ref, im_ref, sa_ref, c0_ref, p_ref, k_ref,
    part_ref, m1_ref, w2_ref, up_ref, dn_ref, gw_ref, gx_ref, gc_ref, gb_ref,
    x_ref, c_ref, o_ref, b_ref,
):
    im = im_ref[...] * STEP
    mass = quad((64, 128)) * mk_ref[0:1]
    v = zfill(yadd(w_ref[...], yl_ref[...], yr_ref[...])) * im[None]
    a2 = sa_ref[F:]
    s1 = sa_ref[0:F] + STEP * c0_ref[...] - v[0:F]
    put_fields(x_ref, s1, True)
    put_fields(c_ref, a2 * mass[None], False)
    w = weights(p_ref)
    ones = bias_rows()

    def chunk(i, acc):
        n0 = i * CH
        x8 = load8(x_ref, n0)
        c8 = load8(c_ref, n0)
        h1, h1h, h1l, h2 = forward(x8, w, ones)
        h2h, h2l = two(h2)
        out = mm(w["lo"], jnp.concatenate([h2h, h2l, h2h, ones], axis=0))
        store8(o_ref, n0, out[0:8])
        back, acc = backward(x8, c8, h1, h1h, h1l, h2, h2h, h2l, w, acc)
        store8(b_ref, n0, back)
        return acc

    acc = lax.fori_loop(0, 64 // CH, chunk, no_grads())
    gw_ref[...], gx_ref[...], gc_ref[...], gb_ref[...] = acc
    back = b_ref[0 : F * 64].reshape(F, 64, 128)
    a1 = a2 - v[F:] + (STEP / mass)[None] * back
    m1_ref[...] = a1 * mass[None]
    part_ref[0:F] = s1 + STEP * o_ref[0 : F * 64].reshape(F, 64, 128)
    part_ref[F:] = a1
    wz = zsum(stiffness(jnp.concatenate([s1, a1], axis=0), k_ref[...], mk_ref[8:9]))
    w2_ref[...] = wz
    up_ref[...], dn_ref[...] = xpack(wz)


def first_body(
    sa_ref, m1_ref, h1_ref, h2_ref, p_ref, gw_ref, gx_ref, gc_ref, gb_ref,
    back_ref, pay_ref, x_ref, c_ref, b_ref,
):
    put_fields(x_ref, sa_ref[0:F], True)
    put_fields(c_ref, m1_ref[...], False)
    w = weights(p_ref)

    def chunk(i, acc):
        n0 = i * CH
        lanes = pl.ds(pl.multiple_of(i * NW, NW), NW)
        h1, h2 = h1_ref[:, lanes], h2_ref[:, lanes]
        h1h, h1l = two(h1)
        h2h, h2l = two(h2)
        back, acc = backward(
            load8(x_ref, n0), load8(c_ref, n0), h1, h1h, h1l, h2, h2h, h2l, w, acc
        )
        store8(b_ref, n0, back)
        return acc

    gw, gx, gc, gb = lax.fori_loop(
        0, 64 // CH, chunk, (gw_ref[...], gx_ref[...], gc_ref[...], gb_ref[...])
    )
    back_ref[...] = b_ref[0 : F * 64].reshape(F, 64, 128)

    def fold(t):
        return t + pltpu.roll(t, 64, 1)

    gw = fold(gw[0:64] + gw[64:128])
    gx1 = fold(gx[0:8, 0:128] + gx[8:16, 0:128])
    gx2 = fold(gx[0:8, 128:256] + gx[8:16, 128:256])
    gc = fold(gc[0:8] + gc[8:16])
    gbs = jnp.broadcast_to(jnp.sum(gb, axis=1, keepdims=True), (8, 128))
    left = iota((32, 128), 1) < 64
    scale = STEP / 256.0
    pay_ref[0:32] = jnp.where(left, gw[0:32], gw[32:64]) * scale
    pay_ref[32:40] = jnp.where(left[:8], gx1, gx2) * scale
    pay_ref[40:48] = jnp.where(left[:8], gc, gbs) * scale


def finish_body(
    w_ref, yl_ref, yr_ref, mk_ref, im_ref, part_ref, back_ref, o_ref, s_ref, a_ref
):
    im = im_ref[...] * STEP
    mass = quad((64, 128)) * mk_ref[0:1]
    v = zfill(yadd(w_ref[...], yl_ref[...], yr_ref[...])) * im[None]
    s2 = part_ref[0:F] - v[0:F]
    a0 = (part_ref[F:] - v[F:]) * mass[None] + STEP * back_ref[...]
    x = jnp.concatenate([s2.reshape(320, 128), a0.reshape(320, 128)], axis=0)
    y = permute_nn(x, one_hot(o_ref[...]))
    for i, ref in enumerate((s_ref, a_ref)):
        for f in range(F):
            for q in range(4):
                r = (i * F + f) * 64 + q * 16
                ref[f, pl.ds(q, 16, stride=4), :] = y[r : r + 16]


def call(body, outs, args, scratch=(), flops=0, trans=0):
    shapes = [jax.ShapeDtypeStruct(s, f32) for s in outs]
    return pl.pallas_call(
        body,
        out_shape=shapes,
        in_specs=[VM] * len(args),
        out_specs=[VM] * len(shapes),
        scratch_shapes=[pltpu.VMEM(s, f32) for s in scratch],
        cost_estimate=pl.CostEstimate(
            flops=flops, bytes_accessed=2000000, transcendentals=trans
        ),
        compiler_params=pltpu.CompilerParams(vmem_limit_bytes=40 * 1024 * 1024),
    )(*args)


def shift(x, axis, step):
    n = lax.axis_size(axis)
    return lax.ppermute(x, axis, [(i, (i + step) % n) for i in range(n)])


def both_ways(up, dn, axis):
    return shift(up, axis, 1), shift(dn, axis, -1)


def partner_maps():
    maps = []
    for dim in range(4):
        group = []
        for k in (1, 2, 3):
            perm = []
            for d in range(256):
                s, c = d // 16, d % 16
                zl, y, core, zh, x = s // 8, (s // 2) % 4, s % 2, c // 4, c % 4
                if dim == 0:
                    v = (core * 2 + zl) ^ k
                    core, zl = v // 2, v % 2
                elif dim == 1:
                    y = (y + k) % 4
                elif dim == 2:
                    x = (x + k) % 4
                else:
                    zh = (zh + k) % 4
                perm.append((d, (zl * 8 + y * 2 + core) * 16 + zh * 4 + x))
            group.append(perm)
        maps.append(group)
    return maps


def all_sum(x):
    if (lax.axis_size("sub"), lax.axis_size("col")) != (16, 16):
        return lax.psum(x, ("sub", "col"))
    for group in partner_maps():
        others = [lax.ppermute(x, ("sub", "col"), perm) for perm in group]
        x = x + others[0] + others[1] + others[2]
    return x


def pack_weights(in_weight, in_bias, mid_weight, mid_bias, out_weight, out_bias):
    def wide(a):
        return jnp.pad(a, ((0, 0), (0, 256 - a.shape[1])))

    w1 = jnp.concatenate([in_weight, in_bias[:, None], jnp.zeros((64, 2), f32)], axis=1)
    wot = jnp.pad(out_weight.T, ((0, 0), (0, 3)))
    wo = jnp.concatenate([out_weight] * 3 + [out_bias[:, None]] * 2, axis=1)
    return jnp.concatenate(
        [
            wide(jnp.concatenate([mid_weight] * 3 + [mid_bias[:, None]] * 2, axis=1)),
            wide(jnp.concatenate([mid_weight.T] * 3, axis=1)),
            wide(jnp.concatenate([w1] * 4, axis=1)),
            wide(jnp.concatenate([wot] * 4, axis=1)),
            jnp.pad(wide(wo), ((0, 3), (0, 0))),
            jnp.pad(wide(jnp.concatenate([in_weight.T] * 3, axis=1)), ((0, 3), (0, 0))),
        ],
        axis=0,
    )


def on_device(
    initial_state,
    state_cotangent,
    element_order,
    element_weight,
    element_diffusivity,
    in_weight,
    in_bias,
    mid_weight,
    mid_bias,
    out_weight,
    out_bias,
):
    kmat = jnp.asarray(stiffness_matrix())
    pw = pack_weights(in_weight, in_bias, mid_weight, mid_bias, out_weight, out_bias)

    def faces(w, up, dn, n):
        rp, rm = both_ways(up, dn, "sub")
        w, y = call(
            lambda *r: xy_body(n, *r), [(n, 3, 2, 8, 128), (n, 2, 8, 128)], [w, rp, rm]
        )
        yl, yr = both_ways(y, y, "col")
        return w, yl, yr

    w, up, dn, mk = call(
        start_body,
        [(12, 48, 128), (18, 8, 128), (18, 8, 128), (16, 128)],
        [
            initial_state,
            state_cotangent,
            element_order,
            element_weight.reshape(1, 128),
            element_diffusivity.reshape(1, 128),
        ],
    )
    w, yl, yr = faces(w, up, dn, 12)
    ten = [(10, 48, 128), (15, 8, 128), (15, 8, 128)]
    sa, im, w, up, dn = call(
        state_body, [(10, 64, 128), (64, 128)] + ten, [w, yl, yr, mk, kmat]
    )
    c0, h1, h2 = call(
        closure_body,
        [(F, 64, 128), (64, 8192), (64, 8192)],
        [sa, pw],
        [(512, 128)] * 2,
        flops=300000000,
        trans=1000000,
    )
    w, yl, yr = faces(w, up, dn, 10)
    part, m1, w, up, dn, gw, gx, gc, gb = call(
        second_body,
        [(10, 64, 128), (F, 64, 128)] + ten + [(128, 128), (16, 256), (16, 128), (8, 128)],
        [w, yl, yr, mk, im, sa, c0, pw, kmat],
        [(512, 128)] * 4,
        flops=900000000,
        trans=1000000,
    )
    back, pay = call(
        first_body,
        [(F, 64, 128), (48, 128)],
        [sa, m1, h1, h2, pw, gw, gx, gc, gb],
        [(512, 128)] * 3,
        flops=600000000,
    )
    w, yl, yr = faces(w, up, dn, 10)
    pay = all_sum(pay)
    out_state, out_adj = call(
        finish_body,
        [(F, 64, 128), (F, 64, 128)],
        [w, yl, yr, mk, im, part, back, element_order],
    )
    return (
        out_state,
        out_adj,
        pay[32:37, 0:64].T,
        pay[37, 0:64],
        jnp.concatenate([pay[0:32, 0:64], pay[0:32, 64:128]], axis=0),
        pay[37, 64:128],
        pay[40:45, 0:64],
        pay[40:45, 64],
    )


def solution(mesh):
    split = P(None, None, ("sub", "col"))
    placed = (split, split, P(("sub", "col"), None), P(("sub", "col")), P(("sub", "col")))
    return jax.shard_map(
        on_device,
        mesh=mesh,
        in_specs=placed + (P(),) * 6,
        out_specs=(split, split) + (P(),) * 6,
        check_vma=False,
    )
```

```python
import math

import jax
import jax.numpy as jnp
import numpy as np
from jax import lax
from jax.experimental import pallas as pl
from jax.experimental.pallas import tpu as pltpu
from jax.sharding import PartitionSpec as P

F = 5
STEP = 0.05
CH = 16
NW = CH * 128
f32, bf16 = jnp.float32, jnp.bfloat16
VM = pl.BlockSpec(memory_space=pltpu.VMEM)


def stiffness_matrix():
    at = [-1.0, -math.sqrt(0.2), math.sqrt(0.2), 1.0]
    w = np.array([1.0 / 6.0, 5.0 / 6.0, 5.0 / 6.0, 1.0 / 6.0])
    prods = [np.prod([at[r] - at[p] for p in range(4) if p != r]) for r in range(4)]
    d = np.zeros((4, 4))
    for r in range(4):
        for c in range(4):
            if r == c:
                d[r, c] = sum(1.0 / (at[r] - at[p]) for p in range(4) if p != r)
            else:
                d[r, c] = prods[r] / (prods[c] * (at[r] - at[c]))
    s = d.T @ np.diag(w) @ d
    m = np.diag(w)
    k = np.kron(m, np.kron(s, m)) + np.kron(m, np.kron(m, s)) + np.kron(s, np.kron(m, m))
    k = k.astype(np.float32)
    hi = k.astype(bf16).astype(np.float32)
    lo = k - hi
    return np.concatenate([hi, hi, lo], axis=1).astype(bf16)


def iota(shape, dim):
    return lax.broadcasted_iota(jnp.int32, shape, dim)


def next_k(x):
    ax = x.ndim - 1
    lane = iota(x.shape, ax) & 63
    return jnp.where(lane == 63, pltpu.roll(x, 63, ax), pltpu.roll(x, 127, ax))


def prev_k(x):
    ax = x.ndim - 1
    lane = iota(x.shape, ax) & 63
    return jnp.where(lane == 0, pltpu.roll(x, 65, ax), pltpu.roll(x, 1, ax))


def zsum(v):
    n = v.shape[0]
    top = v[:, 48:64] + next_k(v[:, 0:16])
    return jnp.concatenate([v[:, 16:48], top], axis=1)


def zfill(w):
    return jnp.concatenate([prev_k(w[:, 32:48]), w], axis=1)


def sroll(x, s):
    return pltpu.roll(x, s % 8, x.ndim - 2) if s % 8 else x


def xpack(w):
    n = w.shape[0]
    h = n // 2
    t = w.reshape(n, 3, 2, 8, 128)
    v0, v1 = t[:, :, 0].reshape(n * 3, 8, 128), t[:, :, 1].reshape(n * 3, 8, 128)
    low = iota((h * 3, 8, 128), 1) < 4
    up = jnp.where(low, sroll(v1[: h * 3], 4), v1[h * 3 :])
    dn = jnp.where(low, v0[: h * 3], sroll(v0[h * 3 :], 4))
    return up, dn


def xadd(w, rp, rm):
    n = w.shape[0]
    h = n // 2
    t = w.reshape(n, 3, 2, 8, 128)
    v0, v1 = t[:, :, 0].reshape(n * 3, 8, 128), t[:, :, 1].reshape(n * 3, 8, 128)
    low = iota((h * 3, 8, 128), 1) < 4
    zero = jnp.zeros_like(rp)
    a0 = jnp.concatenate([jnp.where(low, rp, zero), jnp.where(low, sroll(rp, 4), zero)], axis=0)
    a1 = jnp.concatenate([jnp.where(low, zero, sroll(rm, 4)), jnp.where(low, zero, rm)], axis=0)
    v0, v1 = v0 + a0, v1 + a1
    return v0, v1


def ylocal(v):
    b = iota(v.shape, 1) & 3
    left = iota(v.shape, 2) < 64
    d = jnp.where(b == 0, sroll(v, 5), sroll(v, 3))
    d = pltpu.roll(d, 64, 2)
    zero = jnp.zeros_like(v)
    here = ((b == 0) & (~left)) | ((b == 3) & left)
    out = ((b == 0) & left) | ((b == 3) & (~left))
    return v + jnp.where(here, d, zero), jnp.where(out, d, zero)


def xy_body(n, w_ref, rp_ref, rm_ref, wo_ref, y_ref):
    w = w_ref[...]
    v0, v1 = xadd(w, rp_ref[...], rm_ref[...])
    for part, v in enumerate((v0, v1)):
        v, e = ylocal(v)
        wo_ref[:, :, part] = v.reshape(n, 3, 8, 128)
        e = e.reshape(n, 3, 8, 128)
        y_ref[:, part] = e[:, 0] + sroll(e[:, 1], 1) + sroll(e[:, 2], 2)


def yadd(w, yl, yr):
    n = w.shape[0]
    left = iota((n * 2, 8, 128), 2) < 64
    b = iota((n * 2, 8, 128), 1) & 3
    z = jnp.where(left, yl.reshape(n * 2, 8, 128), yr.reshape(n * 2, 8, 128))
    use = ((b == 0) & left) | ((b == 3) & (~left))
    parts = []
    for q in range(3):
        add = jnp.where(use, sroll(z, -q), jnp.zeros_like(z)).reshape(n, 2, 8, 128)
        parts.append((w[:, q] + add).reshape(n, 16, 128))
    return jnp.concatenate(parts, axis=1)


def one_hot(order):
    row = jnp.broadcast_to(order, (128, 128))
    return jnp.where(row == iota((128, 128), 0), 1.0, 0.0).astype(bf16)


def split3(x):
    h = x.astype(bf16)
    r = x - h.astype(f32)
    m = r.astype(bf16)
    l = (r - m.astype(f32)).astype(bf16)
    return h, m, l


def permute_nt(x, g):
    dims = (((1,), (1,)), ((), ()))
    h, m, l = (lax.dot_general(p, g, dims, preferred_element_type=f32) for p in split3(x))
    return h + m + l


def permute_nn(x, g):
    h, m, l = (jnp.dot(p, g, preferred_element_type=f32) for p in split3(x))
    return h + m + l


def quad(shape):
    r = iota(shape, 0)
    w = 1.0
    for i in (r >> 4, (r >> 2) & 3, r & 3):
        w = w * jnp.where((i == 0) | (i == 3), 1.0 / 6.0, 5.0 / 6.0)
    return w


def fetch(srcs, dsts, sems):
    copies = [pltpu.make_async_copy(a, b, sems.at[i]) for i, (a, b) in enumerate(zip(srcs, dsts))]
    for c in copies:
        c.start()
    for c in copies:
        c.wait()


def start_body(s_in, c_in, o_in, ew_in, ed_in, w_ref, up_ref, dn_ref, mk_ref, g_ref, *scratch):
    s_ref, c_ref, o_ref, ew_ref, ed_ref, sems = scratch
    fetch((s_in, c_in, o_in, ew_in, ed_in), scratch[:5], sems)
    g = one_hot(o_ref[...])
    g_ref[...] = g
    rows = []
    for ref in (s_ref, c_ref):
        for f in range(F):
            for q in range(4):
                rows.append(ref[f, pl.ds(q, 16, stride=4), :])
    el = jnp.concatenate(
        [jnp.broadcast_to(ew_ref[...], (8, 128)), jnp.broadcast_to(ed_ref[...], (8, 128))], axis=0
    )
    x = permute_nt(jnp.concatenate(rows + [el], axis=0), g)
    mass = quad((64, 128)) * x[640:641]
    mk_ref[...] = x[640:656]
    s = x[:320].reshape(F, 64, 128) * mass[None]
    c = x[320:640].reshape(F, 64, 128)
    v = jnp.concatenate([s, mass[None], c, jnp.zeros((1, 64, 128), f32)], axis=0)
    w = zsum(v)
    w_ref[...] = w
    up_ref[...], dn_ref[...] = xpack(w)


def stiffness(v, kmat, kappa):
    n = v.shape[0]
    x = jnp.concatenate([v[i] for i in range(n)], axis=1)
    h = x.astype(bf16)
    l = (x - h.astype(f32)).astype(bf16)
    y = jnp.dot(kmat, jnp.concatenate([h, l, h], axis=0), preferred_element_type=f32)
    return jnp.stack([y[:, i * 128 : (i + 1) * 128] * kappa for i in range(n)], axis=0)


def state_body(w_ref, yl_ref, yr_ref, mk_ref, k_ref, sa_ref, im_ref, w2_ref, up_ref, dn_ref):
    v = zfill(yadd(w_ref[...], yl_ref[...], yr_ref[...]))
    im = 1.0 / v[F]
    im_ref[...] = im
    sa = jnp.concatenate([v[:F], v[F + 1 : 2 * F + 1]], axis=0) * im[None]
    sa_ref[...] = sa
    w = zsum(stiffness(sa, k_ref[...], mk_ref[8:9]))
    w2_ref[...] = w
    up_ref[...], dn_ref[...] = xpack(w)


def prepare_body(w1_in, b1_in, w2_in, b2_in, wo_in, bo_in, p_ref, *scratch):
    fetch((w1_in, b1_in, w2_in, b2_in, wo_in, bo_in), scratch[:6], scratch[6])
    w1, b1, w2, b2, wo, bo = (r[...] for r in scratch[:6])
    z = jnp.zeros((64, 64), f32)
    pad3 = jnp.zeros((3, 64), f32)
    w1b = jnp.concatenate([w1, b1, jnp.zeros((2, 64), f32)], axis=0)
    w1p = jnp.concatenate([w1, pad3], axis=0)
    wop = jnp.concatenate([wo, pad3], axis=0)

    def columns(parts, rows):
        if rows < 256:
            parts = parts + [jnp.zeros((256 - rows, 64), f32)]
        return jnp.concatenate(parts, axis=0).T

    l2 = columns([w2.T] * 3 + [jnp.broadcast_to(b2, (8, 64))], 200)
    l2t = columns([w2] * 3, 192)
    l1 = columns([w1b] * 4, 32)
    lot = columns([wop] * 4, 32)
    both = jnp.concatenate([wop, w1p], axis=0)
    diag = iota((16, 5), 0) == iota((16, 5), 1)
    bias = jnp.sum(jnp.where(diag, jnp.broadcast_to(bo, (16, 5)), 0.0), axis=1, keepdims=True)
    bias = jnp.where(iota((16, 64), 1) < 2, jnp.broadcast_to(bias, (16, 64)), z[:16])
    small = jnp.concatenate([both, both, both, bias], axis=1)

    def parts(p, high):
        h = p.astype(bf16).astype(f32)
        return jnp.where(high, h, p - h).astype(bf16)

    col = iota((128, 256), 1)
    high = (col < 128) | (col == 192)
    p_ref[0:128] = parts(jnp.concatenate([l2, l2t], axis=0), high)
    p_ref[128:256] = parts(jnp.concatenate([l1, lot], axis=0), col < 16)
    p_ref[256:272] = parts(small, high[:16])


def weights(p_ref):
    return dict(
        l2=p_ref[0:64, 0:208],
        l2t=p_ref[64:128, 0:192],
        l1=p_ref[128:192, 0:32],
        lot=p_ref[192:256, 0:32],
        lo=p_ref[256:272, 0:208],
    )


def two(x):
    h = x.astype(bf16)
    return h, (x - h.astype(f32)).astype(bf16)


def stack8(x):
    h = x.astype(bf16).astype(f32)
    l = x - h
    return jnp.concatenate([h, l, h, l], axis=0).astype(bf16)


def mm(a, b):
    return jnp.dot(a, b, preferred_element_type=f32)


def nt(a, b):
    return lax.dot_general(a, b, (((1,), (1,)), ((), ())), preferred_element_type=f32)


def load8(ref, n0):
    return jnp.concatenate([ref[pl.ds(n0 + i, 8, stride=64), :] for i in range(CH)], axis=1)


def store8(ref, n0, x):
    for i in range(CH):
        ref[pl.ds(n0 + i, 8, stride=64), :] = x[:, i * 128 : (i + 1) * 128]


def put_fields(ref, x, ones):
    ref[0 : F * 64, :] = x.reshape(F * 64, 128)
    ref[F * 64 : F * 64 + 64, :] = jnp.full((64, 128), 1.0 if ones else 0.0, f32)
    ref[F * 64 + 64 :, :] = jnp.zeros((128, 128), f32)


def bias_rows():
    return jnp.where(iota((16, NW), 0) < 2, 1.0, 0.0).astype(bf16)


def forward(x8, w, ones):
    h1 = jnp.tanh(mm(w["l1"], stack8(x8)))
    h1h, h1l = two(h1)
    h2 = jnp.tanh(mm(w["l2"], jnp.concatenate([h1h, h1l, h1h, ones], axis=0)))
    return h1, h1h, h1l, h2


def closure_body(sa_ref, p_ref, c_ref, h1_ref, h2_ref, x_ref, o_ref):
    put_fields(x_ref, sa_ref[0:F], True)
    w = weights(p_ref)
    ones = bias_rows()

    def chunk(i, carry):
        n0 = i * CH
        h1, _, _, h2 = forward(load8(x_ref, n0), w, ones)
        lanes = pl.ds(pl.multiple_of(i * NW, NW), NW)
        h1_ref[:, lanes] = h1
        h2_ref[:, lanes] = h2
        h2h, h2l = two(h2)
        out = mm(w["lo"], jnp.concatenate([h2h, h2l, h2h, ones], axis=0))
        store8(o_ref, n0, out[0:8])
        return carry

    lax.fori_loop(0, 64 // CH, chunk, 0)
    c_ref[...] = o_ref[0 : F * 64].reshape(F, 64, 128)


def backward(x8, c8, h1, h1h, h1l, h2, h2h, h2l, w, acc):
    gw, gx, gc, gb = acc
    d2 = mm(w["lot"], stack8(c8)) * (1.0 - h2 * h2)
    d2h, d2l = two(d2)
    d1 = mm(w["l2t"], jnp.concatenate([d2h, d2l, d2h], axis=0)) * (1.0 - h1 * h1)
    d1h, d1l = two(d1)
    back = mm(w["lo"][:, 0:192], jnp.concatenate([d1h, d1l, d1h], axis=0))[8:16]
    gw = gw + nt(jnp.concatenate([d2h, d2l], axis=0), jnp.concatenate([h1h, h1l], axis=0))
    xh = x8.astype(bf16).astype(f32)
    ch = c8.astype(bf16).astype(f32)
    xs = jnp.concatenate([xh, x8 - xh], axis=0).astype(bf16)
    cs = jnp.concatenate([ch, c8 - ch], axis=0).astype(bf16)
    gx = gx + nt(xs, jnp.concatenate([d1h, d1l, d2h, d2l], axis=0))
    gc = gc + nt(cs, jnp.concatenate([h2h, h2l], axis=0))
    for i in range(CH):
        gb = gb + c8[:, i * 128 : (i + 1) * 128]
    return back, (gw, gx, gc, gb)


def no_grads():
    return (
        jnp.zeros((128, 128), f32),
        jnp.zeros((16, 256), f32),
        jnp.zeros((16, 128), f32),
        jnp.zeros((8, 128), f32),
    )


def second_body(
    w_ref, yl_ref, yr_ref, mk_ref, im_ref, sa_ref, c0_ref, p_ref, k_ref,
    part_ref, m1_ref, w2_ref, up_ref, dn_ref, gw_ref, gx_ref, gc_ref, gb_ref,
    x_ref, c_ref, o_ref, b_ref,
):
    im = im_ref[...] * STEP
    mass = quad((64, 128)) * mk_ref[0:1]
    v = zfill(yadd(w_ref[...], yl_ref[...], yr_ref[...])) * im[None]
    a2 = sa_ref[F:]
    s1 = sa_ref[0:F] + STEP * c0_ref[...] - v[0:F]
    put_fields(x_ref, s1, True)
    put_fields(c_ref, a2 * mass[None], False)
    w = weights(p_ref)
    ones = bias_rows()

    def chunk(i, acc):
        n0 = i * CH
        x8 = load8(x_ref, n0)
        c8 = load8(c_ref, n0)
        h1, h1h, h1l, h2 = forward(x8, w, ones)
        h2h, h2l = two(h2)
        out = mm(w["lo"], jnp.concatenate([h2h, h2l, h2h, ones], axis=0))
        store8(o_ref, n0, out[0:8])
        back, acc = backward(x8, c8, h1, h1h, h1l, h2, h2h, h2l, w, acc)
        store8(b_ref, n0, back)
        return acc

    acc = lax.fori_loop(0, 64 // CH, chunk, no_grads())
    gw_ref[...], gx_ref[...], gc_ref[...], gb_ref[...] = acc
    back = b_ref[0 : F * 64].reshape(F, 64, 128)
    a1 = a2 - v[F:] + (STEP / mass)[None] * back
    m1_ref[...] = a1 * mass[None]
    part_ref[0:F] = s1 + STEP * o_ref[0 : F * 64].reshape(F, 64, 128)
    part_ref[F:] = a1
    wz = zsum(stiffness(jnp.concatenate([s1, a1], axis=0), k_ref[...], mk_ref[8:9]))
    w2_ref[...] = wz
    up_ref[...], dn_ref[...] = xpack(wz)


def first_body(
    sa_ref, m1_ref, h1_ref, h2_ref, p_ref, gw_ref, gx_ref, gc_ref, gb_ref,
    back_ref, pay_ref, x_ref, c_ref, b_ref,
):
    put_fields(x_ref, sa_ref[0:F], True)
    put_fields(c_ref, m1_ref[...], False)
    w = weights(p_ref)

    def chunk(i, acc):
        n0 = i * CH
        lanes = pl.ds(pl.multiple_of(i * NW, NW), NW)
        h1, h2 = h1_ref[:, lanes], h2_ref[:, lanes]
        h1h, h1l = two(h1)
        h2h, h2l = two(h2)
        back, acc = backward(
            load8(x_ref, n0), load8(c_ref, n0), h1, h1h, h1l, h2, h2h, h2l, w, acc
        )
        store8(b_ref, n0, back)
        return acc

    gw, gx, gc, gb = lax.fori_loop(
        0, 64 // CH, chunk, (gw_ref[...], gx_ref[...], gc_ref[...], gb_ref[...])
    )
    back_ref[...] = b_ref[0 : F * 64].reshape(F, 64, 128)

    def fold(t):
        return t + pltpu.roll(t, 64, 1)

    gw = fold(gw[0:64] + gw[64:128])
    gx1 = fold(gx[0:8, 0:128] + gx[8:16, 0:128])
    gx2 = fold(gx[0:8, 128:256] + gx[8:16, 128:256])
    gc = fold(gc[0:8] + gc[8:16])
    gbs = jnp.broadcast_to(jnp.sum(gb, axis=1, keepdims=True), (8, 128))
    left = iota((32, 128), 1) < 64
    scale = STEP / 256.0
    pay_ref[0:32] = jnp.where(left, gw[0:32], gw[32:64]) * scale
    pay_ref[32:40] = jnp.where(left[:8], gx1, gx2) * scale
    pay_ref[40:48] = jnp.where(left[:8], gc, gbs) * scale


def finish_body(
    w_ref, yl_ref, yr_ref, mk_ref, im_ref, part_ref, back_ref, g_ref, p_ref,
    s_ref, a_ref, gw1_ref, gb1_ref, gw2_ref, gb2_ref, gwo_ref, gbo_ref,
):
    im = im_ref[...] * STEP
    mass = quad((64, 128)) * mk_ref[0:1]
    v = zfill(yadd(w_ref[...], yl_ref[...], yr_ref[...])) * im[None]
    s2 = part_ref[0:F] - v[0:F]
    a0 = (part_ref[F:] - v[F:]) * mass[None] + STEP * back_ref[...]
    x = jnp.concatenate([s2.reshape(320, 128), a0.reshape(320, 128)], axis=0)
    y = permute_nn(x, g_ref[...])
    for i, ref in enumerate((s_ref, a_ref)):
        for f in range(F):
            for q in range(4):
                r = (i * F + f) * 64 + q * 16
                ref[f, pl.ds(q, 16, stride=4), :] = y[r : r + 16]
    pay = p_ref[0]
    for i in range(1, 8):
        pay = pay + p_ref[i]
    gw2_ref[0:32] = pay[0:32, 0:64]
    other = pltpu.roll(pay, 64, 1)
    gw2_ref[32:64] = other[0:32, 0:64]
    gw1_ref[...] = pay[32:37, 0:64]
    gb1_ref[...] = pay[37:38, 0:64]
    gb2_ref[...] = other[37:38, 0:64]
    gwo_ref[...] = pay[40:45, 0:64]
    diag = iota((8, 5), 0) == iota((8, 5), 1)
    gbo_ref[...] = jnp.sum(jnp.where(diag, other[40:48, 0:5], 0.0), axis=0, keepdims=True)


def call(body, outs, args, scratch=(), flops=0, trans=0, space=pltpu.VMEM):
    if space == pltpu.HBM:
        args = [pltpu.with_memory_space_constraint(x, pltpu.HBM) for x in args]
    shapes = [s if hasattr(s, "dtype") else jax.ShapeDtypeStruct(s, f32) for s in outs]
    scratch = [s if hasattr(s, "memory_space") or hasattr(s, "dtype") else pltpu.VMEM(s, f32) for s in scratch]
    return pl.pallas_call(
        body,
        out_shape=shapes,
        in_specs=[pl.BlockSpec(memory_space=space)] * len(args),
        out_specs=[VM] * len(shapes),
        scratch_shapes=scratch,
        cost_estimate=pl.CostEstimate(
            flops=flops, bytes_accessed=2000000, transcendentals=trans
        ),
        compiler_params=pltpu.CompilerParams(vmem_limit_bytes=40 * 1024 * 1024),
    )(*args)


def shift(x, axis, step):
    n = lax.axis_size(axis)
    return lax.ppermute(x, axis, [(i, (i + step) % n) for i in range(n)])


def both_ways(up, dn, axis):
    return shift(up, axis, 1), shift(dn, axis, -1)


def place(d):
    s, c = d // 16, d % 16
    return s // 8, (s // 2) % 4, s % 2, c // 4, c % 4


def together(fixed):
    groups = {}
    for d in range(256):
        groups.setdefault(tuple(place(d)[i] for i in fixed), []).append(d)
    return [groups[k] for k in sorted(groups)]


def send_to_all(x, groups):
    n = len(groups[0])
    y = jnp.broadcast_to(x[None], (n,) + x.shape)
    return lax.all_to_all(y, ("sub", "col"), 0, 0, axis_index_groups=groups, tiled=True)


def all_sum(x):
    if (lax.axis_size("sub"), lax.axis_size("col")) != (16, 16):
        x = lax.psum(x, ("sub", "col"))
        return jnp.concatenate([x[None], jnp.zeros((7,) + x.shape, f32)], axis=0)
    x = x + lax.ppermute(x, ("sub", "col"), [(d, d ^ 16) for d in range(256)])
    x = send_to_all(x, together((0, 2, 3))).sum(0)
    return send_to_all(x, together((1, 2, 4)))


def on_device(
    initial_state,
    state_cotangent,
    element_order,
    element_weight,
    element_diffusivity,
    in_weight,
    in_bias,
    mid_weight,
    mid_bias,
    out_weight,
    out_bias,
):
    kmat = jnp.asarray(stiffness_matrix())
    hot = jax.ShapeDtypeStruct((128, 128), bf16)

    def in_device(w, up, dn, n):
        rp, rm = both_ways(up, dn, "sub")
        return call(
            lambda *r: xy_body(n, *r), [(n, 3, 2, 8, 128), (n, 2, 8, 128)], [w, rp, rm]
        )

    def faces(w, up, dn, n):
        w, y = in_device(w, up, dn, n)
        yl, yr = both_ways(y, y, "col")
        return w, yl, yr

    w, up, dn, mk, g = call(
        start_body,
        [(12, 48, 128), (18, 8, 128), (18, 8, 128), (16, 128), hot],
        [
            initial_state,
            state_cotangent,
            element_order,
            element_weight.reshape(1, 128),
            element_diffusivity.reshape(1, 128),
        ],
        [(F, 64, 128), (F, 64, 128), pltpu.VMEM((1, 128), jnp.int32), (1, 128), (1, 128)]
        + [pltpu.SemaphoreType.DMA((5,))],
        space=pltpu.HBM,
    )
    (pw,) = call(
        prepare_body,
        [jax.ShapeDtypeStruct((272, 256), bf16)],
        [
            in_weight.T,
            in_bias.reshape(1, 64),
            mid_weight,
            mid_bias.reshape(1, 64),
            out_weight,
            out_bias.reshape(1, 5),
        ],
        [(5, 64), (1, 64), (64, 64), (1, 64), (5, 64), (1, 5), pltpu.SemaphoreType.DMA((6,))],
        flops=2000000,
        space=pltpu.HBM,
    )
    w, yl, yr = faces(w, up, dn, 12)
    ten = [(10, 48, 128), (15, 8, 128), (15, 8, 128)]
    sa, im, w, up, dn = call(
        state_body, [(10, 64, 128), (64, 128)] + ten, [w, yl, yr, mk, kmat]
    )
    c0, h1, h2 = call(
        closure_body,
        [(F, 64, 128), (64, 8192), (64, 8192)],
        [sa, pw],
        [(512, 128)] * 2,
        flops=300000000,
        trans=1000000,
    )
    w, yl, yr = faces(w, up, dn, 10)
    part, m1, w, up, dn, gw, gx, gc, gb = call(
        second_body,
        [(10, 64, 128), (F, 64, 128)] + ten + [(128, 128), (16, 256), (16, 128), (8, 128)],
        [w, yl, yr, mk, im, sa, c0, pw, kmat],
        [(512, 128)] * 4,
        flops=900000000,
        trans=1000000,
    )
    back, pay = call(
        first_body,
        [(F, 64, 128), (48, 128)],
        [sa, m1, h1, h2, pw, gw, gx, gc, gb],
        [(512, 128)] * 3,
        flops=600000000,
    )
    w, y = in_device(w, up, dn, 10)
    pay, y = lax.optimization_barrier((pay, y))
    yl, yr = both_ways(y, y, "col")
    terms = all_sum(pay)
    out_state, out_adj, gw1, gb1, gw2, gb2, gwo, gbo = call(
        finish_body,
        [(F, 64, 128), (F, 64, 128), (5, 64), (1, 64), (64, 64), (1, 64), (5, 64), (1, 5)],
        [w, yl, yr, mk, im, part, back, g, terms],
    )
    return (
        out_state,
        out_adj,
        gw1.T,
        gb1.reshape(64),
        gw2,
        gb2.reshape(64),
        gwo,
        gbo.reshape(5),
    )


def solution(mesh):
    split = P(None, None, ("sub", "col"))
    placed = (split, split, P(("sub", "col"), None), P(("sub", "col")), P(("sub", "col")))
    return jax.shard_map(
        on_device,
        mesh=mesh,
        in_specs=placed + (P(),) * 6,
        out_specs=(split, split) + (P(),) * 6,
        check_vma=False,
    )
```

```python
import math

import jax
import jax.numpy as jnp
import numpy as np
from jax import lax
from jax.experimental import pallas as pl
from jax.experimental.pallas import tpu as pltpu
from jax.sharding import PartitionSpec as P

F = 5
STEP = 0.05
CH = 32
NW = CH * 128
f32, bf16 = jnp.float32, jnp.bfloat16
VM = pl.BlockSpec(memory_space=pltpu.VMEM)


def stiffness_matrix():
    at = [-1.0, -math.sqrt(0.2), math.sqrt(0.2), 1.0]
    w = np.array([1.0 / 6.0, 5.0 / 6.0, 5.0 / 6.0, 1.0 / 6.0])
    prods = [np.prod([at[r] - at[p] for p in range(4) if p != r]) for r in range(4)]
    d = np.zeros((4, 4))
    for r in range(4):
        for c in range(4):
            if r == c:
                d[r, c] = sum(1.0 / (at[r] - at[p]) for p in range(4) if p != r)
            else:
                d[r, c] = prods[r] / (prods[c] * (at[r] - at[c]))
    s = d.T @ np.diag(w) @ d
    m = np.diag(w)
    k = np.kron(m, np.kron(s, m)) + np.kron(m, np.kron(m, s)) + np.kron(s, np.kron(m, m))
    return k.astype(np.float32)


def iota(shape, dim):
    return lax.broadcasted_iota(jnp.int32, shape, dim)


def next_k(x):
    ax = x.ndim - 1
    lane = iota(x.shape, ax) & 63
    return jnp.where(lane == 63, pltpu.roll(x, 63, ax), pltpu.roll(x, 127, ax))


def prev_k(x):
    ax = x.ndim - 1
    lane = iota(x.shape, ax) & 63
    return jnp.where(lane == 0, pltpu.roll(x, 65, ax), pltpu.roll(x, 1, ax))


def zsum(v):
    n = v.shape[0]
    top = v[:, 48:64] + next_k(v[:, 0:16])
    return jnp.concatenate([v[:, 16:48], top], axis=1)


def zfill(w):
    return jnp.concatenate([prev_k(w[:, 32:48]), w], axis=1)


def sroll(x, s):
    return pltpu.roll(x, s % 8, x.ndim - 2) if s % 8 else x


def xpack(w):
    n = w.shape[0]
    h = n // 2
    t = w.reshape(n, 3, 2, 8, 128)
    v0, v1 = t[:, :, 0].reshape(n * 3, 8, 128), t[:, :, 1].reshape(n * 3, 8, 128)
    low = iota((h * 3, 8, 128), 1) < 4
    up = jnp.where(low, sroll(v1[: h * 3], 4), v1[h * 3 :])
    dn = jnp.where(low, v0[: h * 3], sroll(v0[h * 3 :], 4))
    return up, dn


def xadd(w, rp, rm):
    n = w.shape[0]
    h = n // 2
    t = w.reshape(n, 3, 2, 8, 128)
    v0, v1 = t[:, :, 0].reshape(n * 3, 8, 128), t[:, :, 1].reshape(n * 3, 8, 128)
    low = iota((h * 3, 8, 128), 1) < 4
    zero = jnp.zeros_like(rp)
    a0 = jnp.concatenate([jnp.where(low, rp, zero), jnp.where(low, sroll(rp, 4), zero)], axis=0)
    a1 = jnp.concatenate([jnp.where(low, zero, sroll(rm, 4)), jnp.where(low, zero, rm)], axis=0)
    v0, v1 = v0 + a0, v1 + a1
    return v0, v1


def ylocal(v):
    b = iota(v.shape, 1) & 3
    left = iota(v.shape, 2) < 64
    d = jnp.where(b == 0, sroll(v, 5), sroll(v, 3))
    d = pltpu.roll(d, 64, 2)
    zero = jnp.zeros_like(v)
    here = ((b == 0) & (~left)) | ((b == 3) & left)
    out = ((b == 0) & left) | ((b == 3) & (~left))
    return v + jnp.where(here, d, zero), jnp.where(out, d, zero)


def xy_body(n, w_ref, rp_ref, rm_ref, wo_ref, y_ref):
    w = w_ref[...]
    v0, v1 = xadd(w, rp_ref[...], rm_ref[...])
    for part, v in enumerate((v0, v1)):
        v, e = ylocal(v)
        wo_ref[:, :, part] = v.reshape(n, 3, 8, 128)
        e = e.reshape(n, 3, 8, 128)
        y_ref[:, part] = e[:, 0] + sroll(e[:, 1], 1) + sroll(e[:, 2], 2)


def yadd(w, yl, yr):
    n = w.shape[0]
    left = iota((n * 2, 8, 128), 2) < 64
    b = iota((n * 2, 8, 128), 1) & 3
    z = jnp.where(left, yl.reshape(n * 2, 8, 128), yr.reshape(n * 2, 8, 128))
    use = ((b == 0) & left) | ((b == 3) & (~left))
    parts = []
    for q in range(3):
        add = jnp.where(use, sroll(z, -q), jnp.zeros_like(z)).reshape(n, 2, 8, 128)
        parts.append((w[:, q] + add).reshape(n, 16, 128))
    return jnp.concatenate(parts, axis=1)


def one_hot(order):
    row = jnp.broadcast_to(order, (128, 128))
    return jnp.where(row == iota((128, 128), 0), 1.0, 0.0).astype(bf16)


def split3(x):
    h = x.astype(bf16)
    r = x - h.astype(f32)
    m = r.astype(bf16)
    l = (r - m.astype(f32)).astype(bf16)
    return h, m, l


def permute_nt(x, g):
    dims = (((1,), (1,)), ((), ()))
    h, m, l = (lax.dot_general(p, g, dims, preferred_element_type=f32) for p in split3(x))
    return h + m + l


def permute_nn(x, g):
    h, m, l = (jnp.dot(p, g, preferred_element_type=f32) for p in split3(x))
    return h + m + l


def quad(shape):
    r = iota(shape, 0)
    w = 1.0
    for i in (r >> 4, (r >> 2) & 3, r & 3):
        w = w * jnp.where((i == 0) | (i == 3), 1.0 / 6.0, 5.0 / 6.0)
    return w


def fetch(srcs, dsts, sems):
    copies = [pltpu.make_async_copy(a, b, sems.at[i]) for i, (a, b) in enumerate(zip(srcs, dsts))]
    for c in copies:
        c.start()
    for c in copies:
        c.wait()


def start_body(
    s_in, c_in, o_in, ew_in, ed_in, k_in, w_ref, up_ref, dn_ref, mk_ref, g_ref, k_ref, *scratch
):
    s_ref, c_ref, o_ref, ew_ref, ed_ref, kf_ref, sems = scratch
    fetch((s_in, c_in, o_in, ew_in, ed_in, k_in), scratch[:6], sems)
    kh, kl = two(kf_ref[...])
    k_ref[...] = jnp.concatenate([kh, kh, kl], axis=1)
    g = one_hot(o_ref[...])
    g_ref[...] = g
    rows = []
    for ref in (s_ref, c_ref):
        for f in range(F):
            for q in range(4):
                rows.append(ref[f, pl.ds(q, 16, stride=4), :])
    el = jnp.concatenate(
        [jnp.broadcast_to(ew_ref[...], (8, 128)), jnp.broadcast_to(ed_ref[...], (8, 128))], axis=0
    )
    x = permute_nt(jnp.concatenate(rows + [el], axis=0), g)
    mass = quad((64, 128)) * x[640:641]
    mk_ref[...] = x[640:656]
    s = x[:320].reshape(F, 64, 128) * mass[None]
    c = x[320:640].reshape(F, 64, 128)
    v = jnp.concatenate([s, mass[None], c, jnp.zeros((1, 64, 128), f32)], axis=0)
    w = zsum(v)
    w_ref[...] = w
    up_ref[...], dn_ref[...] = xpack(w)


def stiffness(v, kmat, kappa):
    n = v.shape[0]
    x = jnp.concatenate([v[i] for i in range(n)], axis=1)
    h = x.astype(bf16)
    l = (x - h.astype(f32)).astype(bf16)
    y = jnp.dot(kmat, jnp.concatenate([h, l, h], axis=0), preferred_element_type=f32)
    return jnp.stack([y[:, i * 128 : (i + 1) * 128] * kappa for i in range(n)], axis=0)


def state_body(w_ref, yl_ref, yr_ref, mk_ref, k_ref, sa_ref, im_ref, w2_ref, up_ref, dn_ref):
    v = zfill(yadd(w_ref[...], yl_ref[...], yr_ref[...]))
    im = 1.0 / v[F]
    im_ref[...] = im
    sa = jnp.concatenate([v[:F], v[F + 1 : 2 * F + 1]], axis=0) * im[None]
    sa_ref[...] = sa
    w = zsum(stiffness(sa, k_ref[...], mk_ref[8:9]))
    w2_ref[...] = w
    up_ref[...], dn_ref[...] = xpack(w)


def prepare_body(w1_in, b1_in, w2_in, b2_in, wo_in, bo_in, p_ref, *scratch):
    fetch((w1_in, b1_in, w2_in, b2_in, wo_in, bo_in), scratch[:6], scratch[6])
    w1, b1, w2, b2, wo, bo = (r[...] for r in scratch[:6])
    z = jnp.zeros((64, 64), f32)
    pad3 = jnp.zeros((3, 64), f32)
    w1b = jnp.concatenate([w1, b1, jnp.zeros((2, 64), f32)], axis=0)
    w1p = jnp.concatenate([w1, pad3], axis=0)
    wop = jnp.concatenate([wo, pad3], axis=0)

    def columns(parts, rows):
        if rows < 256:
            parts = parts + [jnp.zeros((256 - rows, 64), f32)]
        return jnp.concatenate(parts, axis=0).T

    l2 = columns([w2.T] * 3 + [jnp.broadcast_to(b2, (8, 64))], 200)
    l2t = columns([w2] * 3, 192)
    l1 = columns([w1b] * 4, 32)
    lot = columns([wop] * 4, 32)
    both = jnp.concatenate([wop, w1p], axis=0)
    diag = iota((16, 5), 0) == iota((16, 5), 1)
    bias = jnp.sum(jnp.where(diag, jnp.broadcast_to(bo, (16, 5)), 0.0), axis=1, keepdims=True)
    bias = jnp.where(iota((16, 64), 1) < 2, jnp.broadcast_to(bias, (16, 64)), z[:16])
    small = jnp.concatenate([both, both, both, bias], axis=1)

    def parts(p, high):
        h = p.astype(bf16).astype(f32)
        return jnp.where(high, h, p - h).astype(bf16)

    col = iota((128, 256), 1)
    high = (col < 128) | (col == 192)
    p_ref[0:128] = parts(jnp.concatenate([l2, l2t], axis=0), high)
    p_ref[128:256] = parts(jnp.concatenate([l1, lot], axis=0), col < 16)
    p_ref[256:272] = parts(small, high[:16])


def weights(p_ref):
    return dict(
        l2=p_ref[0:64, 0:208],
        l2t=p_ref[64:128, 0:192],
        l1=p_ref[128:192, 0:32],
        lot=p_ref[192:256, 0:32],
        lo=p_ref[256:272, 0:208],
    )


def two(x):
    h = x.astype(bf16)
    return h, (x - h.astype(f32)).astype(bf16)


def stack8(x):
    h = x.astype(bf16).astype(f32)
    l = x - h
    return jnp.concatenate([h, l, h, l], axis=0).astype(bf16)


def mm(a, b):
    return jnp.dot(a, b, preferred_element_type=f32)


def nt(a, b):
    return lax.dot_general(a, b, (((1,), (1,)), ((), ())), preferred_element_type=f32)


def load8(ref, n0):
    return jnp.concatenate([ref[pl.ds(n0 + i, 8, stride=64), :] for i in range(CH)], axis=1)


def store8(ref, n0, x):
    for i in range(CH):
        ref[pl.ds(n0 + i, 8, stride=64), :] = x[:, i * 128 : (i + 1) * 128]


def put_fields(ref, x, ones):
    ref[0 : F * 64, :] = x.reshape(F * 64, 128)
    ref[F * 64 : F * 64 + 64, :] = jnp.full((64, 128), 1.0 if ones else 0.0, f32)
    ref[F * 64 + 64 :, :] = jnp.zeros((128, 128), f32)


def bias_rows():
    return jnp.where(iota((16, NW), 0) < 2, 1.0, 0.0).astype(bf16)


def forward(x8, w, ones):
    h1 = jnp.tanh(mm(w["l1"], stack8(x8)))
    h1h, h1l = two(h1)
    h2 = jnp.tanh(mm(w["l2"], jnp.concatenate([h1h, h1l, h1h, ones], axis=0)))
    h2h, h2l = two(h2)
    return h1, h1h, h1l, h2, h2h, h2l


def lanes_of(i):
    return pl.ds(pl.multiple_of(i * NW, NW), NW)


def put4(ref, i, parts):
    for k, p in enumerate(parts):
        ref[k * 64 : k * 64 + 64, lanes_of(i)] = p


def closure_body(sa_ref, p_ref, c_ref, x_ref, hh_ref, t_ref, o_ref):
    put_fields(x_ref, sa_ref[0:F], True)
    w = weights(p_ref)
    ones = bias_rows()

    def chunk(i, carry):
        n0 = i * CH
        h1, h1h, h1l, h2, h2h, h2l = forward(load8(x_ref, n0), w, ones)
        put4(hh_ref, i, (h1h, h1l, h2h, h2l))
        t_ref[0:64, lanes_of(i)] = 1.0 - h1 * h1
        t_ref[64:128, lanes_of(i)] = 1.0 - h2 * h2
        out = mm(w["lo"], jnp.concatenate([h2h, h2l, h2h, ones], axis=0))
        store8(o_ref, n0, out[0:8])
        return carry

    lax.fori_loop(0, 64 // CH, chunk, 0)
    c_ref[...] = o_ref[0 : F * 64].reshape(F, 64, 128)


def backward(c8, t1, t2, w):
    d2h, d2l = two(mm(w["lot"], stack8(c8)) * t2)
    d1h, d1l = two(mm(w["l2t"], jnp.concatenate([d2h, d2l, d2h], axis=0)) * t1)
    back = mm(w["lo"][:, 0:192], jnp.concatenate([d1h, d1l, d1h], axis=0))[8:16]
    return back, d2h, d2l, d1h, d1l


def stack2(x):
    h = x.astype(bf16).astype(f32)
    return jnp.concatenate([h, x - h], axis=0).astype(bf16)


def add_grads(acc, x8, c8, h1, h2, d2, d1):
    gw, gb = acc
    right = jnp.concatenate([h1, stack2(x8), stack2(c8)], axis=0)
    gw = gw + nt(jnp.concatenate([d2, d1, h2], axis=0), right)
    for i in range(CH):
        gb = gb + c8[:, i * 128 : (i + 1) * 128]
    return gw, gb


def no_grads():
    return jnp.zeros((384, 160), f32), jnp.zeros((8, 128), f32)


def second_body(
    w_ref, yl_ref, yr_ref, mk_ref, im_ref, sa_ref, c0_ref, p_ref, k_ref,
    part_ref, m1_ref, w2_ref, up_ref, dn_ref, x_ref, c_ref, hh_ref, dd_ref,
    o_ref, b_ref,
):
    im = im_ref[...] * STEP
    mass = quad((64, 128)) * mk_ref[0:1]
    v = zfill(yadd(w_ref[...], yl_ref[...], yr_ref[...])) * im[None]
    a2 = sa_ref[F:]
    s1 = sa_ref[0:F] + STEP * c0_ref[...] - v[0:F]
    put_fields(x_ref, s1, True)
    put_fields(c_ref, a2 * mass[None], False)
    w = weights(p_ref)
    ones = bias_rows()

    def chunk(i, carry):
        n0 = i * CH
        h1, h1h, h1l, h2, h2h, h2l = forward(load8(x_ref, n0), w, ones)
        put4(hh_ref, i, (h1h, h1l, h2h, h2l))
        out = mm(w["lo"], jnp.concatenate([h2h, h2l, h2h, ones], axis=0))
        store8(o_ref, n0, out[0:8])
        back, *ds = backward(load8(c_ref, n0), 1.0 - h1 * h1, 1.0 - h2 * h2, w)
        put4(dd_ref, i, ds)
        store8(b_ref, n0, back)
        return carry

    lax.fori_loop(0, 64 // CH, chunk, 0)
    back = b_ref[0 : F * 64].reshape(F, 64, 128)
    a1 = a2 - v[F:] + (STEP / mass)[None] * back
    m1_ref[...] = a1 * mass[None]
    part_ref[0:F] = s1 + STEP * o_ref[0 : F * 64].reshape(F, 64, 128)
    part_ref[F:] = a1
    wz = zsum(stiffness(jnp.concatenate([s1, a1], axis=0), k_ref[...], mk_ref[8:9]))
    w2_ref[...] = wz
    up_ref[...], dn_ref[...] = xpack(wz)


def grads_body(x_ref, c_ref, hh_ref, dd_ref, gw_ref, gb_ref):
    def chunk(i, acc):
        n0 = i * CH
        at = lanes_of(i)
        return add_grads(
            acc, load8(x_ref, n0), load8(c_ref, n0),
            hh_ref[0:128, at], hh_ref[128:256, at], dd_ref[0:128, at], dd_ref[128:256, at],
        )

    gw_ref[...], gb_ref[...] = lax.fori_loop(0, 64 // CH, chunk, no_grads())


def first_body(
    x_ref, m1_ref, hh_ref, t_ref, p_ref, gw_ref, gb_ref, back_ref, pay_ref, c_ref, b_ref
):
    put_fields(c_ref, m1_ref[...], False)
    w = weights(p_ref)

    def chunk(i, acc):
        n0 = i * CH
        at = lanes_of(i)
        c8 = load8(c_ref, n0)
        back, d2h, d2l, d1h, d1l = backward(c8, t_ref[0:64, at], t_ref[64:128, at], w)
        store8(b_ref, n0, back)
        return add_grads(
            acc, load8(x_ref, n0), c8, hh_ref[0:128, at], hh_ref[128:256, at],
            jnp.concatenate([d2h, d2l], axis=0), jnp.concatenate([d1h, d1l], axis=0),
        )

    g, gb = lax.fori_loop(0, 64 // CH, chunk, (gw_ref[...], gb_ref[...]))
    back_ref[...] = b_ref[0 : F * 64].reshape(F, 64, 128)

    def fold(t):
        return t + pltpu.roll(t, 64, 1)

    gw = fold(g[0:64, 0:128] + g[64:128, 0:128])
    gs = g[:, 128:160].T
    gx2 = fold(gs[0:8, 0:128] + gs[8:16, 0:128])
    gx1 = fold(gs[0:8, 128:256] + gs[8:16, 128:256])
    gc = fold(gs[16:24, 256:384] + gs[24:32, 256:384])
    gbs = jnp.broadcast_to(jnp.sum(gb, axis=1, keepdims=True), (8, 128))
    left = iota((32, 128), 1) < 64
    scale = STEP / 256.0
    pay_ref[0:32] = jnp.where(left, gw[0:32], gw[32:64]) * scale
    pay_ref[32:40] = jnp.where(left[:8], gx1, gx2) * scale
    pay_ref[40:48] = jnp.where(left[:8], gc, gbs) * scale


def finish_body(
    w_ref, yl_ref, yr_ref, mk_ref, im_ref, part_ref, back_ref, g_ref, s_ref, a_ref
):
    im = im_ref[...] * STEP
    mass = quad((64, 128)) * mk_ref[0:1]
    v = zfill(yadd(w_ref[...], yl_ref[...], yr_ref[...])) * im[None]
    s2 = part_ref[0:F] - v[0:F]
    a0 = (part_ref[F:] - v[F:]) * mass[None] + STEP * back_ref[...]
    x = jnp.concatenate([s2.reshape(320, 128), a0.reshape(320, 128)], axis=0)
    y = permute_nn(x, g_ref[...])
    for i, ref in enumerate((s_ref, a_ref)):
        for f in range(F):
            for q in range(4):
                r = (i * F + f) * 64 + q * 16
                ref[f, pl.ds(q, 16, stride=4), :] = y[r : r + 16]


def output_body(p_ref, gw1_ref, gb1_ref, gw2_ref, gb2_ref, gwo_ref, gbo_ref):
    pay = p_ref[0]
    for i in range(1, 8):
        pay = pay + p_ref[i]
    gw2_ref[0:32] = pay[0:32, 0:64]
    other = pltpu.roll(pay, 64, 1)
    gw2_ref[32:64] = other[0:32, 0:64]
    gw1_ref[...] = pay[32:37, 0:64]
    gb1_ref[...] = pay[37:38, 0:64]
    gb2_ref[...] = other[37:38, 0:64]
    gwo_ref[...] = pay[40:45, 0:64]
    diag = iota((8, 5), 0) == iota((8, 5), 1)
    gbo_ref[...] = jnp.sum(jnp.where(diag, other[40:48, 0:5], 0.0), axis=0, keepdims=True)


def call(body, outs, args, scratch=(), flops=0, trans=0, space=pltpu.VMEM):
    if space == pltpu.HBM:
        args = [pltpu.with_memory_space_constraint(x, pltpu.HBM) for x in args]
    shapes = [s if hasattr(s, "dtype") else jax.ShapeDtypeStruct(s, f32) for s in outs]
    scratch = [s if hasattr(s, "memory_space") or hasattr(s, "dtype") else pltpu.VMEM(s, f32) for s in scratch]
    return pl.pallas_call(
        body,
        out_shape=shapes,
        in_specs=[pl.BlockSpec(memory_space=space)] * len(args),
        out_specs=[VM] * len(shapes),
        scratch_shapes=scratch,
        cost_estimate=pl.CostEstimate(
            flops=flops, bytes_accessed=2000000, transcendentals=trans
        ),
        compiler_params=pltpu.CompilerParams(vmem_limit_bytes=40 * 1024 * 1024),
    )(*args)


def shift(x, axis, step):
    n = lax.axis_size(axis)
    return lax.ppermute(x, axis, [(i, (i + step) % n) for i in range(n)])


def both_ways(up, dn, axis):
    return shift(up, axis, 1), shift(dn, axis, -1)


def place(d):
    s, c = d // 16, d % 16
    return s // 8, (s // 2) % 4, s % 2, c // 4, c % 4


def together(fixed):
    groups = {}
    for d in range(256):
        groups.setdefault(tuple(place(d)[i] for i in fixed), []).append(d)
    return [groups[k] for k in sorted(groups)]


def send_to_all(x, groups):
    n = len(groups[0])
    y = jnp.broadcast_to(x[None], (n,) + x.shape)
    return lax.all_to_all(y, ("sub", "col"), 0, 0, axis_index_groups=groups, tiled=True)


def all_sum(x):
    if (lax.axis_size("sub"), lax.axis_size("col")) != (16, 16):
        x = lax.psum(x, ("sub", "col"))
        return jnp.concatenate([x[None], jnp.zeros((7,) + x.shape, f32)], axis=0)
    x = x + lax.ppermute(x, ("sub", "col"), [(d, d ^ 16) for d in range(256)])
    x = send_to_all(x, together((0, 2, 3))).sum(0)
    return send_to_all(x, together((1, 2, 4)))


def on_device(
    initial_state,
    state_cotangent,
    element_order,
    element_weight,
    element_diffusivity,
    in_weight,
    in_bias,
    mid_weight,
    mid_bias,
    out_weight,
    out_bias,
):
    hot = jax.ShapeDtypeStruct((128, 128), bf16)
    wide = jax.ShapeDtypeStruct((256, 8192), bf16)
    khot = jax.ShapeDtypeStruct((64, 192), bf16)

    def in_device(w, up, dn, n):
        rp, rm = both_ways(up, dn, "sub")
        return call(
            lambda *r: xy_body(n, *r), [(n, 3, 2, 8, 128), (n, 2, 8, 128)], [w, rp, rm]
        )

    def faces(w, up, dn, n):
        w, y = in_device(w, up, dn, n)
        yl, yr = both_ways(y, y, "col")
        return w, yl, yr

    w, up, dn, mk, g, kmat = call(
        start_body,
        [(12, 48, 128), (18, 8, 128), (18, 8, 128), (16, 128), hot, khot],
        [
            initial_state,
            state_cotangent,
            element_order,
            element_weight.reshape(1, 128),
            element_diffusivity.reshape(1, 128),
            jnp.asarray(stiffness_matrix()),
        ],
        [(F, 64, 128), (F, 64, 128), pltpu.VMEM((1, 128), jnp.int32), (1, 128), (1, 128)]
        + [(64, 64)]
        + [pltpu.SemaphoreType.DMA((6,))],
        space=pltpu.HBM,
    )
    (pw,) = call(
        prepare_body,
        [jax.ShapeDtypeStruct((272, 256), bf16)],
        [
            in_weight.T,
            in_bias.reshape(1, 64),
            mid_weight,
            mid_bias.reshape(1, 64),
            out_weight,
            out_bias.reshape(1, 5),
        ],
        [(5, 64), (1, 64), (64, 64), (1, 64), (5, 64), (1, 5), pltpu.SemaphoreType.DMA((6,))],
        flops=2000000,
        space=pltpu.HBM,
    )
    w, yl, yr = faces(w, up, dn, 12)
    pw, yl, yr = lax.optimization_barrier((pw, yl, yr))
    ten = [(10, 48, 128), (15, 8, 128), (15, 8, 128)]
    sa, im, w, up, dn = call(
        state_body, [(10, 64, 128), (64, 128)] + ten, [w, yl, yr, mk, kmat]
    )
    c0, x0, hh0, t0 = call(
        closure_body,
        [(F, 64, 128), (512, 128), wide, (128, 8192)],
        [sa, pw],
        [(512, 128)],
        flops=300000000,
        trans=1000000,
    )
    w, yl, yr = faces(w, up, dn, 10)
    part, m1, w, up, dn, x1, c1, hh1, dd1 = call(
        second_body,
        [(10, 64, 128), (F, 64, 128)] + ten + [(512, 128), (512, 128), wide, wide],
        [w, yl, yr, mk, im, sa, c0, pw, kmat],
        [(512, 128)] * 2,
        flops=900000000,
        trans=1000000,
    )
    acc = call(
        grads_body,
        [(384, 160), (8, 128)],
        [x1, c1, hh1, dd1],
        flops=300000000,
    )
    w, y = in_device(w, up, dn, 10)
    acc, y = lax.optimization_barrier((acc, y))
    yl, yr = both_ways(y, y, "col")
    back, pay = call(
        first_body,
        [(F, 64, 128), (48, 128)],
        [x0, m1, hh0, t0, pw, *acc],
        [(512, 128)] * 2,
        flops=600000000,
    )
    pay, yl, yr = lax.optimization_barrier((pay, yl, yr))
    terms = all_sum(pay)
    out_state, out_adj = call(
        finish_body,
        [(F, 64, 128), (F, 64, 128)],
        [w, yl, yr, mk, im, part, back, g],
        flops=20000000,
    )
    gw1, gb1, gw2, gb2, gwo, gbo = call(
        output_body, [(5, 64), (1, 64), (64, 64), (1, 64), (5, 64), (1, 5)], [terms]
    )
    return (
        out_state,
        out_adj,
        gw1.T,
        gb1.reshape(64),
        gw2,
        gb2.reshape(64),
        gwo,
        gbo.reshape(5),
    )


def solution(mesh):
    split = P(None, None, ("sub", "col"))
    placed = (split, split, P(("sub", "col"), None), P(("sub", "col")), P(("sub", "col")))
    return jax.shard_map(
        on_device,
        mesh=mesh,
        in_specs=placed + (P(),) * 6,
        out_specs=(split, split) + (P(),) * 6,
        check_vma=False,
    )
```

```python
import math

import jax
import jax.numpy as jnp
import numpy as np
from jax import lax
from jax.experimental import pallas as pl
from jax.experimental.pallas import tpu as pltpu
from jax.sharding import PartitionSpec as P

F = 5
STEP = 0.05
CH = 32
NW = CH * 128
f32, bf16 = jnp.float32, jnp.bfloat16
VM = pl.BlockSpec(memory_space=pltpu.VMEM)


def stiffness_matrix():
    at = [-1.0, -math.sqrt(0.2), math.sqrt(0.2), 1.0]
    w = np.array([1.0 / 6.0, 5.0 / 6.0, 5.0 / 6.0, 1.0 / 6.0])
    prods = [np.prod([at[r] - at[p] for p in range(4) if p != r]) for r in range(4)]
    d = np.zeros((4, 4))
    for r in range(4):
        for c in range(4):
            if r == c:
                d[r, c] = sum(1.0 / (at[r] - at[p]) for p in range(4) if p != r)
            else:
                d[r, c] = prods[r] / (prods[c] * (at[r] - at[c]))
    s = d.T @ np.diag(w) @ d
    m = np.diag(w)
    k = np.kron(m, np.kron(s, m)) + np.kron(m, np.kron(m, s)) + np.kron(s, np.kron(m, m))
    return k.astype(np.float32)


def iota(shape, dim):
    return lax.broadcasted_iota(jnp.int32, shape, dim)


def next_k(x):
    ax = x.ndim - 1
    lane = iota(x.shape, ax) & 63
    return jnp.where(lane == 63, pltpu.roll(x, 63, ax), pltpu.roll(x, 127, ax))


def prev_k(x):
    ax = x.ndim - 1
    lane = iota(x.shape, ax) & 63
    return jnp.where(lane == 0, pltpu.roll(x, 65, ax), pltpu.roll(x, 1, ax))


def zsum(v):
    n = v.shape[0]
    top = v[:, 48:64] + next_k(v[:, 0:16])
    return jnp.concatenate([v[:, 16:48], top], axis=1)


def zfill(w):
    return jnp.concatenate([prev_k(w[:, 32:48]), w], axis=1)


def sroll(x, s):
    return pltpu.roll(x, s % 8, x.ndim - 2) if s % 8 else x


def xpack(w):
    n = w.shape[0]
    h = n // 2
    t = w.reshape(n, 3, 2, 8, 128)
    v0, v1 = t[:, :, 0].reshape(n * 3, 8, 128), t[:, :, 1].reshape(n * 3, 8, 128)
    low = iota((h * 3, 8, 128), 1) < 4
    up = jnp.where(low, sroll(v1[: h * 3], 4), v1[h * 3 :])
    dn = jnp.where(low, v0[: h * 3], sroll(v0[h * 3 :], 4))
    return up, dn


def xadd(w, rp, rm):
    n = w.shape[0]
    h = n // 2
    t = w.reshape(n, 3, 2, 8, 128)
    v0, v1 = t[:, :, 0].reshape(n * 3, 8, 128), t[:, :, 1].reshape(n * 3, 8, 128)
    low = iota((h * 3, 8, 128), 1) < 4
    zero = jnp.zeros_like(rp)
    a0 = jnp.concatenate([jnp.where(low, rp, zero), jnp.where(low, sroll(rp, 4), zero)], axis=0)
    a1 = jnp.concatenate([jnp.where(low, zero, sroll(rm, 4)), jnp.where(low, zero, rm)], axis=0)
    v0, v1 = v0 + a0, v1 + a1
    return v0, v1


def ylocal(v):
    b = iota(v.shape, 1) & 3
    left = iota(v.shape, 2) < 64
    d = jnp.where(b == 0, sroll(v, 5), sroll(v, 3))
    d = pltpu.roll(d, 64, 2)
    zero = jnp.zeros_like(v)
    here = ((b == 0) & (~left)) | ((b == 3) & left)
    out = ((b == 0) & left) | ((b == 3) & (~left))
    return v + jnp.where(here, d, zero), jnp.where(out, d, zero)


def xy_body(n, w_ref, rp_ref, rm_ref, wo_ref, yu_ref, yd_ref):
    ys = []
    w = w_ref[...]
    v0, v1 = xadd(w, rp_ref[...], rm_ref[...])
    for part, v in enumerate((v0, v1)):
        v, e = ylocal(v)
        wo_ref[:, :, part] = v.reshape(n, 3, 8, 128)
        e = e.reshape(n, 3, 8, 128)
        ys.append(e[:, 0] + sroll(e[:, 1], 1) + sroll(e[:, 2], 2))
    left = iota((n, 8, 128), 2) < 64
    m = yu_ref.shape[0]
    yu_ref[...] = jnp.where(left, ys[0], pltpu.roll(ys[1], 64, 2))[:m]
    yd_ref[...] = jnp.where(left, pltpu.roll(ys[0], 64, 2), ys[1])[:m]


def yadd(w, yl, yr):
    m = yl.shape[0]
    left = iota((m, 8, 128), 2) < 64
    b = iota((m, 8, 128), 1) & 3
    use = ((b == 0) & left) | ((b == 3) & (~left))
    zs = (
        jnp.where(left, yl, pltpu.roll(yr, 64, 2)),
        jnp.where(left, pltpu.roll(yl, 64, 2), yr),
    )
    rows = []
    for q in range(3):
        for part, z in enumerate(zs):
            rows.append(w[:m, q, part] + jnp.where(use, sroll(z, -q), jnp.zeros_like(z)))
    return jnp.concatenate(rows, axis=1)


def one_hot(order):
    row = jnp.broadcast_to(order, (128, 128))
    return jnp.where(row == iota((128, 128), 0), 1.0, 0.0).astype(bf16)


def split3(x):
    h = x.astype(bf16)
    r = x - h.astype(f32)
    m = r.astype(bf16)
    l = (r - m.astype(f32)).astype(bf16)
    return h, m, l


def permute_nt(x, g):
    dims = (((1,), (1,)), ((), ()))
    h, m, l = (lax.dot_general(p, g, dims, preferred_element_type=f32) for p in split3(x))
    return h + m + l


def permute_nn(x, g):
    h, m, l = (jnp.dot(p, g, preferred_element_type=f32) for p in split3(x))
    return h + m + l


def quad(shape):
    r = iota(shape, 0)
    w = 1.0
    for i in (r >> 4, (r >> 2) & 3, r & 3):
        w = w * jnp.where((i == 0) | (i == 3), 1.0 / 6.0, 5.0 / 6.0)
    return w


def fetch(srcs, dsts, sems):
    copies = [pltpu.make_async_copy(a, b, sems.at[i]) for i, (a, b) in enumerate(zip(srcs, dsts))]
    for c in copies:
        c.start()
    for c in copies:
        c.wait()


def start_body(
    s_in, c_in, o_in, ew_in, ed_in, k_in, w_ref, up_ref, dn_ref, mk_ref, g_ref, k_ref, *scratch
):
    s_ref, c_ref, o_ref, ew_ref, ed_ref, kf_ref, sems = scratch
    fetch((s_in, c_in, o_in, ew_in, ed_in, k_in), scratch[:6], sems)
    kh, kl = two(kf_ref[...])
    k_ref[...] = jnp.concatenate([kh, kh, kl], axis=1)
    g = one_hot(o_ref[...])
    g_ref[...] = g
    rows = []
    for ref in (s_ref, c_ref):
        for f in range(F):
            for q in range(4):
                rows.append(ref[f, pl.ds(q, 16, stride=4), :])
    el = jnp.concatenate(
        [jnp.broadcast_to(ew_ref[...], (8, 128)), jnp.broadcast_to(ed_ref[...], (8, 128))], axis=0
    )
    x = permute_nt(jnp.concatenate(rows + [el], axis=0), g)
    mass = quad((64, 128)) * x[640:641]
    mk_ref[...] = x[640:656]
    s = x[:320].reshape(F, 64, 128) * mass[None]
    c = x[320:640].reshape(F, 64, 128)
    v = jnp.concatenate([s, mass[None], c, jnp.zeros((1, 64, 128), f32)], axis=0)
    w = zsum(v)
    w_ref[...] = w
    up_ref[...], dn_ref[...] = xpack(w)


def stiffness(v, kmat, kappa):
    n = v.shape[0]
    x = jnp.concatenate([v[i] for i in range(n)], axis=1)
    h = x.astype(bf16)
    l = (x - h.astype(f32)).astype(bf16)
    y = jnp.dot(kmat, jnp.concatenate([h, l, h], axis=0), preferred_element_type=f32)
    return jnp.stack([y[:, i * 128 : (i + 1) * 128] * kappa for i in range(n)], axis=0)


def state_body(w_ref, yl_ref, yr_ref, mk_ref, k_ref, sa_ref, im_ref, w2_ref, up_ref, dn_ref):
    v = zfill(yadd(w_ref[...], yl_ref[...], yr_ref[...]))
    im = 1.0 / v[F]
    im_ref[...] = im
    sa = jnp.concatenate([v[:F], v[F + 1 : 2 * F + 1]], axis=0) * im[None]
    sa_ref[...] = sa
    w = zsum(stiffness(sa, k_ref[...], mk_ref[8:9]))
    w2_ref[...] = w
    up_ref[...], dn_ref[...] = xpack(w)


def prepare_body(w1_in, b1_in, w2_in, b2_in, wo_in, bo_in, p_ref, *scratch):
    fetch((w1_in, b1_in, w2_in, b2_in, wo_in, bo_in), scratch[:6], scratch[6])
    w1, b1, w2, b2, wo, bo = (r[...] for r in scratch[:6])
    z = jnp.zeros((64, 64), f32)
    pad3 = jnp.zeros((3, 64), f32)
    w1b = jnp.concatenate([w1, b1, jnp.zeros((2, 64), f32)], axis=0)
    w1p = jnp.concatenate([w1, pad3], axis=0)
    wop = jnp.concatenate([wo, pad3], axis=0)

    def columns(parts, rows):
        if rows < 256:
            parts = parts + [jnp.zeros((256 - rows, 64), f32)]
        return jnp.concatenate(parts, axis=0).T

    l2 = columns([w2.T] * 3 + [jnp.broadcast_to(b2, (8, 64))], 200)
    l2t = columns([w2] * 3, 192)
    l1 = columns([w1b] * 4, 32)
    lot = columns([wop] * 4, 32)
    both = jnp.concatenate([wop, w1p], axis=0)
    diag = iota((16, 5), 0) == iota((16, 5), 1)
    bias = jnp.sum(jnp.where(diag, jnp.broadcast_to(bo, (16, 5)), 0.0), axis=1, keepdims=True)
    bias = jnp.where(iota((16, 64), 1) < 2, jnp.broadcast_to(bias, (16, 64)), z[:16])
    small = jnp.concatenate([both, both, both, bias], axis=1)

    def parts(p, high):
        h = p.astype(bf16).astype(f32)
        return jnp.where(high, h, p - h).astype(bf16)

    col = iota((128, 256), 1)
    high = (col < 128) | (col == 192)
    p_ref[0:128] = parts(jnp.concatenate([l2, l2t], axis=0), high)
    p_ref[128:256] = parts(jnp.concatenate([l1, lot], axis=0), col < 16)
    p_ref[256:272] = parts(small, high[:16])


def weights(p_ref):
    return dict(
        l2=p_ref[0:64, 0:208],
        l2t=p_ref[64:128, 0:192],
        l1=p_ref[128:192, 0:32],
        lot=p_ref[192:256, 0:32],
        lo=p_ref[256:272, 0:208],
    )


def two(x):
    h = x.astype(bf16)
    return h, (x - h.astype(f32)).astype(bf16)


def stack8(x):
    h = x.astype(bf16).astype(f32)
    l = x - h
    return jnp.concatenate([h, l, h, l], axis=0).astype(bf16)


def mm(a, b):
    return jnp.dot(a, b, preferred_element_type=f32)


def nt(a, b):
    return lax.dot_general(a, b, (((1,), (1,)), ((), ())), preferred_element_type=f32)


def load8(ref, n0):
    return jnp.concatenate([ref[pl.ds(n0 + i, 8, stride=64), :] for i in range(CH)], axis=1)


def store8(ref, n0, x):
    for i in range(CH):
        ref[pl.ds(n0 + i, 8, stride=64), :] = x[:, i * 128 : (i + 1) * 128]


def put_fields(ref, x, ones):
    ref[0 : F * 64, :] = x.reshape(F * 64, 128)
    ref[F * 64 : F * 64 + 64, :] = jnp.full((64, 128), 1.0 if ones else 0.0, f32)
    ref[F * 64 + 64 :, :] = jnp.zeros((128, 128), f32)


def bias_rows():
    return jnp.where(iota((16, NW), 0) < 2, 1.0, 0.0).astype(bf16)


def forward(x8, w, ones):
    h1 = jnp.tanh(mm(w["l1"], stack8(x8)))
    h1h, h1l = two(h1)
    h2 = jnp.tanh(mm(w["l2"], jnp.concatenate([h1h, h1l, h1h, ones], axis=0)))
    h2h, h2l = two(h2)
    return h1, h1h, h1l, h2, h2h, h2l


def lanes_of(i):
    return pl.ds(pl.multiple_of(i * NW, NW), NW)


def put4(ref, i, parts):
    for k, p in enumerate(parts):
        ref[k * 64 : k * 64 + 64, lanes_of(i)] = p


def closure_body(sa_ref, p_ref, c_ref, x_ref, hh_ref, t_ref, o_ref):
    put_fields(x_ref, sa_ref[0:F], True)
    w = weights(p_ref)
    ones = bias_rows()

    def chunk(i, carry):
        n0 = i * CH
        h1, h1h, h1l, h2, h2h, h2l = forward(load8(x_ref, n0), w, ones)
        put4(hh_ref, i, (h1h, h1l, h2h, h2l))
        t_ref[0:64, lanes_of(i)] = 1.0 - h1 * h1
        t_ref[64:128, lanes_of(i)] = 1.0 - h2 * h2
        out = mm(w["lo"], jnp.concatenate([h2h, h2l, h2h, ones], axis=0))
        store8(o_ref, n0, out[0:8])
        return carry

    lax.fori_loop(0, 64 // CH, chunk, 0)
    c_ref[...] = o_ref[0 : F * 64].reshape(F, 64, 128)


def backward(c8, t1, t2, w):
    d2h, d2l = two(mm(w["lot"], stack8(c8)) * t2)
    d1h, d1l = two(mm(w["l2t"], jnp.concatenate([d2h, d2l, d2h], axis=0)) * t1)
    back = mm(w["lo"][:, 0:192], jnp.concatenate([d1h, d1l, d1h], axis=0))[8:16]
    return back, d2h, d2l, d1h, d1l


def stack2(x):
    h = x.astype(bf16).astype(f32)
    return jnp.concatenate([h, x - h], axis=0).astype(bf16)


def add_grads(acc, x8, c8, h1, h2, d2, d1):
    gw, gb = acc
    right = jnp.concatenate([h1, stack2(x8), stack2(c8)], axis=0)
    gw = gw + nt(jnp.concatenate([d2, d1, h2], axis=0), right)
    for i in range(CH):
        gb = gb + c8[:, i * 128 : (i + 1) * 128]
    return gw, gb


def no_grads():
    return jnp.zeros((384, 160), f32), jnp.zeros((8, 128), f32)


def second_body(
    w_ref, yl_ref, yr_ref, mk_ref, im_ref, sa_ref, c0_ref, p_ref, k_ref,
    part_ref, m1_ref, w2_ref, up_ref, dn_ref, x_ref, c_ref, hh_ref, dd_ref,
    o_ref, b_ref,
):
    im = im_ref[...] * STEP
    mass = quad((64, 128)) * mk_ref[0:1]
    v = zfill(yadd(w_ref[...], yl_ref[...], yr_ref[...])) * im[None]
    a2 = sa_ref[F:]
    s1 = sa_ref[0:F] + STEP * c0_ref[...] - v[0:F]
    put_fields(x_ref, s1, True)
    put_fields(c_ref, a2 * mass[None], False)
    w = weights(p_ref)
    ones = bias_rows()

    def chunk(i, carry):
        n0 = i * CH
        h1, h1h, h1l, h2, h2h, h2l = forward(load8(x_ref, n0), w, ones)
        put4(hh_ref, i, (h1h, h1l, h2h, h2l))
        out = mm(w["lo"], jnp.concatenate([h2h, h2l, h2h, ones], axis=0))
        store8(o_ref, n0, out[0:8])
        back, *ds = backward(load8(c_ref, n0), 1.0 - h1 * h1, 1.0 - h2 * h2, w)
        put4(dd_ref, i, ds)
        store8(b_ref, n0, back)
        return carry

    lax.fori_loop(0, 64 // CH, chunk, 0)
    back = b_ref[0 : F * 64].reshape(F, 64, 128)
    a1 = a2 - v[F:] + (STEP / mass)[None] * back
    m1_ref[...] = a1 * mass[None]
    part_ref[0:F] = s1 + STEP * o_ref[0 : F * 64].reshape(F, 64, 128)
    part_ref[F:] = a1
    wz = zsum(stiffness(jnp.concatenate([s1, a1], axis=0), k_ref[...], mk_ref[8:9]))
    w2_ref[...] = wz
    up_ref[...], dn_ref[...] = xpack(wz)


def first_body(x_ref, m1_ref, hh_ref, t_ref, p_ref, back_ref, gw_ref, gb_ref, c_ref, b_ref):
    put_fields(c_ref, m1_ref[...], False)
    w = weights(p_ref)

    def chunk(i, acc):
        n0 = i * CH
        at = lanes_of(i)
        c8 = load8(c_ref, n0)
        back, d2h, d2l, d1h, d1l = backward(c8, t_ref[0:64, at], t_ref[64:128, at], w)
        store8(b_ref, n0, back)
        return add_grads(
            acc, load8(x_ref, n0), c8, hh_ref[0:128, at], hh_ref[128:256, at],
            jnp.concatenate([d2h, d2l], axis=0), jnp.concatenate([d1h, d1l], axis=0),
        )

    gw_ref[...], gb_ref[...] = lax.fori_loop(0, 64 // CH, chunk, no_grads())
    back_ref[...] = b_ref[0 : F * 64].reshape(F, 64, 128)


def grads_body(x_ref, c_ref, hh_ref, dd_ref, gw_ref, gb_ref, pay_ref):
    def chunk(i, acc):
        n0 = i * CH
        at = lanes_of(i)
        return add_grads(
            acc, load8(x_ref, n0), load8(c_ref, n0),
            hh_ref[0:128, at], hh_ref[128:256, at], dd_ref[0:128, at], dd_ref[128:256, at],
        )

    g, gb = lax.fori_loop(0, 64 // CH, chunk, (gw_ref[...], gb_ref[...]))

    def fold(t):
        return t + pltpu.roll(t, 64, 1)

    gw = fold(g[0:64, 0:128] + g[64:128, 0:128])
    gs = g[:, 128:160].T
    gx2 = fold(gs[0:8, 0:128] + gs[8:16, 0:128])
    gx1 = fold(gs[0:8, 128:256] + gs[8:16, 128:256])
    gc = fold(gs[16:24, 256:384] + gs[24:32, 256:384])
    gbs = jnp.broadcast_to(jnp.sum(gb, axis=1, keepdims=True), (8, 128))
    left = iota((32, 128), 1) < 64
    scale = STEP / 256.0
    pay_ref[0:32] = jnp.where(left, gw[0:32], gw[32:64]) * scale
    pay_ref[32:40] = jnp.where(left[:8], gx1, gx2) * scale
    pay_ref[40:48] = jnp.where(left[:8], gc, gbs) * scale


def finish_body(
    w_ref, yl_ref, yr_ref, mk_ref, im_ref, part_ref, back_ref, g_ref, s_ref, a_ref
):
    im = im_ref[...] * STEP
    mass = quad((64, 128)) * mk_ref[0:1]
    v = zfill(yadd(w_ref[...], yl_ref[...], yr_ref[...])) * im[None]
    s2 = part_ref[0:F] - v[0:F]
    a0 = (part_ref[F:] - v[F:]) * mass[None] + STEP * back_ref[...]
    x = jnp.concatenate([s2.reshape(320, 128), a0.reshape(320, 128)], axis=0)
    y = permute_nn(x, g_ref[...])
    for i, ref in enumerate((s_ref, a_ref)):
        for f in range(F):
            for q in range(4):
                r = (i * F + f) * 64 + q * 16
                ref[f, pl.ds(q, 16, stride=4), :] = y[r : r + 16]


def output_body(l_ref, h_ref, gw1_ref, gb1_ref, gw2_ref, gb2_ref, gwo_ref, gbo_ref):
    pay = jnp.concatenate([l_ref[...], h_ref[...]], axis=0)
    gw2_ref[0:32] = pay[0:32, 0:64]
    other = pltpu.roll(pay, 64, 1)
    gw2_ref[32:64] = other[0:32, 0:64]
    gw1_ref[...] = pay[32:37, 0:64]
    gb1_ref[...] = pay[37:38, 0:64]
    gb2_ref[...] = other[37:38, 0:64]
    gwo_ref[...] = pay[40:45, 0:64]
    diag = iota((8, 5), 0) == iota((8, 5), 1)
    gbo_ref[...] = jnp.sum(jnp.where(diag, other[40:48, 0:5], 0.0), axis=0, keepdims=True)


def call(body, outs, args, scratch=(), flops=0, trans=0, space=pltpu.VMEM):
    if space == pltpu.HBM:
        args = [pltpu.with_memory_space_constraint(x, pltpu.HBM) for x in args]
    shapes = [s if hasattr(s, "dtype") else jax.ShapeDtypeStruct(s, f32) for s in outs]
    scratch = [s if hasattr(s, "memory_space") or hasattr(s, "dtype") else pltpu.VMEM(s, f32) for s in scratch]
    return pl.pallas_call(
        body,
        out_shape=shapes,
        in_specs=[pl.BlockSpec(memory_space=space)] * len(args),
        out_specs=[VM] * len(shapes),
        scratch_shapes=scratch,
        cost_estimate=pl.CostEstimate(
            flops=flops, bytes_accessed=2000000, transcendentals=trans
        ),
        compiler_params=pltpu.CompilerParams(vmem_limit_bytes=40 * 1024 * 1024),
    )(*args)


def shift(x, axis, step):
    n = lax.axis_size(axis)
    return lax.ppermute(x, axis, [(i, (i + step) % n) for i in range(n)])


def both_ways(up, dn, axis):
    return shift(up, axis, 1), shift(dn, axis, -1)


def place(d):
    s, c = d // 16, d % 16
    return s // 8, (s // 2) % 4, s % 2, c // 4, c % 4


def together(fixed):
    groups = {}
    for d in range(256):
        groups.setdefault(tuple(place(d)[i] for i in fixed), []).append(d)
    return [groups[k] for k in sorted(groups)]


def send_to_all(x, groups):
    n = len(groups[0])
    y = jnp.broadcast_to(x[None], (n,) + x.shape)
    return lax.all_to_all(y, ("sub", "col"), 0, 0, axis_index_groups=groups, tiled=True)


SWAP = [(d, d ^ 16) for d in range(256)]


def grid_is_whole():
    return (lax.axis_size("sub"), lax.axis_size("col")) == (16, 16)


def on_first_core():
    return lax.axis_index("sub") % 2 == 0


def chip_sum(x):
    core, low, high = on_first_core(), x[:24], x[24:]
    mine = jnp.where(core, low, high)
    return mine + lax.ppermute(jnp.where(core, high, low), ("sub", "col"), SWAP)


def plane_sum(x):
    return send_to_all(x, together((0, 2, 3))).sum(0)


def rest_sum(x):
    core = on_first_core()
    x = send_to_all(x, together((1, 2, 4))).sum(0)
    other = lax.ppermute(x, ("sub", "col"), SWAP)
    return jnp.where(core, x, other), jnp.where(core, other, x)


def on_device(
    initial_state,
    state_cotangent,
    element_order,
    element_weight,
    element_diffusivity,
    in_weight,
    in_bias,
    mid_weight,
    mid_bias,
    out_weight,
    out_bias,
):
    hot = jax.ShapeDtypeStruct((128, 128), bf16)
    wide = jax.ShapeDtypeStruct((256, 8192), bf16)
    khot = jax.ShapeDtypeStruct((64, 192), bf16)

    def in_device(w, rp, rm, n):
        m = 10 if n == 10 else 11
        return call(
            lambda *r: xy_body(n, *r), [(n, 3, 2, 8, 128), (m, 8, 128), (m, 8, 128)], [w, rp, rm]
        )

    def faces(w, up, dn, n):
        w, yu, yd = in_device(w, *both_ways(up, dn, "sub"), n)
        yl, yr = both_ways(yu, yd, "col")
        return w, yl, yr

    w, up, dn, mk, g, kmat = call(
        start_body,
        [(12, 48, 128), (18, 8, 128), (18, 8, 128), (16, 128), hot, khot],
        [
            initial_state,
            state_cotangent,
            element_order,
            element_weight.reshape(1, 128),
            element_diffusivity.reshape(1, 128),
            jnp.asarray(stiffness_matrix()),
        ],
        [(F, 64, 128), (F, 64, 128), pltpu.VMEM((1, 128), jnp.int32), (1, 128), (1, 128)]
        + [(64, 64)]
        + [pltpu.SemaphoreType.DMA((6,))],
        space=pltpu.HBM,
    )
    (pw,) = call(
        prepare_body,
        [jax.ShapeDtypeStruct((272, 256), bf16)],
        [
            in_weight.T,
            in_bias.reshape(1, 64),
            mid_weight,
            mid_bias.reshape(1, 64),
            out_weight,
            out_bias.reshape(1, 5),
        ],
        [(5, 64), (1, 64), (64, 64), (1, 64), (5, 64), (1, 5), pltpu.SemaphoreType.DMA((6,))],
        flops=2000000,
        space=pltpu.HBM,
    )
    w, yl, yr = faces(w, up, dn, 12)
    pw, yl, yr = lax.optimization_barrier((pw, yl, yr))
    ten = [(10, 48, 128), (15, 8, 128), (15, 8, 128)]
    sa, im, w, up, dn = call(
        state_body, [(10, 64, 128), (64, 128)] + ten, [w, yl, yr, mk, kmat]
    )
    c0, x0, hh0, t0 = call(
        closure_body,
        [(F, 64, 128), (512, 128), wide, (128, 8192)],
        [sa, pw],
        [(512, 128)],
        flops=300000000,
        trans=1000000,
    )
    w, yl, yr = faces(w, up, dn, 10)
    part, m1, w, up, dn, x1, c1, hh1, dd1 = call(
        second_body,
        [(10, 64, 128), (F, 64, 128)] + ten + [(512, 128), (512, 128), wide, wide],
        [w, yl, yr, mk, im, sa, c0, pw, kmat],
        [(512, 128)] * 2,
        flops=900000000,
        trans=1000000,
    )
    back, gw, gb = call(
        first_body,
        [(F, 64, 128), (384, 160), (8, 128)],
        [x0, m1, hh0, t0, pw],
        [(512, 128)] * 2,
        flops=600000000,
    )
    rp, rm = both_ways(up, dn, "sub")
    gw, rp, rm = lax.optimization_barrier((gw, rp, rm))
    (pay,) = call(grads_body, [(48, 128)], [x1, c1, hh1, dd1, gw, gb], flops=300000000)
    w, yu, yd = in_device(w, rp, rm, 10)
    if grid_is_whole():
        pay = chip_sum(pay)
        pay, yu, yd = lax.optimization_barrier((pay, yu, yd))
        yl, yr = both_ways(yu, yd, "col")
        pay = plane_sum(pay)
        pay, yl, yr = lax.optimization_barrier((pay, yl, yr))
        terms = list(rest_sum(pay))
    else:
        yl, yr = both_ways(yu, yd, "col")
        pay = lax.psum(pay, ("sub", "col"))
        terms = [pay[:24], pay[24:]]
    out_state, out_adj = call(
        finish_body,
        [(F, 64, 128), (F, 64, 128)],
        [w, yl, yr, mk, im, part, back, g],
        flops=20000000,
    )
    gw1, gb1, gw2, gb2, gwo, gbo = call(
        output_body, [(5, 64), (1, 64), (64, 64), (1, 64), (5, 64), (1, 5)], terms
    )
    return (
        out_state,
        out_adj,
        gw1.T,
        gb1.reshape(64),
        gw2,
        gb2.reshape(64),
        gwo,
        gbo.reshape(5),
    )


def solution(mesh):
    split = P(None, None, ("sub", "col"))
    placed = (split, split, P(("sub", "col"), None), P(("sub", "col")), P(("sub", "col")))
    return jax.shard_map(
        on_device,
        mesh=mesh,
        in_specs=placed + (P(),) * 6,
        out_specs=(split, split) + (P(),) * 6,
        check_vma=False,
    )
```

```python
import math

import jax
import jax.numpy as jnp
import numpy as np
from jax import lax
from jax.experimental import pallas as pl
from jax.experimental.pallas import tpu as pltpu
from jax.sharding import PartitionSpec as P

F = 5
STEP = 0.05
CH = 32
NW = CH * 128
f32, bf16 = jnp.float32, jnp.bfloat16
VM = pl.BlockSpec(memory_space=pltpu.VMEM)


def stiffness_matrix():
    at = [-1.0, -math.sqrt(0.2), math.sqrt(0.2), 1.0]
    w = np.array([1.0 / 6.0, 5.0 / 6.0, 5.0 / 6.0, 1.0 / 6.0])
    prods = [np.prod([at[r] - at[p] for p in range(4) if p != r]) for r in range(4)]
    d = np.zeros((4, 4))
    for r in range(4):
        for c in range(4):
            if r == c:
                d[r, c] = sum(1.0 / (at[r] - at[p]) for p in range(4) if p != r)
            else:
                d[r, c] = prods[r] / (prods[c] * (at[r] - at[c]))
    s = d.T @ np.diag(w) @ d
    m = np.diag(w)
    k = np.kron(m, np.kron(s, m)) + np.kron(m, np.kron(m, s)) + np.kron(s, np.kron(m, m))
    return k.astype(np.float32)


def iota(shape, dim):
    return lax.broadcasted_iota(jnp.int32, shape, dim)


def next_k(x):
    ax = x.ndim - 1
    lane = iota(x.shape, ax) & 63
    return jnp.where(lane == 63, pltpu.roll(x, 63, ax), pltpu.roll(x, 127, ax))


def prev_k(x):
    ax = x.ndim - 1
    lane = iota(x.shape, ax) & 63
    return jnp.where(lane == 0, pltpu.roll(x, 65, ax), pltpu.roll(x, 1, ax))


def zsum(v):
    n = v.shape[0]
    top = v[:, 48:64] + next_k(v[:, 0:16])
    return jnp.concatenate([v[:, 16:48], top], axis=1)


def zfill(w):
    return jnp.concatenate([prev_k(w[:, 32:48]), w], axis=1)


def sroll(x, s):
    return pltpu.roll(x, s % 8, x.ndim - 2) if s % 8 else x


def xpack(w):
    n = w.shape[0]
    h = n // 2
    t = w.reshape(n, 3, 2, 8, 128)
    v0, v1 = t[:, :, 0].reshape(n * 3, 8, 128), t[:, :, 1].reshape(n * 3, 8, 128)
    low = iota((h * 3, 8, 128), 1) < 4
    up = jnp.where(low, sroll(v1[: h * 3], 4), v1[h * 3 :])
    dn = jnp.where(low, v0[: h * 3], sroll(v0[h * 3 :], 4))
    return up, dn


def xadd(w, rp, rm):
    n = w.shape[0]
    h = n // 2
    t = w.reshape(n, 3, 2, 8, 128)
    v0, v1 = t[:, :, 0].reshape(n * 3, 8, 128), t[:, :, 1].reshape(n * 3, 8, 128)
    low = iota((h * 3, 8, 128), 1) < 4
    zero = jnp.zeros_like(rp)
    a0 = jnp.concatenate([jnp.where(low, rp, zero), jnp.where(low, sroll(rp, 4), zero)], axis=0)
    a1 = jnp.concatenate([jnp.where(low, zero, sroll(rm, 4)), jnp.where(low, zero, rm)], axis=0)
    v0, v1 = v0 + a0, v1 + a1
    return v0, v1


def ylocal(v):
    b = iota(v.shape, 1) & 3
    left = iota(v.shape, 2) < 64
    d = jnp.where(b == 0, sroll(v, 5), sroll(v, 3))
    d = pltpu.roll(d, 64, 2)
    zero = jnp.zeros_like(v)
    here = ((b == 0) & (~left)) | ((b == 3) & left)
    out = ((b == 0) & left) | ((b == 3) & (~left))
    return v + jnp.where(here, d, zero), jnp.where(out, d, zero)


def xy_body(n, w_ref, rp_ref, rm_ref, wo_ref, yu_ref, yd_ref):
    ys = []
    w = w_ref[...]
    v0, v1 = xadd(w, rp_ref[...], rm_ref[...])
    for part, v in enumerate((v0, v1)):
        v, e = ylocal(v)
        wo_ref[:, :, part] = v.reshape(n, 3, 8, 128)
        e = e.reshape(n, 3, 8, 128)
        ys.append(e[:, 0] + sroll(e[:, 1], 1) + sroll(e[:, 2], 2))
    left = iota((n, 8, 128), 2) < 64
    m = yu_ref.shape[0]
    yu_ref[...] = jnp.where(left, ys[0], pltpu.roll(ys[1], 64, 2))[:m]
    yd_ref[...] = jnp.where(left, pltpu.roll(ys[0], 64, 2), ys[1])[:m]


def yadd(w, yl, yr):
    m = yl.shape[0]
    left = iota((m, 8, 128), 2) < 64
    b = iota((m, 8, 128), 1) & 3
    use = ((b == 0) & left) | ((b == 3) & (~left))
    zs = (
        jnp.where(left, yl, pltpu.roll(yr, 64, 2)),
        jnp.where(left, pltpu.roll(yl, 64, 2), yr),
    )
    rows = []
    for q in range(3):
        for part, z in enumerate(zs):
            rows.append(w[:m, q, part] + jnp.where(use, sroll(z, -q), jnp.zeros_like(z)))
    return jnp.concatenate(rows, axis=1)


def one_hot(order):
    row = jnp.broadcast_to(order, (128, 128))
    return jnp.where(row == iota((128, 128), 0), 1.0, 0.0).astype(bf16)


def split3(x):
    h = x.astype(bf16)
    r = x - h.astype(f32)
    m = r.astype(bf16)
    l = (r - m.astype(f32)).astype(bf16)
    return h, m, l


def permute_nt(x, g):
    dims = (((1,), (1,)), ((), ()))
    h, m, l = (lax.dot_general(p, g, dims, preferred_element_type=f32) for p in split3(x))
    return h + m + l


def permute_nn(x, g):
    h, m, l = (jnp.dot(p, g, preferred_element_type=f32) for p in split3(x))
    return h + m + l


def quad(shape):
    r = iota(shape, 0)
    w = 1.0
    for i in (r >> 4, (r >> 2) & 3, r & 3):
        w = w * jnp.where((i == 0) | (i == 3), 1.0 / 6.0, 5.0 / 6.0)
    return w


def fetch(srcs, dsts, sems):
    copies = [pltpu.make_async_copy(a, b, sems.at[i]) for i, (a, b) in enumerate(zip(srcs, dsts))]
    for c in copies:
        c.start()
    for c in copies:
        c.wait()


def start_body(
    s_in, c_in, o_in, ew_in, ed_in, k_in, w_ref, up_ref, dn_ref, mk_ref, g_ref, k_ref, *scratch
):
    s_ref, c_ref, o_ref, ew_ref, ed_ref, kf_ref, sems = scratch
    fetch((s_in, c_in, o_in, ew_in, ed_in, k_in), scratch[:6], sems)
    kh, kl = two(kf_ref[...])
    k_ref[...] = jnp.concatenate([kh, kh, kl], axis=1)
    g = one_hot(o_ref[...])
    g_ref[...] = g
    rows = []
    for ref in (s_ref, c_ref):
        for f in range(F):
            for q in range(4):
                rows.append(ref[f, pl.ds(q, 16, stride=4), :])
    el = jnp.concatenate(
        [jnp.broadcast_to(ew_ref[...], (8, 128)), jnp.broadcast_to(ed_ref[...], (8, 128))], axis=0
    )
    x = permute_nt(jnp.concatenate(rows + [el], axis=0), g)
    mass = quad((64, 128)) * x[640:641]
    mk_ref[...] = x[640:656]
    s = x[:320].reshape(F, 64, 128) * mass[None]
    c = x[320:640].reshape(F, 64, 128)
    v = jnp.concatenate([s, mass[None], c, jnp.zeros((1, 64, 128), f32)], axis=0)
    w = zsum(v)
    w_ref[...] = w
    up_ref[...], dn_ref[...] = xpack(w)


def stiffness(v, kmat, kappa):
    n = v.shape[0]
    x = jnp.concatenate([v[i] for i in range(n)], axis=1)
    h = x.astype(bf16)
    l = (x - h.astype(f32)).astype(bf16)
    y = jnp.dot(kmat, jnp.concatenate([h, l, h], axis=0), preferred_element_type=f32)
    return jnp.stack([y[:, i * 128 : (i + 1) * 128] * kappa for i in range(n)], axis=0)


def state_body(w_ref, yl_ref, yr_ref, mk_ref, k_ref, sa_ref, im_ref, w2_ref, up_ref, dn_ref):
    v = zfill(yadd(w_ref[...], yl_ref[...], yr_ref[...]))
    im = 1.0 / v[F]
    im_ref[...] = im
    sa = jnp.concatenate([v[:F], v[F + 1 : 2 * F + 1]], axis=0) * im[None]
    sa_ref[...] = sa
    w = zsum(stiffness(sa, k_ref[...], mk_ref[8:9]))
    w2_ref[...] = w
    up_ref[...], dn_ref[...] = xpack(w)


def prepare_body(w1_in, b1_in, w2_in, b2_in, wo_in, bo_in, p_ref, *scratch):
    fetch((w1_in, b1_in, w2_in, b2_in, wo_in, bo_in), scratch[:6], scratch[6])
    w1, b1, w2, b2, wo, bo = (r[...] for r in scratch[:6])
    z = jnp.zeros((64, 64), f32)
    pad3 = jnp.zeros((3, 64), f32)
    w1b = jnp.concatenate([w1, b1, jnp.zeros((2, 64), f32)], axis=0)
    w1p = jnp.concatenate([w1, pad3], axis=0)
    wop = jnp.concatenate([wo, pad3], axis=0)

    def columns(parts, rows):
        if rows < 256:
            parts = parts + [jnp.zeros((256 - rows, 64), f32)]
        return jnp.concatenate(parts, axis=0).T

    l2 = columns([w2.T] * 3 + [jnp.broadcast_to(b2, (8, 64))], 200)
    l2t = columns([w2] * 3, 192)
    l1 = columns([w1b] * 4, 32)
    lot = columns([wop] * 4, 32)
    both = jnp.concatenate([wop, w1p], axis=0)
    diag = iota((16, 5), 0) == iota((16, 5), 1)
    bias = jnp.sum(jnp.where(diag, jnp.broadcast_to(bo, (16, 5)), 0.0), axis=1, keepdims=True)
    bias = jnp.where(iota((16, 64), 1) < 2, jnp.broadcast_to(bias, (16, 64)), z[:16])
    small = jnp.concatenate([both, both, both, bias], axis=1)

    def parts(p, high):
        h = p.astype(bf16).astype(f32)
        return jnp.where(high, h, p - h).astype(bf16)

    col = iota((128, 256), 1)
    high = (col < 128) | (col == 192)
    p_ref[0:128] = parts(jnp.concatenate([l2, l2t], axis=0), high)
    p_ref[128:256] = parts(jnp.concatenate([l1, lot], axis=0), col < 16)
    p_ref[256:272] = parts(small, high[:16])


def weights(p_ref):
    return dict(
        l2=p_ref[0:64, 0:208],
        l2t=p_ref[64:128, 0:192],
        l1=p_ref[128:192, 0:32],
        lot=p_ref[192:256, 0:32],
        lo=p_ref[256:272, 0:208],
    )


def two(x):
    h = x.astype(bf16)
    return h, (x - h.astype(f32)).astype(bf16)


def stack8(x):
    h = x.astype(bf16).astype(f32)
    l = x - h
    return jnp.concatenate([h, l, h, l], axis=0).astype(bf16)


def mm(a, b):
    return jnp.dot(a, b, preferred_element_type=f32)


def nt(a, b):
    return lax.dot_general(a, b, (((1,), (1,)), ((), ())), preferred_element_type=f32)


def load8(ref, n0):
    return jnp.concatenate([ref[pl.ds(n0 + i, 8, stride=64), :] for i in range(CH)], axis=1)


def store8(ref, n0, x):
    for i in range(CH):
        ref[pl.ds(n0 + i, 8, stride=64), :] = x[:, i * 128 : (i + 1) * 128]


def put_fields(ref, x, ones):
    ref[0 : F * 64, :] = x.reshape(F * 64, 128)
    ref[F * 64 : F * 64 + 64, :] = jnp.full((64, 128), 1.0 if ones else 0.0, f32)
    ref[F * 64 + 64 :, :] = jnp.zeros((128, 128), f32)


def bias_rows():
    return jnp.where(iota((16, NW), 0) < 2, 1.0, 0.0).astype(bf16)


def forward(x8, w, ones):
    h1 = jnp.tanh(mm(w["l1"], stack8(x8)))
    h1h, h1l = two(h1)
    h2 = jnp.tanh(mm(w["l2"], jnp.concatenate([h1h, h1l, h1h, ones], axis=0)))
    h2h, h2l = two(h2)
    return h1, h1h, h1l, h2, h2h, h2l


def lanes_of(i):
    return pl.ds(pl.multiple_of(i * NW, NW), NW)


def put4(ref, i, parts):
    for k, p in enumerate(parts):
        ref[k * 64 : k * 64 + 64, lanes_of(i)] = p


def closure_body(sa_ref, p_ref, c_ref, x_ref, hh_ref, t_ref, o_ref):
    put_fields(x_ref, sa_ref[0:F], True)
    w = weights(p_ref)
    ones = bias_rows()

    def chunk(i, carry):
        n0 = i * CH
        h1, h1h, h1l, h2, h2h, h2l = forward(load8(x_ref, n0), w, ones)
        put4(hh_ref, i, (h1h, h1l, h2h, h2l))
        t_ref[0:64, lanes_of(i)] = 1.0 - h1 * h1
        t_ref[64:128, lanes_of(i)] = 1.0 - h2 * h2
        out = mm(w["lo"], jnp.concatenate([h2h, h2l, h2h, ones], axis=0))
        store8(o_ref, n0, out[0:8])
        return carry

    lax.fori_loop(0, 64 // CH, chunk, 0)
    c_ref[...] = o_ref[0 : F * 64].reshape(F, 64, 128)


def backward(c8, t1, t2, w):
    d2h, d2l = two(mm(w["lot"], stack8(c8)) * t2)
    d1h, d1l = two(mm(w["l2t"], jnp.concatenate([d2h, d2l, d2h], axis=0)) * t1)
    back = mm(w["lo"][:, 0:192], jnp.concatenate([d1h, d1l, d1h], axis=0))[8:16]
    return back, d2h, d2l, d1h, d1l


def stack2(x):
    h = x.astype(bf16).astype(f32)
    return jnp.concatenate([h, x - h], axis=0).astype(bf16)


def add_grads(acc, x8, c8, h1, h2, d2, d1):
    gw, gb = acc
    right = jnp.concatenate([h1, stack2(x8), stack2(c8)], axis=0)
    gw = gw + nt(jnp.concatenate([d2, d1, h2], axis=0), right)
    for i in range(CH):
        gb = gb + c8[:, i * 128 : (i + 1) * 128]
    return gw, gb


def no_grads():
    return jnp.zeros((384, 160), f32), jnp.zeros((8, 128), f32)


def second_body(
    w_ref, yl_ref, yr_ref, mk_ref, im_ref, sa_ref, c0_ref, p_ref, k_ref,
    part_ref, m1_ref, w2_ref, up_ref, dn_ref, x_ref, c_ref, hh_ref, dd_ref,
    o_ref, b_ref,
):
    im = im_ref[...] * STEP
    mass = quad((64, 128)) * mk_ref[0:1]
    v = zfill(yadd(w_ref[...], yl_ref[...], yr_ref[...])) * im[None]
    a2 = sa_ref[F:]
    s1 = sa_ref[0:F] + STEP * c0_ref[...] - v[0:F]
    put_fields(x_ref, s1, True)
    put_fields(c_ref, a2 * mass[None], False)
    w = weights(p_ref)
    ones = bias_rows()

    def chunk(i, carry):
        n0 = i * CH
        h1, h1h, h1l, h2, h2h, h2l = forward(load8(x_ref, n0), w, ones)
        put4(hh_ref, i, (h1h, h1l, h2h, h2l))
        out = mm(w["lo"], jnp.concatenate([h2h, h2l, h2h, ones], axis=0))
        store8(o_ref, n0, out[0:8])
        back, *ds = backward(load8(c_ref, n0), 1.0 - h1 * h1, 1.0 - h2 * h2, w)
        put4(dd_ref, i, ds)
        store8(b_ref, n0, back)
        return carry

    lax.fori_loop(0, 64 // CH, chunk, 0)
    back = b_ref[0 : F * 64].reshape(F, 64, 128)
    a1 = a2 - v[F:] + (STEP / mass)[None] * back
    m1_ref[...] = a1 * mass[None]
    part_ref[0:F] = s1 + STEP * o_ref[0 : F * 64].reshape(F, 64, 128)
    part_ref[F:] = a1
    wz = zsum(stiffness(jnp.concatenate([s1, a1], axis=0), k_ref[...], mk_ref[8:9]))
    w2_ref[...] = wz
    up_ref[...], dn_ref[...] = xpack(wz)


def first_body(x_ref, m1_ref, hh_ref, t_ref, p_ref, back_ref, gw_ref, gb_ref, c_ref, b_ref):
    put_fields(c_ref, m1_ref[...], False)
    w = weights(p_ref)

    def chunk(i, acc):
        n0 = i * CH
        at = lanes_of(i)
        c8 = load8(c_ref, n0)
        back, d2h, d2l, d1h, d1l = backward(c8, t_ref[0:64, at], t_ref[64:128, at], w)
        store8(b_ref, n0, back)
        return add_grads(
            acc, load8(x_ref, n0), c8, hh_ref[0:128, at], hh_ref[128:256, at],
            jnp.concatenate([d2h, d2l], axis=0), jnp.concatenate([d1h, d1l], axis=0),
        )

    gw_ref[...], gb_ref[...] = lax.fori_loop(0, 64 // CH, chunk, no_grads())
    back_ref[...] = b_ref[0 : F * 64].reshape(F, 64, 128)


def grads_body(x_ref, c_ref, hh_ref, dd_ref, gw_ref, gb_ref, pay_ref):
    def chunk(i, acc):
        n0 = i * CH
        at = lanes_of(i)
        return add_grads(
            acc, load8(x_ref, n0), load8(c_ref, n0),
            hh_ref[0:128, at], hh_ref[128:256, at], dd_ref[0:128, at], dd_ref[128:256, at],
        )

    g, gb = lax.fori_loop(0, 64 // CH, chunk, (gw_ref[...], gb_ref[...]))

    def fold(t):
        return t + pltpu.roll(t, 64, 1)

    gw = fold(g[0:64, 0:128] + g[64:128, 0:128])
    gs = g[:, 128:160].T
    gx2 = fold(gs[0:8, 0:128] + gs[8:16, 0:128])
    gx1 = fold(gs[0:8, 128:256] + gs[8:16, 128:256])
    gc = fold(gs[16:24, 256:384] + gs[24:32, 256:384])
    gbs = jnp.broadcast_to(jnp.sum(gb, axis=1, keepdims=True), (8, 128))
    left = iota((32, 128), 1) < 64
    scale = STEP / 256.0
    pay_ref[0:32] = jnp.where(left, gw[0:32], gw[32:64]) * scale
    pay_ref[32:40] = jnp.where(left[:8], gx1, gx2) * scale
    pay_ref[40:48] = jnp.where(left[:8], gc, gbs) * scale


def finish_body(
    w_ref, yl_ref, yr_ref, mk_ref, im_ref, part_ref, back_ref, g_ref, s_ref, a_ref
):
    im = im_ref[...] * STEP
    mass = quad((64, 128)) * mk_ref[0:1]
    v = zfill(yadd(w_ref[...], yl_ref[...], yr_ref[...])) * im[None]
    s2 = part_ref[0:F] - v[0:F]
    a0 = (part_ref[F:] - v[F:]) * mass[None] + STEP * back_ref[...]
    x = jnp.concatenate([s2.reshape(320, 128), a0.reshape(320, 128)], axis=0)
    y = permute_nn(x, g_ref[...])
    for i, ref in enumerate((s_ref, a_ref)):
        for f in range(F):
            for q in range(4):
                r = (i * F + f) * 64 + q * 16
                ref[f, pl.ds(q, 16, stride=4), :] = y[r : r + 16]


def output_body(l_ref, h_ref, gw1_ref, gb1_ref, gw2_ref, gb2_ref, gwo_ref, gbo_ref):
    pay = jnp.concatenate([l_ref[...], h_ref[...]], axis=0)
    gw2_ref[0:32] = pay[0:32, 0:64]
    other = pltpu.roll(pay, 64, 1)
    gw2_ref[32:64] = other[0:32, 0:64]
    gw1_ref[...] = pay[32:37, 0:64]
    gb1_ref[...] = pay[37:38, 0:64]
    gb2_ref[...] = other[37:38, 0:64]
    gwo_ref[...] = pay[40:45, 0:64]
    diag = iota((8, 5), 0) == iota((8, 5), 1)
    gbo_ref[...] = jnp.sum(jnp.where(diag, other[40:48, 0:5], 0.0), axis=0, keepdims=True)


def call(body, outs, args, scratch=(), flops=0, trans=0, space=pltpu.VMEM):
    if space == pltpu.HBM:
        args = [pltpu.with_memory_space_constraint(x, pltpu.HBM) for x in args]
    shapes = [s if hasattr(s, "dtype") else jax.ShapeDtypeStruct(s, f32) for s in outs]
    scratch = [s if hasattr(s, "memory_space") or hasattr(s, "dtype") else pltpu.VMEM(s, f32) for s in scratch]
    return pl.pallas_call(
        body,
        out_shape=shapes,
        in_specs=[pl.BlockSpec(memory_space=space)] * len(args),
        out_specs=[VM] * len(shapes),
        scratch_shapes=scratch,
        cost_estimate=pl.CostEstimate(
            flops=flops, bytes_accessed=2000000, transcendentals=trans
        ),
        compiler_params=pltpu.CompilerParams(vmem_limit_bytes=40 * 1024 * 1024),
    )(*args)


def shift(x, axis, step):
    n = lax.axis_size(axis)
    return lax.ppermute(x, axis, [(i, (i + step) % n) for i in range(n)])


def both_ways(up, dn, axis):
    return shift(up, axis, 1), shift(dn, axis, -1)


def place(d):
    s, c = d // 16, d % 16
    return s // 8, (s // 2) % 4, s % 2, c // 4, c % 4


def together(fixed):
    groups = {}
    for d in range(256):
        groups.setdefault(tuple(place(d)[i] for i in fixed), []).append(d)
    return [groups[k] for k in sorted(groups)]


def send_to_all(x, groups):
    n = len(groups[0])
    y = jnp.broadcast_to(x[None], (n,) + x.shape)
    return lax.all_to_all(y, ("sub", "col"), 0, 0, axis_index_groups=groups, tiled=True)


SWAP = [(d, d ^ 16) for d in range(256)]


def grid_is_whole():
    return (lax.axis_size("sub"), lax.axis_size("col")) == (16, 16)


def on_first_core():
    return lax.axis_index("sub") % 2 == 0


def chip_sum(x, core):
    low, high = x[:24], x[24:]
    mine = jnp.where(core, low, high)
    return mine + lax.ppermute(jnp.where(core, high, low), ("sub", "col"), SWAP)


def plane_sum(x):
    return send_to_all(x, together((0, 2, 3))).sum(0)


def rest_sum(x, core):
    x = send_to_all(x, together((1, 2, 4))).sum(0)
    other = lax.ppermute(x, ("sub", "col"), SWAP)
    return jnp.where(core, x, other), jnp.where(core, other, x)


def on_device(
    initial_state,
    state_cotangent,
    element_order,
    element_weight,
    element_diffusivity,
    in_weight,
    in_bias,
    mid_weight,
    mid_bias,
    out_weight,
    out_bias,
):
    core, element_weight = lax.optimization_barrier((on_first_core(), element_weight))
    hot = jax.ShapeDtypeStruct((128, 128), bf16)
    wide = jax.ShapeDtypeStruct((256, 8192), bf16)
    khot = jax.ShapeDtypeStruct((64, 192), bf16)

    def in_device(w, rp, rm, n):
        m = 10 if n == 10 else 11
        return call(
            lambda *r: xy_body(n, *r), [(n, 3, 2, 8, 128), (m, 8, 128), (m, 8, 128)], [w, rp, rm]
        )

    def faces(w, up, dn, n):
        w, yu, yd = in_device(w, *both_ways(up, dn, "sub"), n)
        yl, yr = both_ways(yu, yd, "col")
        return w, yl, yr

    w, up, dn, mk, g, kmat = call(
        start_body,
        [(12, 48, 128), (18, 8, 128), (18, 8, 128), (16, 128), hot, khot],
        [
            initial_state,
            state_cotangent,
            element_order,
            element_weight.reshape(1, 128),
            element_diffusivity.reshape(1, 128),
            jnp.asarray(stiffness_matrix()),
        ],
        [(F, 64, 128), (F, 64, 128), pltpu.VMEM((1, 128), jnp.int32), (1, 128), (1, 128)]
        + [(64, 64)]
        + [pltpu.SemaphoreType.DMA((6,))],
        space=pltpu.HBM,
    )
    (pw,) = call(
        prepare_body,
        [jax.ShapeDtypeStruct((272, 256), bf16)],
        [
            in_weight.T,
            in_bias.reshape(1, 64),
            mid_weight,
            mid_bias.reshape(1, 64),
            out_weight,
            out_bias.reshape(1, 5),
        ],
        [(5, 64), (1, 64), (64, 64), (1, 64), (5, 64), (1, 5), pltpu.SemaphoreType.DMA((6,))],
        flops=2000000,
        space=pltpu.HBM,
    )
    w, yl, yr = faces(w, up, dn, 12)
    pw, yl, yr = lax.optimization_barrier((pw, yl, yr))
    ten = [(10, 48, 128), (15, 8, 128), (15, 8, 128)]
    sa, im, w, up, dn = call(
        state_body, [(10, 64, 128), (64, 128)] + ten, [w, yl, yr, mk, kmat]
    )
    c0, x0, hh0, t0 = call(
        closure_body,
        [(F, 64, 128), (512, 128), wide, (128, 8192)],
        [sa, pw],
        [(512, 128)],
        flops=300000000,
        trans=1000000,
    )
    w, yl, yr = faces(w, up, dn, 10)
    part, m1, w, up, dn, x1, c1, hh1, dd1 = call(
        second_body,
        [(10, 64, 128), (F, 64, 128)] + ten + [(512, 128), (512, 128), wide, wide],
        [w, yl, yr, mk, im, sa, c0, pw, kmat],
        [(512, 128)] * 2,
        flops=900000000,
        trans=1000000,
    )
    back, gw, gb = call(
        first_body,
        [(F, 64, 128), (384, 160), (8, 128)],
        [x0, m1, hh0, t0, pw],
        [(512, 128)] * 2,
        flops=600000000,
    )
    rp, rm = both_ways(up, dn, "sub")
    gw, rp, rm = lax.optimization_barrier((gw, rp, rm))
    (pay,) = call(grads_body, [(48, 128)], [x1, c1, hh1, dd1, gw, gb], flops=300000000)
    w, yu, yd = in_device(w, rp, rm, 10)
    if grid_is_whole():
        pay = chip_sum(pay, core)
        pay, yu, yd = lax.optimization_barrier((pay, yu, yd))
        yl, yr = both_ways(yu, yd, "col")
        pay = plane_sum(pay)
        pay, yl, yr = lax.optimization_barrier((pay, yl, yr))
        terms = list(rest_sum(pay, core))
    else:
        yl, yr = both_ways(yu, yd, "col")
        pay = lax.psum(pay, ("sub", "col"))
        terms = [pay[:24], pay[24:]]
    out_state, out_adj = call(
        finish_body,
        [(F, 64, 128), (F, 64, 128)],
        [w, yl, yr, mk, im, part, back, g],
        flops=20000000,
    )
    gw1, gb1, gw2, gb2, gwo, gbo = call(
        output_body, [(5, 64), (1, 64), (64, 64), (1, 64), (5, 64), (1, 5)], terms
    )
    return (
        out_state,
        out_adj,
        gw1.T,
        gb1.reshape(64),
        gw2,
        gb2.reshape(64),
        gwo,
        gbo.reshape(5),
    )


def solution(mesh):
    split = P(None, None, ("sub", "col"))
    placed = (split, split, P(("sub", "col"), None), P(("sub", "col")), P(("sub", "col")))
    return jax.shard_map(
        on_device,
        mesh=mesh,
        in_specs=placed + (P(),) * 6,
        out_specs=(split, split) + (P(),) * 6,
        check_vma=False,
    )
```

```python
import math

import jax
import jax.numpy as jnp
import numpy as np
from jax import lax
from jax.experimental import pallas as pl
from jax.experimental.pallas import tpu as pltpu
from jax.sharding import PartitionSpec as P

F = 5
STEP = 0.05
CH = 32
NW = CH * 128
f32, bf16 = jnp.float32, jnp.bfloat16
VM = pl.BlockSpec(memory_space=pltpu.VMEM)


def stiffness_matrix():
    at = [-1.0, -math.sqrt(0.2), math.sqrt(0.2), 1.0]
    w = np.array([1.0 / 6.0, 5.0 / 6.0, 5.0 / 6.0, 1.0 / 6.0])
    prods = [np.prod([at[r] - at[p] for p in range(4) if p != r]) for r in range(4)]
    d = np.zeros((4, 4))
    for r in range(4):
        for c in range(4):
            if r == c:
                d[r, c] = sum(1.0 / (at[r] - at[p]) for p in range(4) if p != r)
            else:
                d[r, c] = prods[r] / (prods[c] * (at[r] - at[c]))
    s = d.T @ np.diag(w) @ d
    m = np.diag(w)
    k = np.kron(m, np.kron(s, m)) + np.kron(m, np.kron(m, s)) + np.kron(s, np.kron(m, m))
    return k.astype(np.float32)


def iota(shape, dim):
    return lax.broadcasted_iota(jnp.int32, shape, dim)


def next_k(x):
    ax = x.ndim - 1
    lane = iota(x.shape, ax) & 63
    return jnp.where(lane == 63, pltpu.roll(x, 63, ax), pltpu.roll(x, 127, ax))


def prev_k(x):
    ax = x.ndim - 1
    lane = iota(x.shape, ax) & 63
    return jnp.where(lane == 0, pltpu.roll(x, 65, ax), pltpu.roll(x, 1, ax))


def zsum(v):
    n = v.shape[0]
    top = v[:, 48:64] + next_k(v[:, 0:16])
    return jnp.concatenate([v[:, 16:48], top], axis=1)


def zfill(w):
    return jnp.concatenate([prev_k(w[:, 32:48]), w], axis=1)


def sroll(x, s):
    return pltpu.roll(x, s % 8, x.ndim - 2) if s % 8 else x


def xpack(w):
    n = w.shape[0]
    h = n // 2
    t = w.reshape(n, 3, 2, 8, 128)
    v0, v1 = t[:, :, 0].reshape(n * 3, 8, 128), t[:, :, 1].reshape(n * 3, 8, 128)
    low = iota((h * 3, 8, 128), 1) < 4
    up = jnp.where(low, sroll(v1[: h * 3], 4), v1[h * 3 :])
    dn = jnp.where(low, v0[: h * 3], sroll(v0[h * 3 :], 4))
    return up, dn


def xadd(w, rp, rm):
    n = w.shape[0]
    h = n // 2
    t = w.reshape(n, 3, 2, 8, 128)
    v0, v1 = t[:, :, 0].reshape(n * 3, 8, 128), t[:, :, 1].reshape(n * 3, 8, 128)
    low = iota((h * 3, 8, 128), 1) < 4
    zero = jnp.zeros_like(rp)
    a0 = jnp.concatenate([jnp.where(low, rp, zero), jnp.where(low, sroll(rp, 4), zero)], axis=0)
    a1 = jnp.concatenate([jnp.where(low, zero, sroll(rm, 4)), jnp.where(low, zero, rm)], axis=0)
    v0, v1 = v0 + a0, v1 + a1
    return v0, v1


def ylocal(v):
    b = iota(v.shape, 1) & 3
    left = iota(v.shape, 2) < 64
    d = jnp.where(b == 0, sroll(v, 5), sroll(v, 3))
    d = pltpu.roll(d, 64, 2)
    zero = jnp.zeros_like(v)
    here = ((b == 0) & (~left)) | ((b == 3) & left)
    out = ((b == 0) & left) | ((b == 3) & (~left))
    return v + jnp.where(here, d, zero), jnp.where(out, d, zero)


def xy_body(n, w_ref, rp_ref, rm_ref, wo_ref, yu_ref, yd_ref):
    ys = []
    w = w_ref[...]
    v0, v1 = xadd(w, rp_ref[...], rm_ref[...])
    for part, v in enumerate((v0, v1)):
        v, e = ylocal(v)
        wo_ref[:, :, part] = v.reshape(n, 3, 8, 128)
        e = e.reshape(n, 3, 8, 128)
        ys.append(e[:, 0] + sroll(e[:, 1], 1) + sroll(e[:, 2], 2))
    left = iota((n, 8, 128), 2) < 64
    m = yu_ref.shape[0]
    yu_ref[...] = jnp.where(left, ys[0], pltpu.roll(ys[1], 64, 2))[:m]
    yd_ref[...] = jnp.where(left, pltpu.roll(ys[0], 64, 2), ys[1])[:m]


def yadd(w, yl, yr):
    m = yl.shape[0]
    left = iota((m, 8, 128), 2) < 64
    b = iota((m, 8, 128), 1) & 3
    use = ((b == 0) & left) | ((b == 3) & (~left))
    zs = (
        jnp.where(left, yl, pltpu.roll(yr, 64, 2)),
        jnp.where(left, pltpu.roll(yl, 64, 2), yr),
    )
    rows = []
    for q in range(3):
        for part, z in enumerate(zs):
            rows.append(w[:m, q, part] + jnp.where(use, sroll(z, -q), jnp.zeros_like(z)))
    return jnp.concatenate(rows, axis=1)


def one_hot(order):
    row = jnp.broadcast_to(order, (128, 128))
    return jnp.where(row == iota((128, 128), 0), 1.0, 0.0).astype(bf16)


def split3(x):
    h = x.astype(bf16)
    r = x - h.astype(f32)
    m = r.astype(bf16)
    l = (r - m.astype(f32)).astype(bf16)
    return h, m, l


def permute_nt(x, g):
    dims = (((1,), (1,)), ((), ()))
    h, m, l = (lax.dot_general(p, g, dims, preferred_element_type=f32) for p in split3(x))
    return h + m + l


def permute_nn(x, g):
    h, m, l = (jnp.dot(p, g, preferred_element_type=f32) for p in split3(x))
    return h + m + l


def quad(shape):
    r = iota(shape, 0)
    w = 1.0
    for i in (r >> 4, (r >> 2) & 3, r & 3):
        w = w * jnp.where((i == 0) | (i == 3), 1.0 / 6.0, 5.0 / 6.0)
    return w


def fetch(srcs, dsts, sems):
    copies = [pltpu.make_async_copy(a, b, sems.at[i]) for i, (a, b) in enumerate(zip(srcs, dsts))]
    for c in copies:
        c.start()
    for c in copies:
        c.wait()


def start_body(
    s_in, c_in, o_in, ew_in, ed_in, k_in, w_ref, up_ref, dn_ref, mk_ref, g_ref, k_ref, *scratch
):
    s_ref, c_ref, o_ref, ew_ref, ed_ref, kf_ref, sems = scratch
    fetch((s_in, c_in, o_in, ew_in, ed_in, k_in), scratch[:6], sems)
    kh, kl = two(kf_ref[...])
    k_ref[...] = jnp.concatenate([kh, kh, kl], axis=1)
    g = one_hot(o_ref[...])
    g_ref[...] = g
    rows = []
    for ref in (s_ref, c_ref):
        for f in range(F):
            for q in range(4):
                rows.append(ref[f, pl.ds(q, 16, stride=4), :])
    el = jnp.concatenate(
        [jnp.broadcast_to(ew_ref[...], (8, 128)), jnp.broadcast_to(ed_ref[...], (8, 128))], axis=0
    )
    x = permute_nt(jnp.concatenate(rows + [el], axis=0), g)
    mass = quad((64, 128)) * x[640:641]
    mk_ref[...] = x[640:656]
    s = x[:320].reshape(F, 64, 128) * mass[None]
    c = x[320:640].reshape(F, 64, 128)
    v = jnp.concatenate([s, mass[None], c, jnp.zeros((1, 64, 128), f32)], axis=0)
    w = zsum(v)
    w_ref[...] = w
    up_ref[...], dn_ref[...] = xpack(w)


def stiffness(v, kmat, kappa):
    n = v.shape[0]
    x = jnp.concatenate([v[i] for i in range(n)], axis=1)
    h = x.astype(bf16)
    l = (x - h.astype(f32)).astype(bf16)
    y = jnp.dot(kmat, jnp.concatenate([h, l, h], axis=0), preferred_element_type=f32)
    return jnp.stack([y[:, i * 128 : (i + 1) * 128] * kappa for i in range(n)], axis=0)


def state_body(w_ref, yl_ref, yr_ref, mk_ref, k_ref, sa_ref, im_ref, w2_ref, up_ref, dn_ref):
    v = zfill(yadd(w_ref[...], yl_ref[...], yr_ref[...]))
    im = 1.0 / v[F]
    im_ref[...] = im
    sa = jnp.concatenate([v[:F], v[F + 1 : 2 * F + 1]], axis=0) * im[None]
    sa_ref[...] = sa
    w = zsum(stiffness(sa, k_ref[...], mk_ref[8:9]))
    w2_ref[...] = w
    up_ref[...], dn_ref[...] = xpack(w)


def prepare_body(w1_in, b1_in, w2_in, b2_in, wo_in, bo_in, p_ref, *scratch):
    fetch((w1_in, b1_in, w2_in, b2_in, wo_in, bo_in), scratch[:6], scratch[6])
    w1, b1, w2, b2, wo, bo = (r[...] for r in scratch[:6])
    z = jnp.zeros((64, 64), f32)
    pad3 = jnp.zeros((3, 64), f32)
    w1b = jnp.concatenate([w1, b1, jnp.zeros((2, 64), f32)], axis=0)
    w1p = jnp.concatenate([w1, pad3], axis=0)
    wop = jnp.concatenate([wo, pad3], axis=0)

    def columns(parts, rows):
        if rows < 256:
            parts = parts + [jnp.zeros((256 - rows, 64), f32)]
        return jnp.concatenate(parts, axis=0).T

    l2 = columns([w2.T] * 3 + [jnp.broadcast_to(b2, (8, 64))], 200)
    l2t = columns([w2] * 3, 192)
    l1 = columns([w1b] * 4, 32)
    lot = columns([wop] * 4, 32)
    both = jnp.concatenate([wop, w1p], axis=0)
    diag = iota((16, 5), 0) == iota((16, 5), 1)
    bias = jnp.sum(jnp.where(diag, jnp.broadcast_to(bo, (16, 5)), 0.0), axis=1, keepdims=True)
    bias = jnp.where(iota((16, 64), 1) < 2, jnp.broadcast_to(bias, (16, 64)), z[:16])
    small = jnp.concatenate([both, both, both, bias], axis=1)

    def parts(p, high):
        h = p.astype(bf16).astype(f32)
        return jnp.where(high, h, p - h).astype(bf16)

    col = iota((128, 256), 1)
    high = (col < 128) | (col == 192)
    p_ref[0:128] = parts(jnp.concatenate([l2, l2t], axis=0), high)
    p_ref[128:256] = parts(jnp.concatenate([l1, lot], axis=0), col < 16)
    p_ref[256:272] = parts(small, high[:16])


def weights(p_ref):
    return dict(
        l2=p_ref[0:64, 0:208],
        l2t=p_ref[64:128, 0:192],
        l1=p_ref[128:192, 0:32],
        lot=p_ref[192:256, 0:32],
        lo=p_ref[256:272, 0:208],
    )


def two(x):
    h = x.astype(bf16)
    return h, (x - h.astype(f32)).astype(bf16)


def stack8(x):
    h = x.astype(bf16).astype(f32)
    l = x - h
    return jnp.concatenate([h, l, h, l], axis=0).astype(bf16)


def mm(a, b):
    return jnp.dot(a, b, preferred_element_type=f32)


def nt(a, b):
    return lax.dot_general(a, b, (((1,), (1,)), ((), ())), preferred_element_type=f32)


def load8(ref, n0, ch=CH):
    return jnp.concatenate([ref[pl.ds(n0 + i, 8, stride=64), :] for i in range(ch)], axis=1)


def store8(ref, n0, x):
    for i in range(x.shape[1] // 128):
        ref[pl.ds(n0 + i, 8, stride=64), :] = x[:, i * 128 : (i + 1) * 128]


def put_fields(ref, x, ones):
    ref[0 : F * 64, :] = x.reshape(F * 64, 128)
    ref[F * 64 : F * 64 + 64, :] = jnp.full((64, 128), 1.0 if ones else 0.0, f32)
    ref[F * 64 + 64 :, :] = jnp.zeros((128, 128), f32)


def bias_rows():
    return jnp.where(iota((16, NW), 0) < 2, 1.0, 0.0).astype(bf16)


def forward(x8, w, ones):
    h1 = jnp.tanh(mm(w["l1"], stack8(x8)))
    h1h, h1l = two(h1)
    h2 = jnp.tanh(mm(w["l2"], jnp.concatenate([h1h, h1l, h1h, ones], axis=0)))
    h2h, h2l = two(h2)
    return h1, h1h, h1l, h2, h2h, h2l


def lanes_of(i):
    return pl.ds(pl.multiple_of(i * NW, NW), NW)


def put4(ref, i, parts):
    for k, p in enumerate(parts):
        ref[k * 64 : k * 64 + 64, lanes_of(i)] = p


def closure_body(sa_ref, p_ref, c_ref, x_ref, hh_ref, t_ref, o_ref):
    put_fields(x_ref, sa_ref[0:F], True)
    w = weights(p_ref)
    ones = bias_rows()

    def chunk(i, carry):
        n0 = i * CH
        h1, h1h, h1l, h2, h2h, h2l = forward(load8(x_ref, n0), w, ones)
        put4(hh_ref, i, (h1h, h1l, h2h, h2l))
        t_ref[0:64, lanes_of(i)] = 1.0 - h1 * h1
        t_ref[64:128, lanes_of(i)] = 1.0 - h2 * h2
        out = mm(w["lo"], jnp.concatenate([h2h, h2l, h2h, ones], axis=0))
        store8(o_ref, n0, out[0:8])
        return carry

    lax.fori_loop(0, 64 // CH, chunk, 0)
    c_ref[...] = o_ref[0 : F * 64].reshape(F, 64, 128)


def backward(c8, t1, t2, w):
    d2h, d2l = two(mm(w["lot"], stack8(c8)) * t2)
    d1h, d1l = two(mm(w["l2t"], jnp.concatenate([d2h, d2l, d2h], axis=0)) * t1)
    back = mm(w["lo"][:, 0:192], jnp.concatenate([d1h, d1l, d1h], axis=0))[8:16]
    return back, d2h, d2l, d1h, d1l


def stack2(x):
    h = x.astype(bf16).astype(f32)
    return jnp.concatenate([h, x - h], axis=0).astype(bf16)


def add_grads(acc, x8, c8, h1, h2, d2, d1):
    gw, gb = acc
    right = jnp.concatenate([h1, stack2(x8), stack2(c8)], axis=0)
    gw = gw + nt(jnp.concatenate([d2, d1, h2], axis=0), right)
    for i in range(c8.shape[1] // 128):
        gb = gb + c8[:, i * 128 : (i + 1) * 128]
    return gw, gb


def no_grads():
    return jnp.zeros((384, 160), f32), jnp.zeros((8, 128), f32)


def second_body(
    w_ref, yl_ref, yr_ref, mk_ref, im_ref, sa_ref, c0_ref, p_ref, k_ref,
    part_ref, m1_ref, w2_ref, up_ref, dn_ref, x_ref, c_ref, hh_ref, dd_ref,
    o_ref, b_ref,
):
    im = im_ref[...] * STEP
    mass = quad((64, 128)) * mk_ref[0:1]
    v = zfill(yadd(w_ref[...], yl_ref[...], yr_ref[...])) * im[None]
    a2 = sa_ref[F:]
    s1 = sa_ref[0:F] + STEP * c0_ref[...] - v[0:F]
    put_fields(x_ref, s1, True)
    put_fields(c_ref, a2 * mass[None], False)
    w = weights(p_ref)
    ones = bias_rows()

    def chunk(i, carry):
        n0 = i * CH
        h1, h1h, h1l, h2, h2h, h2l = forward(load8(x_ref, n0), w, ones)
        put4(hh_ref, i, (h1h, h1l, h2h, h2l))
        out = mm(w["lo"], jnp.concatenate([h2h, h2l, h2h, ones], axis=0))
        store8(o_ref, n0, out[0:8])
        back, *ds = backward(load8(c_ref, n0), 1.0 - h1 * h1, 1.0 - h2 * h2, w)
        put4(dd_ref, i, ds)
        store8(b_ref, n0, back)
        return carry

    lax.fori_loop(0, 64 // CH, chunk, 0)
    back = b_ref[0 : F * 64].reshape(F, 64, 128)
    a1 = a2 - v[F:] + (STEP / mass)[None] * back
    m1_ref[...] = a1 * mass[None]
    part_ref[0:F] = s1 + STEP * o_ref[0 : F * 64].reshape(F, 64, 128)
    part_ref[F:] = a1
    wz = zsum(stiffness(jnp.concatenate([s1, a1], axis=0), k_ref[...], mk_ref[8:9]))
    w2_ref[...] = wz
    up_ref[...], dn_ref[...] = xpack(wz)


def first_body(x_ref, m1_ref, hh_ref, t_ref, p_ref, back_ref, gw_ref, gb_ref, c_ref, b_ref):
    put_fields(c_ref, m1_ref[...], False)
    w = weights(p_ref)

    c8 = load8(c_ref, 0, 64)
    back, d2h, d2l, d1h, d1l = backward(c8, t_ref[0:64], t_ref[64:128], w)
    store8(b_ref, 0, back)
    gw_ref[...], gb_ref[...] = add_grads(
        no_grads(), load8(x_ref, 0, 64), c8, hh_ref[0:128], hh_ref[128:256],
        jnp.concatenate([d2h, d2l], axis=0), jnp.concatenate([d1h, d1l], axis=0),
    )
    back_ref[...] = b_ref[0 : F * 64].reshape(F, 64, 128)


def grads_body(x_ref, c_ref, hh_ref, dd_ref, gw_ref, gb_ref, pay_ref):
    g, gb = add_grads(
        (gw_ref[...], gb_ref[...]), load8(x_ref, 0, 64), load8(c_ref, 0, 64),
        hh_ref[0:128], hh_ref[128:256], dd_ref[0:128], dd_ref[128:256],
    )

    def fold(t):
        return t + pltpu.roll(t, 64, 1)

    gw = fold(g[0:64, 0:128] + g[64:128, 0:128])
    gs = g[:, 128:160].T
    gx2 = fold(gs[0:8, 0:128] + gs[8:16, 0:128])
    gx1 = fold(gs[0:8, 128:256] + gs[8:16, 128:256])
    gc = fold(gs[16:24, 256:384] + gs[24:32, 256:384])
    gbs = jnp.broadcast_to(jnp.sum(gb, axis=1, keepdims=True), (8, 128))
    left = iota((32, 128), 1) < 64
    scale = STEP / 256.0
    pay_ref[0:32] = jnp.where(left, gw[0:32], gw[32:64]) * scale
    pay_ref[32:40] = jnp.where(left[:8], gx1, gx2) * scale
    pay_ref[40:48] = jnp.where(left[:8], gc, gbs) * scale


def finish_body(
    w_ref, yl_ref, yr_ref, mk_ref, im_ref, part_ref, back_ref, g_ref, s_ref, a_ref
):
    im = im_ref[...] * STEP
    mass = quad((64, 128)) * mk_ref[0:1]
    v = zfill(yadd(w_ref[...], yl_ref[...], yr_ref[...])) * im[None]
    s2 = part_ref[0:F] - v[0:F]
    a0 = (part_ref[F:] - v[F:]) * mass[None] + STEP * back_ref[...]
    x = jnp.concatenate([s2.reshape(320, 128), a0.reshape(320, 128)], axis=0)
    y = permute_nn(x, g_ref[...])
    for i, ref in enumerate((s_ref, a_ref)):
        for f in range(F):
            for q in range(4):
                r = (i * F + f) * 64 + q * 16
                ref[f, pl.ds(q, 16, stride=4), :] = y[r : r + 16]


def output_body(l_ref, h_ref, gw1_ref, gb1_ref, gw2_ref, gb2_ref, gwo_ref, gbo_ref):
    pay = jnp.concatenate([l_ref[...], h_ref[...]], axis=0)
    gw2_ref[0:32] = pay[0:32, 0:64]
    other = pltpu.roll(pay, 64, 1)
    gw2_ref[32:64] = other[0:32, 0:64]
    gw1_ref[...] = pay[32:37, 0:64]
    gb1_ref[...] = pay[37:38, 0:64]
    gb2_ref[...] = other[37:38, 0:64]
    gwo_ref[...] = pay[40:45, 0:64]
    diag = iota((8, 5), 0) == iota((8, 5), 1)
    gbo_ref[...] = jnp.sum(jnp.where(diag, other[40:48, 0:5], 0.0), axis=0, keepdims=True)


def call(body, outs, args, scratch=(), flops=0, trans=0, space=pltpu.VMEM):
    if space == pltpu.HBM:
        args = [pltpu.with_memory_space_constraint(x, pltpu.HBM) for x in args]
    shapes = [s if hasattr(s, "dtype") else jax.ShapeDtypeStruct(s, f32) for s in outs]
    scratch = [s if hasattr(s, "memory_space") or hasattr(s, "dtype") else pltpu.VMEM(s, f32) for s in scratch]
    return pl.pallas_call(
        body,
        out_shape=shapes,
        in_specs=[pl.BlockSpec(memory_space=space)] * len(args),
        out_specs=[VM] * len(shapes),
        scratch_shapes=scratch,
        cost_estimate=pl.CostEstimate(
            flops=flops, bytes_accessed=2000000, transcendentals=trans
        ),
        compiler_params=pltpu.CompilerParams(vmem_limit_bytes=40 * 1024 * 1024),
    )(*args)


def shift(x, axis, step):
    n = lax.axis_size(axis)
    return lax.ppermute(x, axis, [(i, (i + step) % n) for i in range(n)])


def both_ways(up, dn, axis, even):
    n = lax.axis_size(axis)
    in_pair = lax.ppermute(jnp.where(even, up, dn), axis, [(i, i ^ 1) for i in range(n)])
    across = lax.ppermute(
        jnp.where(even, dn, up), axis, [(i, (i + 1 if i % 2 else i - 1) % n) for i in range(n)]
    )
    return jnp.where(even, across, in_pair), jnp.where(even, in_pair, across)


def place(d):
    s, c = d // 16, d % 16
    return s // 8, (s // 2) % 4, s % 2, c // 4, c % 4


def together(fixed):
    groups = {}
    for d in range(256):
        groups.setdefault(tuple(place(d)[i] for i in fixed), []).append(d)
    return [groups[k] for k in sorted(groups)]


def send_to_all(x, groups):
    n = len(groups[0])
    y = jnp.broadcast_to(x[None], (n,) + x.shape)
    return lax.all_to_all(y, ("sub", "col"), 0, 0, axis_index_groups=groups, tiled=True)


SWAP = [(d, d ^ 16) for d in range(256)]


def grid_is_whole():
    return (lax.axis_size("sub"), lax.axis_size("col")) == (16, 16)


def even_at(axis):
    return lax.axis_index(axis) % 2 == 0


def chip_sum(x, core):
    low, high = x[:24], x[24:]
    mine = jnp.where(core, low, high)
    return mine + lax.ppermute(jnp.where(core, high, low), ("sub", "col"), SWAP)


def plane_sum(x):
    return send_to_all(x, together((0, 2, 3))).sum(0)


def rest_sum(x, core):
    x = send_to_all(x, together((1, 2, 4))).sum(0)
    other = lax.ppermute(x, ("sub", "col"), SWAP)
    return jnp.where(core, x, other), jnp.where(core, other, x)


def on_device(
    initial_state,
    state_cotangent,
    element_order,
    element_weight,
    element_diffusivity,
    in_weight,
    in_bias,
    mid_weight,
    mid_bias,
    out_weight,
    out_bias,
):
    flags = (even_at("sub"), even_at("col"), element_weight)
    even_s, even_c, element_weight = lax.optimization_barrier(flags)
    hot = jax.ShapeDtypeStruct((128, 128), bf16)
    wide = jax.ShapeDtypeStruct((256, 8192), bf16)
    khot = jax.ShapeDtypeStruct((64, 192), bf16)

    def in_device(w, rp, rm, n):
        m = 10 if n == 10 else 11
        return call(
            lambda *r: xy_body(n, *r), [(n, 3, 2, 8, 128), (m, 8, 128), (m, 8, 128)], [w, rp, rm]
        )

    def faces(w, up, dn, n):
        w, yu, yd = in_device(w, *both_ways(up, dn, "sub", even_s), n)
        yl, yr = both_ways(yu, yd, "col", even_c)
        return w, yl, yr

    w, up, dn, mk, g, kmat = call(
        start_body,
        [(12, 48, 128), (18, 8, 128), (18, 8, 128), (16, 128), hot, khot],
        [
            initial_state,
            state_cotangent,
            element_order,
            element_weight.reshape(1, 128),
            element_diffusivity.reshape(1, 128),
            jnp.asarray(stiffness_matrix()),
        ],
        [(F, 64, 128), (F, 64, 128), pltpu.VMEM((1, 128), jnp.int32), (1, 128), (1, 128)]
        + [(64, 64)]
        + [pltpu.SemaphoreType.DMA((6,))],
        space=pltpu.HBM,
    )
    (pw,) = call(
        prepare_body,
        [jax.ShapeDtypeStruct((272, 256), bf16)],
        [
            in_weight.T,
            in_bias.reshape(1, 64),
            mid_weight,
            mid_bias.reshape(1, 64),
            out_weight,
            out_bias.reshape(1, 5),
        ],
        [(5, 64), (1, 64), (64, 64), (1, 64), (5, 64), (1, 5), pltpu.SemaphoreType.DMA((6,))],
        flops=2000000,
        space=pltpu.HBM,
    )
    w, yl, yr = faces(w, up, dn, 12)
    pw, yl, yr = lax.optimization_barrier((pw, yl, yr))
    ten = [(10, 48, 128), (15, 8, 128), (15, 8, 128)]
    sa, im, w, up, dn = call(
        state_body, [(10, 64, 128), (64, 128)] + ten, [w, yl, yr, mk, kmat]
    )
    c0, x0, hh0, t0 = call(
        closure_body,
        [(F, 64, 128), (512, 128), wide, (128, 8192)],
        [sa, pw],
        [(512, 128)],
        flops=300000000,
        trans=1000000,
    )
    w, yl, yr = faces(w, up, dn, 10)
    part, m1, w, up, dn, x1, c1, hh1, dd1 = call(
        second_body,
        [(10, 64, 128), (F, 64, 128)] + ten + [(512, 128), (512, 128), wide, wide],
        [w, yl, yr, mk, im, sa, c0, pw, kmat],
        [(512, 128)] * 2,
        flops=900000000,
        trans=1000000,
    )
    back, gw, gb = call(
        first_body,
        [(F, 64, 128), (384, 160), (8, 128)],
        [x0, m1, hh0, t0, pw],
        [(512, 128)] * 2,
        flops=600000000,
    )
    rp, rm = both_ways(up, dn, "sub", even_s)
    gw, rp, rm = lax.optimization_barrier((gw, rp, rm))
    (pay,) = call(grads_body, [(48, 128)], [x1, c1, hh1, dd1, gw, gb], flops=300000000)
    w, yu, yd = in_device(w, rp, rm, 10)
    if grid_is_whole():
        pay = chip_sum(pay, even_s)
        pay, yu, yd = lax.optimization_barrier((pay, yu, yd))
        yl, yr = both_ways(yu, yd, "col", even_c)
        out_state, out_adj = call(
            finish_body,
            [(F, 64, 128), (F, 64, 128)],
            [w, yl, yr, mk, im, part, back, g],
            flops=20000000,
        )
        pay = plane_sum(pay)
        pay, out_state, out_adj = lax.optimization_barrier((pay, out_state, out_adj))
        terms = list(rest_sum(pay, even_s))
    else:
        yl, yr = both_ways(yu, yd, "col", even_c)
        pay = lax.psum(pay, ("sub", "col"))
        out_state, out_adj = call(
            finish_body,
            [(F, 64, 128), (F, 64, 128)],
            [w, yl, yr, mk, im, part, back, g],
            flops=20000000,
        )
        terms = [pay[:24], pay[24:]]
    gw1, gb1, gw2, gb2, gwo, gbo = call(
        output_body, [(5, 64), (1, 64), (64, 64), (1, 64), (5, 64), (1, 5)], terms
    )
    return (
        out_state,
        out_adj,
        gw1.T,
        gb1.reshape(64),
        gw2,
        gb2.reshape(64),
        gwo,
        gbo.reshape(5),
    )


def solution(mesh):
    split = P(None, None, ("sub", "col"))
    placed = (split, split, P(("sub", "col"), None), P(("sub", "col")), P(("sub", "col")))
    return jax.shard_map(
        on_device,
        mesh=mesh,
        in_specs=placed + (P(),) * 6,
        out_specs=(split, split) + (P(),) * 6,
        check_vma=False,
    )
```

```python
import math

import jax
import jax.numpy as jnp
import numpy as np
from jax import lax
from jax.experimental import pallas as pl
from jax.experimental.pallas import tpu as pltpu
from jax.sharding import PartitionSpec as P

F = 5
STEP = 0.05
CH = 32
NW = CH * 128
f32, bf16 = jnp.float32, jnp.bfloat16
VM = pl.BlockSpec(memory_space=pltpu.VMEM)


def stiffness_matrix():
    at = [-1.0, -math.sqrt(0.2), math.sqrt(0.2), 1.0]
    w = np.array([1.0 / 6.0, 5.0 / 6.0, 5.0 / 6.0, 1.0 / 6.0])
    prods = [np.prod([at[r] - at[p] for p in range(4) if p != r]) for r in range(4)]
    d = np.zeros((4, 4))
    for r in range(4):
        for c in range(4):
            if r == c:
                d[r, c] = sum(1.0 / (at[r] - at[p]) for p in range(4) if p != r)
            else:
                d[r, c] = prods[r] / (prods[c] * (at[r] - at[c]))
    s = d.T @ np.diag(w) @ d
    m = np.diag(w)
    k = np.kron(m, np.kron(s, m)) + np.kron(m, np.kron(m, s)) + np.kron(s, np.kron(m, m))
    return k.astype(np.float32)


def iota(shape, dim):
    return lax.broadcasted_iota(jnp.int32, shape, dim)


def next_k(x):
    ax = x.ndim - 1
    lane = iota(x.shape, ax) & 63
    return jnp.where(lane == 63, pltpu.roll(x, 63, ax), pltpu.roll(x, 127, ax))


def prev_k(x):
    ax = x.ndim - 1
    lane = iota(x.shape, ax) & 63
    return jnp.where(lane == 0, pltpu.roll(x, 65, ax), pltpu.roll(x, 1, ax))


def zsum(v):
    n = v.shape[0]
    top = v[:, 48:64] + next_k(v[:, 0:16])
    return jnp.concatenate([v[:, 16:48], top], axis=1)


def zfill(w):
    return jnp.concatenate([prev_k(w[:, 32:48]), w], axis=1)


def sroll(x, s):
    return pltpu.roll(x, s % 8, x.ndim - 2) if s % 8 else x


def xpack(w):
    n = w.shape[0]
    h = n // 2
    t = w.reshape(n, 3, 2, 8, 128)
    v0, v1 = t[:, :, 0].reshape(n * 3, 8, 128), t[:, :, 1].reshape(n * 3, 8, 128)
    low = iota((h * 3, 8, 128), 1) < 4
    up = jnp.where(low, sroll(v1[: h * 3], 4), v1[h * 3 :])
    dn = jnp.where(low, v0[: h * 3], sroll(v0[h * 3 :], 4))
    return up, dn


def xadd(w, rp, rm):
    n = w.shape[0]
    h = n // 2
    t = w.reshape(n, 3, 2, 8, 128)
    v0, v1 = t[:, :, 0].reshape(n * 3, 8, 128), t[:, :, 1].reshape(n * 3, 8, 128)
    low = iota((h * 3, 8, 128), 1) < 4
    zero = jnp.zeros_like(rp)
    a0 = jnp.concatenate([jnp.where(low, rp, zero), jnp.where(low, sroll(rp, 4), zero)], axis=0)
    a1 = jnp.concatenate([jnp.where(low, zero, sroll(rm, 4)), jnp.where(low, zero, rm)], axis=0)
    v0, v1 = v0 + a0, v1 + a1
    return v0, v1


def ylocal(v):
    b = iota(v.shape, 1) & 3
    left = iota(v.shape, 2) < 64
    d = jnp.where(b == 0, sroll(v, 5), sroll(v, 3))
    d = pltpu.roll(d, 64, 2)
    zero = jnp.zeros_like(v)
    here = ((b == 0) & (~left)) | ((b == 3) & left)
    out = ((b == 0) & left) | ((b == 3) & (~left))
    return v + jnp.where(here, d, zero), jnp.where(out, d, zero)


def xy_body(n, w_ref, rp_ref, rm_ref, wo_ref, yu_ref, yd_ref):
    ys = []
    w = w_ref[...]
    v0, v1 = xadd(w, rp_ref[...], rm_ref[...])
    for part, v in enumerate((v0, v1)):
        v, e = ylocal(v)
        wo_ref[:, :, part] = v.reshape(n, 3, 8, 128)
        e = e.reshape(n, 3, 8, 128)
        ys.append(e[:, 0] + sroll(e[:, 1], 1) + sroll(e[:, 2], 2))
    left = iota((n, 8, 128), 2) < 64
    m = yu_ref.shape[0]
    yu_ref[...] = jnp.where(left, ys[0], pltpu.roll(ys[1], 64, 2))[:m]
    yd_ref[...] = jnp.where(left, pltpu.roll(ys[0], 64, 2), ys[1])[:m]


def yadd(w, yl, yr):
    m = yl.shape[0]
    left = iota((m, 8, 128), 2) < 64
    b = iota((m, 8, 128), 1) & 3
    use = ((b == 0) & left) | ((b == 3) & (~left))
    zs = (
        jnp.where(left, yl, pltpu.roll(yr, 64, 2)),
        jnp.where(left, pltpu.roll(yl, 64, 2), yr),
    )
    rows = []
    for q in range(3):
        for part, z in enumerate(zs):
            rows.append(w[:m, q, part] + jnp.where(use, sroll(z, -q), jnp.zeros_like(z)))
    return jnp.concatenate(rows, axis=1)


def one_hot(order):
    row = jnp.broadcast_to(order, (128, 128))
    return jnp.where(row == iota((128, 128), 0), 1.0, 0.0).astype(bf16)


def split3(x):
    h = x.astype(bf16)
    r = x - h.astype(f32)
    m = r.astype(bf16)
    l = (r - m.astype(f32)).astype(bf16)
    return h, m, l


def permute_nt(x, g):
    dims = (((1,), (1,)), ((), ()))
    h, m, l = (lax.dot_general(p, g, dims, preferred_element_type=f32) for p in split3(x))
    return h + m + l


def permute_nn(x, g):
    h, m, l = (jnp.dot(p, g, preferred_element_type=f32) for p in split3(x))
    return h + m + l


def quad(shape):
    r = iota(shape, 0)
    w = 1.0
    for i in (r >> 4, (r >> 2) & 3, r & 3):
        w = w * jnp.where((i == 0) | (i == 3), 1.0 / 6.0, 5.0 / 6.0)
    return w


def fetch(srcs, dsts, sems):
    copies = [pltpu.make_async_copy(a, b, sems.at[i]) for i, (a, b) in enumerate(zip(srcs, dsts))]
    for c in copies:
        c.start()
    for c in copies:
        c.wait()


def start_body(
    s_in, c_in, o_in, ew_in, ed_in, k_in, w_ref, up_ref, dn_ref, mk_ref, g_ref, k_ref, *scratch
):
    s_ref, c_ref, o_ref, ew_ref, ed_ref, kf_ref, sems = scratch
    fetch((s_in, c_in, o_in, ew_in, ed_in, k_in), scratch[:6], sems)
    kh, kl = two(kf_ref[...])
    k_ref[...] = jnp.concatenate([kh, kh, kl], axis=1)
    g = one_hot(o_ref[...])
    g_ref[...] = g
    rows = []
    for ref in (s_ref, c_ref):
        for f in range(F):
            for q in range(4):
                rows.append(ref[f, pl.ds(q, 16, stride=4), :])
    el = jnp.concatenate(
        [jnp.broadcast_to(ew_ref[...], (8, 128)), jnp.broadcast_to(ed_ref[...], (8, 128))], axis=0
    )
    x = permute_nt(jnp.concatenate(rows + [el], axis=0), g)
    mass = quad((64, 128)) * x[640:641]
    mk_ref[...] = x[640:656]
    s = x[:320].reshape(F, 64, 128) * mass[None]
    c = x[320:640].reshape(F, 64, 128)
    v = jnp.concatenate([s, mass[None], c, jnp.zeros((1, 64, 128), f32)], axis=0)
    w = zsum(v)
    w_ref[...] = w
    up_ref[...], dn_ref[...] = xpack(w)


def stiffness(v, kmat, kappa):
    n = v.shape[0]
    x = jnp.concatenate([v[i] for i in range(n)], axis=1)
    h = x.astype(bf16)
    l = (x - h.astype(f32)).astype(bf16)
    y = jnp.dot(kmat, jnp.concatenate([h, l, h], axis=0), preferred_element_type=f32)
    return jnp.stack([y[:, i * 128 : (i + 1) * 128] * kappa for i in range(n)], axis=0)


def state_body(w_ref, yl_ref, yr_ref, mk_ref, k_ref, sa_ref, im_ref, w2_ref, up_ref, dn_ref):
    v = zfill(yadd(w_ref[...], yl_ref[...], yr_ref[...]))
    im = 1.0 / v[F]
    im_ref[...] = im
    sa = jnp.concatenate([v[:F], v[F + 1 : 2 * F + 1]], axis=0) * im[None]
    sa_ref[...] = sa
    w = zsum(stiffness(sa, k_ref[...], mk_ref[8:9]))
    w2_ref[...] = w
    up_ref[...], dn_ref[...] = xpack(w)


def prepare_body(w1_in, b1_in, w2_in, b2_in, wo_in, bo_in, p_ref, *scratch):
    fetch((w1_in, b1_in, w2_in, b2_in, wo_in, bo_in), scratch[:6], scratch[6])
    w1, b1, w2, b2, wo, bo = (r[...] for r in scratch[:6])
    z = jnp.zeros((64, 64), f32)
    pad3 = jnp.zeros((3, 64), f32)
    w1b = jnp.concatenate([w1, b1, jnp.zeros((2, 64), f32)], axis=0)
    w1p = jnp.concatenate([w1, pad3], axis=0)
    wop = jnp.concatenate([wo, pad3], axis=0)

    def columns(parts, rows):
        if rows < 256:
            parts = parts + [jnp.zeros((256 - rows, 64), f32)]
        return jnp.concatenate(parts, axis=0).T

    l2 = columns([w2.T] * 3 + [jnp.broadcast_to(b2, (8, 64))], 200)
    l2t = columns([w2] * 3, 192)
    l1 = columns([w1b] * 4, 32)
    lot = columns([wop] * 4, 32)
    both = jnp.concatenate([wop, w1p], axis=0)
    diag = iota((16, 5), 0) == iota((16, 5), 1)
    bias = jnp.sum(jnp.where(diag, jnp.broadcast_to(bo, (16, 5)), 0.0), axis=1, keepdims=True)
    bias = jnp.where(iota((16, 64), 1) < 2, jnp.broadcast_to(bias, (16, 64)), z[:16])
    small = jnp.concatenate([both, both, both, bias], axis=1)

    def parts(p, high):
        h = p.astype(bf16).astype(f32)
        return jnp.where(high, h, p - h).astype(bf16)

    col = iota((128, 256), 1)
    high = (col < 128) | (col == 192)
    p_ref[0:128] = parts(jnp.concatenate([l2, l2t], axis=0), high)
    p_ref[128:256] = parts(jnp.concatenate([l1, lot], axis=0), col < 16)
    p_ref[256:272] = parts(small, high[:16])


def weights(p_ref):
    return dict(
        l2=p_ref[0:64, 0:208],
        l2t=p_ref[64:128, 0:192],
        l1=p_ref[128:192, 0:32],
        lot=p_ref[192:256, 0:32],
        lo=p_ref[256:272, 0:208],
    )


def two(x):
    h = x.astype(bf16)
    return h, (x - h.astype(f32)).astype(bf16)


def stack8(x):
    h = x.astype(bf16).astype(f32)
    l = x - h
    return jnp.concatenate([h, l, h, l], axis=0).astype(bf16)


def mm(a, b):
    return jnp.dot(a, b, preferred_element_type=f32)


def nt(a, b):
    return lax.dot_general(a, b, (((1,), (1,)), ((), ())), preferred_element_type=f32)


def load8(ref, n0, ch=CH):
    return jnp.concatenate([ref[pl.ds(n0 + i, 8, stride=64), :] for i in range(ch)], axis=1)


def store8(ref, n0, x):
    for i in range(x.shape[1] // 128):
        ref[pl.ds(n0 + i, 8, stride=64), :] = x[:, i * 128 : (i + 1) * 128]


def put_fields(ref, x, ones):
    ref[0 : F * 64, :] = x.reshape(F * 64, 128)
    ref[F * 64 : F * 64 + 64, :] = jnp.full((64, 128), 1.0 if ones else 0.0, f32)
    ref[F * 64 + 64 :, :] = jnp.zeros((128, 128), f32)


def bias_rows():
    return jnp.where(iota((16, NW), 0) < 2, 1.0, 0.0).astype(bf16)


def forward(x8, w, ones):
    h1 = jnp.tanh(mm(w["l1"], stack8(x8)))
    h1h, h1l = two(h1)
    h2 = jnp.tanh(mm(w["l2"], jnp.concatenate([h1h, h1l, h1h, ones], axis=0)))
    h2h, h2l = two(h2)
    return h1, h1h, h1l, h2, h2h, h2l


def lanes_of(i):
    return pl.ds(pl.multiple_of(i * NW, NW), NW)


def put4(ref, i, parts):
    for k, p in enumerate(parts):
        ref[k * 64 : k * 64 + 64, lanes_of(i)] = p


def closure_body(sa_ref, p_ref, c_ref, x_ref, hh_ref, t_ref, o_ref):
    put_fields(x_ref, sa_ref[0:F], True)
    w = weights(p_ref)
    ones = bias_rows()

    def chunk(i, carry):
        n0 = i * CH
        h1, h1h, h1l, h2, h2h, h2l = forward(load8(x_ref, n0), w, ones)
        put4(hh_ref, i, (h1h, h1l, h2h, h2l))
        t_ref[0:64, lanes_of(i)] = 1.0 - h1 * h1
        t_ref[64:128, lanes_of(i)] = 1.0 - h2 * h2
        out = mm(w["lo"], jnp.concatenate([h2h, h2l, h2h, ones], axis=0))
        store8(o_ref, n0, out[0:8])
        return carry

    lax.fori_loop(0, 64 // CH, chunk, 0)
    c_ref[...] = o_ref[0 : F * 64].reshape(F, 64, 128)


def backward(c8, t1, t2, w):
    d2h, d2l = two(mm(w["lot"], stack8(c8)) * t2)
    d1h, d1l = two(mm(w["l2t"], jnp.concatenate([d2h, d2l, d2h], axis=0)) * t1)
    back = mm(w["lo"][:, 0:192], jnp.concatenate([d1h, d1l, d1h], axis=0))[8:16]
    return back, d2h, d2l, d1h, d1l


def stack2(x):
    h = x.astype(bf16).astype(f32)
    return jnp.concatenate([h, x - h], axis=0).astype(bf16)


def add_grads(acc, x8, c8, h1, h2, d2, d1):
    gw, gb = acc
    right = jnp.concatenate([h1, stack2(x8), stack2(c8)], axis=0)
    gw = gw + nt(jnp.concatenate([d2, d1, h2], axis=0), right)
    for i in range(c8.shape[1] // 128):
        gb = gb + c8[:, i * 128 : (i + 1) * 128]
    return gw, gb


def no_grads():
    return jnp.zeros((384, 160), f32), jnp.zeros((8, 128), f32)


def second_body(
    w_ref, yl_ref, yr_ref, mk_ref, im_ref, sa_ref, c0_ref, p_ref, k_ref,
    part_ref, m1_ref, w2_ref, up_ref, dn_ref, x_ref, c_ref, ha_ref, hb_ref, dd_ref,
    b_ref,
):
    im = im_ref[...] * STEP
    mass = quad((64, 128)) * mk_ref[0:1]
    v = zfill(yadd(w_ref[...], yl_ref[...], yr_ref[...])) * im[None]
    a2 = sa_ref[F:]
    s1 = sa_ref[0:F] + STEP * c0_ref[...] - v[0:F]
    put_fields(x_ref, s1, True)
    put_fields(c_ref, a2 * mass[None], False)
    w = weights(p_ref)
    ones = bias_rows()

    def chunk(i, carry):
        n0 = i * CH
        h1, h1h, h1l, h2, h2h, h2l = forward(load8(x_ref, n0), w, ones)
        put4(ha_ref, i, (h1h, h1l))
        put4(hb_ref, i, (h2h, h2l))
        back, *ds = backward(load8(c_ref, n0), 1.0 - h1 * h1, 1.0 - h2 * h2, w)
        put4(dd_ref, i, ds)
        store8(b_ref, n0, back)
        return carry

    lax.fori_loop(0, 64 // CH, chunk, 0)
    back = b_ref[0 : F * 64].reshape(F, 64, 128)
    a1 = a2 - v[F:] + (STEP / mass)[None] * back
    m1_ref[...] = a1 * mass[None]
    part_ref[0:F] = s1
    part_ref[F:] = a1
    wz = zsum(stiffness(jnp.concatenate([s1, a1], axis=0), k_ref[...], mk_ref[8:9]))
    w2_ref[...] = wz
    up_ref[...], dn_ref[...] = xpack(wz)


def first_body(x_ref, m1_ref, hh_ref, t_ref, p_ref, back_ref, gw_ref, gb_ref, c_ref, b_ref):
    put_fields(c_ref, m1_ref[...], False)
    w = weights(p_ref)

    c8 = load8(c_ref, 0, 64)
    back, d2h, d2l, d1h, d1l = backward(c8, t_ref[0:64], t_ref[64:128], w)
    store8(b_ref, 0, back)
    gw_ref[...], gb_ref[...] = add_grads(
        no_grads(), load8(x_ref, 0, 64), c8, hh_ref[0:128], hh_ref[128:256],
        jnp.concatenate([d2h, d2l], axis=0), jnp.concatenate([d1h, d1l], axis=0),
    )
    back_ref[...] = b_ref[0 : F * 64].reshape(F, 64, 128)


def grads_body(x_ref, c_ref, ha_ref, hb_ref, dd_ref, gw_ref, gb_ref, pay_ref):
    g, gb = add_grads(
        (gw_ref[...], gb_ref[...]), load8(x_ref, 0, 64), load8(c_ref, 0, 64),
        ha_ref[...], hb_ref[...], dd_ref[0:128], dd_ref[128:256],
    )

    def fold(t):
        return t + pltpu.roll(t, 64, 1)

    gw = fold(g[0:64, 0:128] + g[64:128, 0:128])
    gs = g[:, 128:160].T
    gx2 = fold(gs[0:8, 0:128] + gs[8:16, 0:128])
    gx1 = fold(gs[0:8, 128:256] + gs[8:16, 128:256])
    gc = fold(gs[16:24, 256:384] + gs[24:32, 256:384])
    gbs = jnp.broadcast_to(jnp.sum(gb, axis=1, keepdims=True), (8, 128))
    left = iota((32, 128), 1) < 64
    scale = STEP / 256.0
    pay_ref[0:32] = jnp.where(left, gw[0:32], gw[32:64]) * scale
    pay_ref[32:40] = jnp.where(left[:8], gx1, gx2) * scale
    pay_ref[40:48] = jnp.where(left[:8], gc, gbs) * scale


def finish_body(
    w_ref, yl_ref, yr_ref, mk_ref, im_ref, part_ref, back_ref, g_ref, hb_ref, p_ref, s_ref, a_ref, o_ref
):
    im = im_ref[...] * STEP
    mass = quad((64, 128)) * mk_ref[0:1]
    v = zfill(yadd(w_ref[...], yl_ref[...], yr_ref[...])) * im[None]
    w = weights(p_ref)
    ones = bias_rows()

    def chunk(i, carry):
        at = lanes_of(i)
        h2h, h2l = hb_ref[0:64, at], hb_ref[64:128, at]
        out = mm(w["lo"], jnp.concatenate([h2h, h2l, h2h, ones], axis=0))
        store8(o_ref, i * CH, out[0:8])
        return carry

    lax.fori_loop(0, 64 // CH, chunk, 0)
    forcing = o_ref[0 : F * 64].reshape(F, 64, 128)
    s2 = part_ref[0:F] + STEP * forcing - v[0:F]
    a0 = (part_ref[F:] - v[F:]) * mass[None] + STEP * back_ref[...]
    x = jnp.concatenate([s2.reshape(320, 128), a0.reshape(320, 128)], axis=0)
    y = permute_nn(x, g_ref[...])
    for i, ref in enumerate((s_ref, a_ref)):
        for f in range(F):
            for q in range(4):
                r = (i * F + f) * 64 + q * 16
                ref[f, pl.ds(q, 16, stride=4), :] = y[r : r + 16]


def output_body(l_ref, h_ref, gw1_ref, gb1_ref, gw2_ref, gb2_ref, gwo_ref, gbo_ref):
    pay = jnp.concatenate([l_ref[...], h_ref[...]], axis=0)
    gw2_ref[0:32] = pay[0:32, 0:64]
    other = pltpu.roll(pay, 64, 1)
    gw2_ref[32:64] = other[0:32, 0:64]
    gw1_ref[...] = pay[32:37, 0:64]
    gb1_ref[...] = pay[37:38, 0:64]
    gb2_ref[...] = other[37:38, 0:64]
    gwo_ref[...] = pay[40:45, 0:64]
    diag = iota((8, 5), 0) == iota((8, 5), 1)
    gbo_ref[...] = jnp.sum(jnp.where(diag, other[40:48, 0:5], 0.0), axis=0, keepdims=True)


def call(body, outs, args, scratch=(), flops=0, trans=0, space=pltpu.VMEM):
    if space == pltpu.HBM:
        args = [pltpu.with_memory_space_constraint(x, pltpu.HBM) for x in args]
    shapes = [s if hasattr(s, "dtype") else jax.ShapeDtypeStruct(s, f32) for s in outs]
    scratch = [s if hasattr(s, "memory_space") or hasattr(s, "dtype") else pltpu.VMEM(s, f32) for s in scratch]
    return pl.pallas_call(
        body,
        out_shape=shapes,
        in_specs=[pl.BlockSpec(memory_space=space)] * len(args),
        out_specs=[VM] * len(shapes),
        scratch_shapes=scratch,
        cost_estimate=pl.CostEstimate(
            flops=flops, bytes_accessed=2000000, transcendentals=trans
        ),
        compiler_params=pltpu.CompilerParams(vmem_limit_bytes=40 * 1024 * 1024),
    )(*args)


def shift(x, axis, step):
    n = lax.axis_size(axis)
    return lax.ppermute(x, axis, [(i, (i + step) % n) for i in range(n)])


def both_ways(up, dn, axis, even):
    n = lax.axis_size(axis)
    in_pair = lax.ppermute(jnp.where(even, up, dn), axis, [(i, i ^ 1) for i in range(n)])
    across = lax.ppermute(
        jnp.where(even, dn, up), axis, [(i, (i + 1 if i % 2 else i - 1) % n) for i in range(n)]
    )
    return jnp.where(even, across, in_pair), jnp.where(even, in_pair, across)


def place(d):
    s, c = d // 16, d % 16
    return s // 8, (s // 2) % 4, s % 2, c // 4, c % 4


def together(fixed):
    groups = {}
    for d in range(256):
        groups.setdefault(tuple(place(d)[i] for i in fixed), []).append(d)
    return [groups[k] for k in sorted(groups)]


def send_to_all(x, groups):
    n = len(groups[0])
    y = jnp.broadcast_to(x[None], (n,) + x.shape)
    return lax.all_to_all(y, ("sub", "col"), 0, 0, axis_index_groups=groups, tiled=True)


SWAP = [(d, d ^ 16) for d in range(256)]


def grid_is_whole():
    return (lax.axis_size("sub"), lax.axis_size("col")) == (16, 16)


def even_at(axis):
    return lax.axis_index(axis) % 2 == 0


def chip_sum(x, core):
    low, high = x[:24], x[24:]
    mine = jnp.where(core, low, high)
    return mine + lax.ppermute(jnp.where(core, high, low), ("sub", "col"), SWAP)


def plane_sum(x):
    return send_to_all(x, together((0, 2, 3))).sum(0)


def rest_sum(x, core):
    x = send_to_all(x, together((1, 2, 4))).sum(0)
    other = lax.ppermute(x, ("sub", "col"), SWAP)
    return jnp.where(core, x, other), jnp.where(core, other, x)


def on_device(
    initial_state,
    state_cotangent,
    element_order,
    element_weight,
    element_diffusivity,
    in_weight,
    in_bias,
    mid_weight,
    mid_bias,
    out_weight,
    out_bias,
):
    flags = (even_at("sub"), even_at("col"), element_weight)
    even_s, even_c, element_weight = lax.optimization_barrier(flags)
    hot = jax.ShapeDtypeStruct((128, 128), bf16)
    half = jax.ShapeDtypeStruct((128, 8192), bf16)
    wide = jax.ShapeDtypeStruct((256, 8192), bf16)
    khot = jax.ShapeDtypeStruct((64, 192), bf16)

    def in_device(w, rp, rm, n):
        m = 10 if n == 10 else 11
        return call(
            lambda *r: xy_body(n, *r), [(n, 3, 2, 8, 128), (m, 8, 128), (m, 8, 128)], [w, rp, rm]
        )

    def faces(w, up, dn, n):
        w, yu, yd = in_device(w, *both_ways(up, dn, "sub", even_s), n)
        yl, yr = both_ways(yu, yd, "col", even_c)
        return w, yl, yr

    w, up, dn, mk, g, kmat = call(
        start_body,
        [(12, 48, 128), (18, 8, 128), (18, 8, 128), (16, 128), hot, khot],
        [
            initial_state,
            state_cotangent,
            element_order,
            element_weight.reshape(1, 128),
            element_diffusivity.reshape(1, 128),
            jnp.asarray(stiffness_matrix()),
        ],
        [(F, 64, 128), (F, 64, 128), pltpu.VMEM((1, 128), jnp.int32), (1, 128), (1, 128)]
        + [(64, 64)]
        + [pltpu.SemaphoreType.DMA((6,))],
        space=pltpu.HBM,
    )
    (pw,) = call(
        prepare_body,
        [jax.ShapeDtypeStruct((272, 256), bf16)],
        [
            in_weight.T,
            in_bias.reshape(1, 64),
            mid_weight,
            mid_bias.reshape(1, 64),
            out_weight,
            out_bias.reshape(1, 5),
        ],
        [(5, 64), (1, 64), (64, 64), (1, 64), (5, 64), (1, 5), pltpu.SemaphoreType.DMA((6,))],
        flops=2000000,
        space=pltpu.HBM,
    )
    w, yl, yr = faces(w, up, dn, 12)
    pw, yl, yr = lax.optimization_barrier((pw, yl, yr))
    ten = [(10, 48, 128), (15, 8, 128), (15, 8, 128)]
    sa, im, w, up, dn = call(
        state_body, [(10, 64, 128), (64, 128)] + ten, [w, yl, yr, mk, kmat]
    )
    c0, x0, hh0, t0 = call(
        closure_body,
        [(F, 64, 128), (512, 128), wide, (128, 8192)],
        [sa, pw],
        [(512, 128)],
        flops=300000000,
        trans=1000000,
    )
    w, yl, yr = faces(w, up, dn, 10)
    part, m1, w, up, dn, x1, c1, ha1, hb1, dd1 = call(
        second_body,
        [(10, 64, 128), (F, 64, 128)] + ten + [(512, 128), (512, 128), half, half, wide],
        [w, yl, yr, mk, im, sa, c0, pw, kmat],
        [(512, 128)],
        flops=900000000,
        trans=1000000,
    )
    back, gw, gb = call(
        first_body,
        [(F, 64, 128), (384, 160), (8, 128)],
        [x0, m1, hh0, t0, pw],
        [(512, 128)] * 2,
        flops=600000000,
    )
    rp, rm = both_ways(up, dn, "sub", even_s)
    gw, rp, rm = lax.optimization_barrier((gw, rp, rm))
    (pay,) = call(grads_body, [(48, 128)], [x1, c1, ha1, hb1, dd1, gw, gb], flops=300000000)
    w, yu, yd = in_device(w, rp, rm, 10)
    if grid_is_whole():
        pay = chip_sum(pay, even_s)
        pay, yu, yd = lax.optimization_barrier((pay, yu, yd))
        yl, yr = both_ways(yu, yd, "col", even_c)
        out_state, out_adj = call(
            finish_body,
            [(F, 64, 128), (F, 64, 128)],
            [w, yl, yr, mk, im, part, back, g, hb1, pw],
            [(512, 128)],
            flops=20000000,
        )
        pay = plane_sum(pay)
        pay, out_state, out_adj = lax.optimization_barrier((pay, out_state, out_adj))
        terms = list(rest_sum(pay, even_s))
    else:
        yl, yr = both_ways(yu, yd, "col", even_c)
        pay = lax.psum(pay, ("sub", "col"))
        out_state, out_adj = call(
            finish_body,
            [(F, 64, 128), (F, 64, 128)],
            [w, yl, yr, mk, im, part, back, g, hb1, pw],
            [(512, 128)],
            flops=20000000,
        )
        terms = [pay[:24], pay[24:]]
    gw1, gb1, gw2, gb2, gwo, gbo = call(
        output_body, [(5, 64), (1, 64), (64, 64), (1, 64), (5, 64), (1, 5)], terms
    )
    return (
        out_state,
        out_adj,
        gw1.T,
        gb1.reshape(64),
        gw2,
        gb2.reshape(64),
        gwo,
        gbo.reshape(5),
    )


def solution(mesh):
    split = P(None, None, ("sub", "col"))
    placed = (split, split, P(("sub", "col"), None), P(("sub", "col")), P(("sub", "col")))
    return jax.shard_map(
        on_device,
        mesh=mesh,
        in_specs=placed + (P(),) * 6,
        out_specs=(split, split) + (P(),) * 6,
        check_vma=False,
    )
```

```python
import math

import jax
import jax.numpy as jnp
import numpy as np
from jax import lax
from jax.experimental import pallas as pl
from jax.experimental.pallas import tpu as pltpu
from jax.sharding import PartitionSpec as P

F = 5
STEP = 0.05
CH = 32
NW = CH * 128
f32, bf16 = jnp.float32, jnp.bfloat16
VM = pl.BlockSpec(memory_space=pltpu.VMEM)


def stiffness_matrix():
    at = [-1.0, -math.sqrt(0.2), math.sqrt(0.2), 1.0]
    w = np.array([1.0 / 6.0, 5.0 / 6.0, 5.0 / 6.0, 1.0 / 6.0])
    prods = [np.prod([at[r] - at[p] for p in range(4) if p != r]) for r in range(4)]
    d = np.zeros((4, 4))
    for r in range(4):
        for c in range(4):
            if r == c:
                d[r, c] = sum(1.0 / (at[r] - at[p]) for p in range(4) if p != r)
            else:
                d[r, c] = prods[r] / (prods[c] * (at[r] - at[c]))
    s = d.T @ np.diag(w) @ d
    m = np.diag(w)
    k = np.kron(m, np.kron(s, m)) + np.kron(m, np.kron(m, s)) + np.kron(s, np.kron(m, m))
    return k.astype(np.float32)


def iota(shape, dim):
    return lax.broadcasted_iota(jnp.int32, shape, dim)


def next_k(x):
    ax = x.ndim - 1
    lane = iota(x.shape, ax) & 63
    return jnp.where(lane == 63, pltpu.roll(x, 63, ax), pltpu.roll(x, 127, ax))


def prev_k(x):
    ax = x.ndim - 1
    lane = iota(x.shape, ax) & 63
    return jnp.where(lane == 0, pltpu.roll(x, 65, ax), pltpu.roll(x, 1, ax))


def zsum(v):
    n = v.shape[0]
    top = v[:, 48:64] + next_k(v[:, 0:16])
    return jnp.concatenate([v[:, 16:48], top], axis=1)


def zfill(w):
    return jnp.concatenate([prev_k(w[:, 32:48]), w], axis=1)


def sroll(x, s):
    return pltpu.roll(x, s % 8, x.ndim - 2) if s % 8 else x


def xpack(w):
    n = w.shape[0]
    h = n // 2
    t = w.reshape(n, 3, 2, 8, 128)
    v0, v1 = t[:, :, 0].reshape(n * 3, 8, 128), t[:, :, 1].reshape(n * 3, 8, 128)
    low = iota((h * 3, 8, 128), 1) < 4
    up = jnp.where(low, sroll(v1[: h * 3], 4), v1[h * 3 :])
    dn = jnp.where(low, v0[: h * 3], sroll(v0[h * 3 :], 4))
    return up, dn


def xadd(w, rp, rm):
    n = w.shape[0]
    h = n // 2
    t = w.reshape(n, 3, 2, 8, 128)
    v0, v1 = t[:, :, 0].reshape(n * 3, 8, 128), t[:, :, 1].reshape(n * 3, 8, 128)
    low = iota((h * 3, 8, 128), 1) < 4
    zero = jnp.zeros_like(rp)
    a0 = jnp.concatenate([jnp.where(low, rp, zero), jnp.where(low, sroll(rp, 4), zero)], axis=0)
    a1 = jnp.concatenate([jnp.where(low, zero, sroll(rm, 4)), jnp.where(low, zero, rm)], axis=0)
    v0, v1 = v0 + a0, v1 + a1
    return v0, v1


def ylocal(v):
    b = iota(v.shape, 1) & 3
    left = iota(v.shape, 2) < 64
    d = jnp.where(b == 0, sroll(v, 5), sroll(v, 3))
    d = pltpu.roll(d, 64, 2)
    zero = jnp.zeros_like(v)
    here = ((b == 0) & (~left)) | ((b == 3) & left)
    out = ((b == 0) & left) | ((b == 3) & (~left))
    return v + jnp.where(here, d, zero), jnp.where(out, d, zero)


def xy_body(n, w_ref, rp_ref, rm_ref, wo_ref, yu_ref, yd_ref):
    ys = []
    w = w_ref[...]
    v0, v1 = xadd(w, rp_ref[...], rm_ref[...])
    for part, v in enumerate((v0, v1)):
        v, e = ylocal(v)
        wo_ref[:, :, part] = v.reshape(n, 3, 8, 128)
        e = e.reshape(n, 3, 8, 128)
        ys.append(e[:, 0] + sroll(e[:, 1], 1) + sroll(e[:, 2], 2))
    left = iota((n, 8, 128), 2) < 64
    m = yu_ref.shape[0]
    yu_ref[...] = jnp.where(left, ys[0], pltpu.roll(ys[1], 64, 2))[:m]
    yd_ref[...] = jnp.where(left, pltpu.roll(ys[0], 64, 2), ys[1])[:m]


def yadd(w, yl, yr):
    m = yl.shape[0]
    left = iota((m, 8, 128), 2) < 64
    b = iota((m, 8, 128), 1) & 3
    use = ((b == 0) & left) | ((b == 3) & (~left))
    zs = (
        jnp.where(left, yl, pltpu.roll(yr, 64, 2)),
        jnp.where(left, pltpu.roll(yl, 64, 2), yr),
    )
    rows = []
    for q in range(3):
        for part, z in enumerate(zs):
            rows.append(w[:m, q, part] + jnp.where(use, sroll(z, -q), jnp.zeros_like(z)))
    return jnp.concatenate(rows, axis=1)


def one_hot(order):
    row = jnp.broadcast_to(order, (128, 128))
    return jnp.where(row == iota((128, 128), 0), 1.0, 0.0).astype(bf16)


def split3(x):
    h = x.astype(bf16)
    r = x - h.astype(f32)
    m = r.astype(bf16)
    l = (r - m.astype(f32)).astype(bf16)
    return h, m, l


def permute_nt(x, g):
    dims = (((1,), (1,)), ((), ()))
    h, m, l = (lax.dot_general(p, g, dims, preferred_element_type=f32) for p in split3(x))
    return h + m + l


def permute_nn(x, g):
    h, m, l = (jnp.dot(p, g, preferred_element_type=f32) for p in split3(x))
    return h + m + l


def quad(shape):
    r = iota(shape, 0)
    w = 1.0
    for i in (r >> 4, (r >> 2) & 3, r & 3):
        w = w * jnp.where((i == 0) | (i == 3), 1.0 / 6.0, 5.0 / 6.0)
    return w


def fetch(srcs, dsts, sems):
    copies = [pltpu.make_async_copy(a, b, sems.at[i]) for i, (a, b) in enumerate(zip(srcs, dsts))]
    for c in copies:
        c.start()
    for c in copies:
        c.wait()


def start_body(
    s_in, c_in, o_in, ew_in, ed_in, k_in, w_ref, up_ref, dn_ref, mk_ref, g_ref, k_ref, *scratch
):
    s_ref, c_ref, o_ref, ew_ref, ed_ref, kf_ref, sems = scratch
    fetch((s_in, c_in, o_in, ew_in, ed_in, k_in), scratch[:6], sems)
    kh, kl = two(kf_ref[...])
    k_ref[...] = jnp.concatenate([kh, kh, kl], axis=1)
    g = one_hot(o_ref[...])
    g_ref[...] = g
    rows = []
    for ref in (s_ref, c_ref):
        for f in range(F):
            for q in range(4):
                rows.append(ref[f, pl.ds(q, 16, stride=4), :])
    el = jnp.concatenate(
        [jnp.broadcast_to(ew_ref[...], (8, 128)), jnp.broadcast_to(ed_ref[...], (8, 128))], axis=0
    )
    x = permute_nt(jnp.concatenate(rows + [el], axis=0), g)
    mass = quad((64, 128)) * x[640:641]
    mk_ref[...] = x[640:656]
    s = x[:320].reshape(F, 64, 128) * mass[None]
    c = x[320:640].reshape(F, 64, 128)
    v = jnp.concatenate([s, mass[None], c, jnp.zeros((1, 64, 128), f32)], axis=0)
    w = zsum(v)
    w_ref[...] = w
    up_ref[...], dn_ref[...] = xpack(w)


def stiffness(v, kmat, kappa):
    n = v.shape[0]
    x = jnp.concatenate([v[i] for i in range(n)], axis=1)
    h = x.astype(bf16)
    l = (x - h.astype(f32)).astype(bf16)
    y = jnp.dot(kmat, jnp.concatenate([h, l, h], axis=0), preferred_element_type=f32)
    return jnp.stack([y[:, i * 128 : (i + 1) * 128] * kappa for i in range(n)], axis=0)


def state_body(w_ref, yl_ref, yr_ref, mk_ref, k_ref, sa_ref, im_ref, w2_ref, up_ref, dn_ref):
    v = zfill(yadd(w_ref[...], yl_ref[...], yr_ref[...]))
    im = 1.0 / v[F]
    im_ref[...] = im
    sa = jnp.concatenate([v[:F], v[F + 1 : 2 * F + 1]], axis=0) * im[None]
    sa_ref[...] = sa
    w = zsum(stiffness(sa, k_ref[...], mk_ref[8:9]))
    w2_ref[...] = w
    up_ref[...], dn_ref[...] = xpack(w)


def prepare_body(w1_in, b1_in, w2_in, b2_in, wo_in, bo_in, p_ref, *scratch):
    fetch((w1_in, b1_in, w2_in, b2_in, wo_in, bo_in), scratch[:6], scratch[6])
    w1, b1, w2, b2, wo, bo = (r[...] for r in scratch[:6])
    z = jnp.zeros((64, 64), f32)
    pad3 = jnp.zeros((3, 64), f32)
    w1b = jnp.concatenate([w1, b1, jnp.zeros((2, 64), f32)], axis=0)
    w1p = jnp.concatenate([w1, pad3], axis=0)
    wop = jnp.concatenate([wo, pad3], axis=0)

    def columns(parts, rows):
        if rows < 256:
            parts = parts + [jnp.zeros((256 - rows, 64), f32)]
        return jnp.concatenate(parts, axis=0).T

    l2 = columns([w2.T] * 3 + [jnp.broadcast_to(b2, (8, 64))], 200)
    l2t = columns([w2] * 3, 192)
    l1 = columns([w1b] * 4, 32)
    lot = columns([wop] * 4, 32)
    both = jnp.concatenate([wop, w1p], axis=0)
    diag = iota((16, 5), 0) == iota((16, 5), 1)
    bias = jnp.sum(jnp.where(diag, jnp.broadcast_to(bo, (16, 5)), 0.0), axis=1, keepdims=True)
    bias = jnp.where(iota((16, 64), 1) < 2, jnp.broadcast_to(bias, (16, 64)), z[:16])
    small = jnp.concatenate([both, both, both, bias], axis=1)

    def parts(p, high):
        h = p.astype(bf16).astype(f32)
        return jnp.where(high, h, p - h).astype(bf16)

    col = iota((128, 256), 1)
    high = (col < 128) | (col == 192)
    p_ref[0:128] = parts(jnp.concatenate([l2, l2t], axis=0), high)
    p_ref[128:256] = parts(jnp.concatenate([l1, lot], axis=0), col < 16)
    p_ref[256:272] = parts(small, high[:16])


def weights(p_ref):
    return dict(
        l2=p_ref[0:64, 0:208],
        l2t=p_ref[64:128, 0:192],
        l1=p_ref[128:192, 0:32],
        lot=p_ref[192:256, 0:32],
        lo=p_ref[256:272, 0:208],
    )


def two(x):
    h = x.astype(bf16)
    return h, (x - h.astype(f32)).astype(bf16)


def stack8(x):
    h = x.astype(bf16).astype(f32)
    l = x - h
    return jnp.concatenate([h, l, h, l], axis=0).astype(bf16)


def mm(a, b):
    return jnp.dot(a, b, preferred_element_type=f32)


def nt(a, b):
    return lax.dot_general(a, b, (((1,), (1,)), ((), ())), preferred_element_type=f32)


def load8(ref, n0, ch=CH):
    return jnp.concatenate([ref[pl.ds(n0 + i, 8, stride=64), :] for i in range(ch)], axis=1)


def store8(ref, n0, x):
    for i in range(x.shape[1] // 128):
        ref[pl.ds(n0 + i, 8, stride=64), :] = x[:, i * 128 : (i + 1) * 128]


def put_fields(ref, x, ones):
    ref[0 : F * 64, :] = x.reshape(F * 64, 128)
    ref[F * 64 : F * 64 + 64, :] = jnp.full((64, 128), 1.0 if ones else 0.0, f32)
    ref[F * 64 + 64 :, :] = jnp.zeros((128, 128), f32)


def bias_rows():
    return jnp.where(iota((16, NW), 0) < 2, 1.0, 0.0).astype(bf16)


def forward(x8, w, ones):
    h1 = jnp.tanh(mm(w["l1"], stack8(x8)))
    h1h, h1l = two(h1)
    h2 = jnp.tanh(mm(w["l2"], jnp.concatenate([h1h, h1l, h1h, ones], axis=0)))
    h2h, h2l = two(h2)
    return h1, h1h, h1l, h2, h2h, h2l


def lanes_of(i):
    return pl.ds(pl.multiple_of(i * NW, NW), NW)


def put4(ref, i, parts):
    for k, p in enumerate(parts):
        ref[k * 64 : k * 64 + 64, lanes_of(i)] = p


def closure_body(sa_ref, p_ref, c_ref, x_ref, hh_ref, t_ref, o_ref):
    put_fields(x_ref, sa_ref[0:F], True)
    w = weights(p_ref)
    ones = bias_rows()

    def chunk(i, carry):
        n0 = i * CH
        h1, h1h, h1l, h2, h2h, h2l = forward(load8(x_ref, n0), w, ones)
        put4(hh_ref, i, (h1h, h1l, h2h, h2l))
        t_ref[0:64, lanes_of(i)] = 1.0 - h1 * h1
        t_ref[64:128, lanes_of(i)] = 1.0 - h2 * h2
        out = mm(w["lo"], jnp.concatenate([h2h, h2l, h2h, ones], axis=0))
        store8(o_ref, n0, out[0:8])
        return carry

    lax.fori_loop(0, 64 // CH, chunk, 0)
    c_ref[...] = o_ref[0 : F * 64].reshape(F, 64, 128)


def backward(c8, t1, t2, w):
    d2h, d2l = two(mm(w["lot"], stack8(c8)) * t2)
    d1h, d1l = two(mm(w["l2t"], jnp.concatenate([d2h, d2l, d2h], axis=0)) * t1)
    back = mm(w["lo"][:, 0:192], jnp.concatenate([d1h, d1l, d1h], axis=0))[8:16]
    return back, d2h, d2l, d1h, d1l


def stack2(x):
    h = x.astype(bf16).astype(f32)
    return jnp.concatenate([h, x - h], axis=0).astype(bf16)


def add_grads(acc, x8, c8, h1, h2, d2, d1):
    gw, gb = acc
    right = jnp.concatenate([h1, stack2(x8), stack2(c8)], axis=0)
    gw = gw + nt(jnp.concatenate([d2, d1, h2], axis=0), right)
    for i in range(c8.shape[1] // 128):
        gb = gb + c8[:, i * 128 : (i + 1) * 128]
    return gw, gb


def no_grads():
    return jnp.zeros((384, 160), f32), jnp.zeros((8, 128), f32)


def second_body(
    w_ref, yl_ref, yr_ref, mk_ref, im_ref, sa_ref, c0_ref, p_ref, k_ref,
    part_ref, m1_ref, w2_ref, up_ref, dn_ref, x_ref, c_ref, ha_ref, hb_ref, dd_ref,
    b_ref,
):
    im = im_ref[...] * STEP
    mass = quad((64, 128)) * mk_ref[0:1]
    v = zfill(yadd(w_ref[...], yl_ref[...], yr_ref[...])) * im[None]
    a2 = sa_ref[F:]
    s1 = sa_ref[0:F] + STEP * c0_ref[...] - v[0:F]
    put_fields(x_ref, s1, True)
    put_fields(c_ref, a2 * mass[None], False)
    w = weights(p_ref)
    ones = bias_rows()

    def chunk(i, carry):
        n0 = i * CH
        h1, h1h, h1l, h2, h2h, h2l = forward(load8(x_ref, n0), w, ones)
        put4(ha_ref, i, (h1h, h1l))
        put4(hb_ref, i, (h2h, h2l))
        back, *ds = backward(load8(c_ref, n0), 1.0 - h1 * h1, 1.0 - h2 * h2, w)
        put4(dd_ref, i, ds)
        store8(b_ref, n0, back)
        return carry

    lax.fori_loop(0, 64 // CH, chunk, 0)
    back = b_ref[0 : F * 64].reshape(F, 64, 128)
    a1 = a2 - v[F:] + (STEP / mass)[None] * back
    m1_ref[...] = a1 * mass[None]
    part_ref[0:F] = s1
    part_ref[F:] = a1
    wz = zsum(stiffness(jnp.concatenate([s1, a1], axis=0), k_ref[...], mk_ref[8:9]))
    w2_ref[...] = wz
    up_ref[...], dn_ref[...] = xpack(wz)


def first_body(x_ref, m1_ref, hh_ref, t_ref, p_ref, back_ref, gw_ref, gb_ref, c_ref, b_ref):
    put_fields(c_ref, m1_ref[...], False)
    w = weights(p_ref)

    c8 = load8(c_ref, 0, 64)
    back, d2h, d2l, d1h, d1l = backward(c8, t_ref[0:64], t_ref[64:128], w)
    store8(b_ref, 0, back)
    gw_ref[...], gb_ref[...] = add_grads(
        no_grads(), load8(x_ref, 0, 64), c8, hh_ref[0:128], hh_ref[128:256],
        jnp.concatenate([d2h, d2l], axis=0), jnp.concatenate([d1h, d1l], axis=0),
    )
    back_ref[...] = b_ref[0 : F * 64].reshape(F, 64, 128)


def grads_body(x_ref, c_ref, ha_ref, hb_ref, dd_ref, gw_ref, gb_ref, pay_ref):
    g, gb = add_grads(
        (gw_ref[...], gb_ref[...]), load8(x_ref, 0, 64), load8(c_ref, 0, 64),
        ha_ref[...], hb_ref[...], dd_ref[0:128], dd_ref[128:256],
    )

    def fold(t):
        return t + pltpu.roll(t, 64, 1)

    gw = fold(g[0:64, 0:128] + g[64:128, 0:128])
    gs = g[:, 128:160].T
    gx2 = fold(gs[0:8, 0:128] + gs[8:16, 0:128])
    gx1 = fold(gs[0:8, 128:256] + gs[8:16, 128:256])
    gc = fold(gs[16:24, 256:384] + gs[24:32, 256:384])
    gbs = jnp.broadcast_to(jnp.sum(gb, axis=1, keepdims=True), (8, 128))
    left = iota((32, 128), 1) < 64
    scale = STEP / 256.0
    pay_ref[0:32] = jnp.where(left, gw[0:32], gw[32:64]) * scale
    pay_ref[32:40] = jnp.where(left[:8], gx1, gx2) * scale
    pay_ref[40:48] = jnp.where(left[:8], gc, gbs) * scale


def finish_body(
    w_ref, yl_ref, yr_ref, mk_ref, im_ref, part_ref, back_ref, g_ref, hb_ref, p_ref, s_ref, a_ref, o_ref
):
    im = im_ref[...] * STEP
    mass = quad((64, 128)) * mk_ref[0:1]
    v = zfill(yadd(w_ref[...], yl_ref[...], yr_ref[...])) * im[None]
    w = weights(p_ref)
    ones = bias_rows()

    def chunk(i, carry):
        at = lanes_of(i)
        h2h, h2l = hb_ref[0:64, at], hb_ref[64:128, at]
        out = mm(w["lo"], jnp.concatenate([h2h, h2l, h2h, ones], axis=0))
        store8(o_ref, i * CH, out[0:8])
        return carry

    lax.fori_loop(0, 64 // CH, chunk, 0)
    forcing = o_ref[0 : F * 64].reshape(F, 64, 128)
    s2 = part_ref[0:F] + STEP * forcing - v[0:F]
    a0 = (part_ref[F:] - v[F:]) * mass[None] + STEP * back_ref[...]
    x = jnp.concatenate([s2.reshape(320, 128), a0.reshape(320, 128)], axis=0)
    y = permute_nn(x, g_ref[...])
    for i, ref in enumerate((s_ref, a_ref)):
        for f in range(F):
            for q in range(4):
                r = (i * F + f) * 64 + q * 16
                ref[f, pl.ds(q, 16, stride=4), :] = y[r : r + 16]


def output_body(l_ref, h_ref, gw1_ref, gb1_ref, gw2_ref, gb2_ref, gwo_ref, gbo_ref):
    pay = jnp.concatenate([l_ref[...], h_ref[...]], axis=0)
    gw2_ref[0:32] = pay[0:32, 0:64]
    other = pltpu.roll(pay, 64, 1)
    gw2_ref[32:64] = other[0:32, 0:64]
    gw1_ref[...] = pay[32:37, 0:64]
    gb1_ref[...] = pay[37:38, 0:64]
    gb2_ref[...] = other[37:38, 0:64]
    gwo_ref[...] = pay[40:45, 0:64]
    diag = iota((8, 5), 0) == iota((8, 5), 1)
    gbo_ref[...] = jnp.sum(jnp.where(diag, other[40:48, 0:5], 0.0), axis=0, keepdims=True)


def call(body, outs, args, scratch=(), flops=0, trans=0, space=pltpu.VMEM):
    if space == pltpu.HBM:
        args = [pltpu.with_memory_space_constraint(x, pltpu.HBM) for x in args]
    shapes = [s if hasattr(s, "dtype") else jax.ShapeDtypeStruct(s, f32) for s in outs]
    scratch = [s if hasattr(s, "memory_space") or hasattr(s, "dtype") else pltpu.VMEM(s, f32) for s in scratch]
    return pl.pallas_call(
        body,
        out_shape=shapes,
        in_specs=[pl.BlockSpec(memory_space=space)] * len(args),
        out_specs=[VM] * len(shapes),
        scratch_shapes=scratch,
        cost_estimate=pl.CostEstimate(
            flops=flops, bytes_accessed=2000000, transcendentals=trans
        ),
        compiler_params=pltpu.CompilerParams(vmem_limit_bytes=40 * 1024 * 1024),
    )(*args)


def shift(x, axis, step):
    n = lax.axis_size(axis)
    return lax.ppermute(x, axis, [(i, (i + step) % n) for i in range(n)])


def both_ways(up, dn, axis, even):
    n = lax.axis_size(axis)
    in_pair = lax.ppermute(jnp.where(even, up, dn), axis, [(i, i ^ 1) for i in range(n)])
    across = lax.ppermute(
        jnp.where(even, dn, up), axis, [(i, (i + 1 if i % 2 else i - 1) % n) for i in range(n)]
    )
    return jnp.where(even, across, in_pair), jnp.where(even, in_pair, across)


def place(d):
    s, c = d // 16, d % 16
    return s // 8, (s // 2) % 4, s % 2, c // 4, c % 4


def together(fixed):
    groups = {}
    for d in range(256):
        groups.setdefault(tuple(place(d)[i] for i in fixed), []).append(d)
    return [groups[k] for k in sorted(groups)]


def send_to_all(x, groups):
    n = len(groups[0])
    y = jnp.broadcast_to(x[None], (n,) + x.shape)
    return lax.all_to_all(y, ("sub", "col"), 0, 0, axis_index_groups=groups, tiled=True)


SWAP = [(d, d ^ 16) for d in range(256)]


def grid_is_whole():
    return (lax.axis_size("sub"), lax.axis_size("col")) == (16, 16)


def even_at(axis):
    return lax.axis_index(axis) % 2 == 0


def chip_sum(x, core):
    low, high = x[:24], x[24:]
    mine = jnp.where(core, low, high)
    return mine + lax.ppermute(jnp.where(core, high, low), ("sub", "col"), SWAP)


def column_sum(x):
    return send_to_all(x, together((1, 2, 4))).sum(0)


def rest_sum(x, core):
    x = send_to_all(x, together((0, 2, 3))).sum(0)
    other = lax.ppermute(x, ("sub", "col"), SWAP)
    return jnp.where(core, x, other), jnp.where(core, other, x)


def on_device(
    initial_state,
    state_cotangent,
    element_order,
    element_weight,
    element_diffusivity,
    in_weight,
    in_bias,
    mid_weight,
    mid_bias,
    out_weight,
    out_bias,
):
    flags = (even_at("sub"), even_at("col"), element_weight)
    even_s, even_c, element_weight = lax.optimization_barrier(flags)
    hot = jax.ShapeDtypeStruct((128, 128), bf16)
    half = jax.ShapeDtypeStruct((128, 8192), bf16)
    wide = jax.ShapeDtypeStruct((256, 8192), bf16)
    khot = jax.ShapeDtypeStruct((64, 192), bf16)

    def in_device(w, rp, rm, n):
        m = 10 if n == 10 else 11
        return call(
            lambda *r: xy_body(n, *r), [(n, 3, 2, 8, 128), (m, 8, 128), (m, 8, 128)], [w, rp, rm]
        )

    def faces(w, up, dn, n):
        w, yu, yd = in_device(w, *both_ways(up, dn, "sub", even_s), n)
        yl, yr = both_ways(yu, yd, "col", even_c)
        return w, yl, yr

    w, up, dn, mk, g, kmat = call(
        start_body,
        [(12, 48, 128), (18, 8, 128), (18, 8, 128), (16, 128), hot, khot],
        [
            initial_state,
            state_cotangent,
            element_order,
            element_weight.reshape(1, 128),
            element_diffusivity.reshape(1, 128),
            jnp.asarray(stiffness_matrix()),
        ],
        [(F, 64, 128), (F, 64, 128), pltpu.VMEM((1, 128), jnp.int32), (1, 128), (1, 128)]
        + [(64, 64)]
        + [pltpu.SemaphoreType.DMA((6,))],
        space=pltpu.HBM,
    )
    (pw,) = call(
        prepare_body,
        [jax.ShapeDtypeStruct((272, 256), bf16)],
        [
            in_weight.T,
            in_bias.reshape(1, 64),
            mid_weight,
            mid_bias.reshape(1, 64),
            out_weight,
            out_bias.reshape(1, 5),
        ],
        [(5, 64), (1, 64), (64, 64), (1, 64), (5, 64), (1, 5), pltpu.SemaphoreType.DMA((6,))],
        flops=2000000,
        space=pltpu.HBM,
    )
    w, yl, yr = faces(w, up, dn, 12)
    pw, yl, yr = lax.optimization_barrier((pw, yl, yr))
    ten = [(10, 48, 128), (15, 8, 128), (15, 8, 128)]
    sa, im, w, up, dn = call(
        state_body, [(10, 64, 128), (64, 128)] + ten, [w, yl, yr, mk, kmat]
    )
    c0, x0, hh0, t0 = call(
        closure_body,
        [(F, 64, 128), (512, 128), wide, (128, 8192)],
        [sa, pw],
        [(512, 128)],
        flops=300000000,
        trans=1000000,
    )
    w, yl, yr = faces(w, up, dn, 10)
    part, m1, w, up, dn, x1, c1, ha1, hb1, dd1 = call(
        second_body,
        [(10, 64, 128), (F, 64, 128)] + ten + [(512, 128), (512, 128), half, half, wide],
        [w, yl, yr, mk, im, sa, c0, pw, kmat],
        [(512, 128)],
        flops=900000000,
        trans=1000000,
    )
    back, gw, gb = call(
        first_body,
        [(F, 64, 128), (384, 160), (8, 128)],
        [x0, m1, hh0, t0, pw],
        [(512, 128)] * 2,
        flops=600000000,
    )
    rp, rm = both_ways(up, dn, "sub", even_s)
    gw, rp, rm = lax.optimization_barrier((gw, rp, rm))
    (pay,) = call(grads_body, [(48, 128)], [x1, c1, ha1, hb1, dd1, gw, gb], flops=300000000)
    w, yu, yd = in_device(w, rp, rm, 10)
    if grid_is_whole():
        pay = chip_sum(pay, even_s)
        pay, yu, yd = lax.optimization_barrier((pay, yu, yd))
        yl, yr = both_ways(yu, yd, "col", even_c)
        out_state, out_adj = call(
            finish_body,
            [(F, 64, 128), (F, 64, 128)],
            [w, yl, yr, mk, im, part, back, g, hb1, pw],
            [(512, 128)],
            flops=20000000,
        )
        pay = column_sum(pay)
        pay, out_state, out_adj = lax.optimization_barrier((pay, out_state, out_adj))
        terms = list(rest_sum(pay, even_s))
    else:
        yl, yr = both_ways(yu, yd, "col", even_c)
        pay = lax.psum(pay, ("sub", "col"))
        out_state, out_adj = call(
            finish_body,
            [(F, 64, 128), (F, 64, 128)],
            [w, yl, yr, mk, im, part, back, g, hb1, pw],
            [(512, 128)],
            flops=20000000,
        )
        terms = [pay[:24], pay[24:]]
    gw1, gb1, gw2, gb2, gwo, gbo = call(
        output_body, [(5, 64), (1, 64), (64, 64), (1, 64), (5, 64), (1, 5)], terms
    )
    return (
        out_state,
        out_adj,
        gw1.T,
        gb1.reshape(64),
        gw2,
        gb2.reshape(64),
        gwo,
        gbo.reshape(5),
    )


def solution(mesh):
    split = P(None, None, ("sub", "col"))
    placed = (split, split, P(("sub", "col"), None), P(("sub", "col")), P(("sub", "col")))
    return jax.shard_map(
        on_device,
        mesh=mesh,
        in_specs=placed + (P(),) * 6,
        out_specs=(split, split) + (P(),) * 6,
        check_vma=False,
    )
```
